32 devices in a mesh: dp: 4 (over y, x), fsdp: 8 (over z, core).
Axes of the slice: x: 2, y: 2, z: 4, core: 2. Of those that a mesh axis runs over, the one named last changes fastest.
Arguments:
- images: bfloat16 [96, 196, 768], P(('dp', 'fsdp')), may hold values from -8 to 8
- tissue: int32 [96, 196], P(('dp', 'fsdp')), may hold values from 0 to 1, as said below
- pair_index: int32 [96], P(('dp', 'fsdp')), may hold values from 0 to 95, each once
- text_embed: bfloat16 [96, 768], P(('dp', 'fsdp')), may hold values from -0.25 to 0.25
- logit_scale: float32 [], replicated, may hold values from 30 to 80
- ln1_gain: bfloat16 [768], P(('dp', 'fsdp')), may hold values from 0.5 to 1.5
- ln1_bias: bfloat16 [768], P(('dp', 'fsdp')), may hold values from -1.25 to 1.25
- w_qkv: bfloat16 [768, 2304], P(None, ('dp', 'fsdp')), may hold values from -0.21875 to 0.21875
- bias_qv: bfloat16 [1536], P(('dp', 'fsdp')), may hold values from -1.25 to 1.25
- w_out: bfloat16 [768, 768], P(None, ('dp', 'fsdp')), may hold values from -0.625 to 0.625
- bias_out: bfloat16 [768], P(('dp', 'fsdp')), may hold values from -1.25 to 1.25
- ln2_gain: bfloat16 [768], P(('dp', 'fsdp')), may hold values from 0.5 to 1.5
- ln2_bias: bfloat16 [768], P(('dp', 'fsdp')), may hold values from -1.25 to 1.25
- w_fc1: bfloat16 [768, 3072], P(None, ('dp', 'fsdp')), may hold values from -0.21875 to 0.21875
- bias_fc1: bfloat16 [3072], P(('dp', 'fsdp')), may hold values from -1.25 to 1.25
- w_fc2: bfloat16 [3072, 768], P(('dp', 'fsdp')), may hold values from -0.15625 to 0.15625
- bias_fc2: bfloat16 [768], P(('dp', 'fsdp')), may hold values from -1.25 to 1.25
- cotangent: bfloat16 [96, 196, 768], P(('dp', 'fsdp')), may hold values from -0.0625 to 0.0625
Outputs:
- mixed_out: bfloat16 [96, 196, 768], P(('dp', 'fsdp'))
- input_grad: float32 [96, 196, 768], P(('dp', 'fsdp'))
- loss_value: float32 [], replicated
- text_grad: float32 [96, 768], P(('dp', 'fsdp'))
- grad_ln1_gain: float32 [768], P(('dp', 'fsdp'))
- grad_ln1_bias: float32 [768], P(('dp', 'fsdp'))
- grad_w_qkv: float32 [768, 2304], P(None, ('dp', 'fsdp'))
- grad_bias_qv: float32 [1536], P(('dp', 'fsdp'))
- grad_w_out: float32 [768, 768], P(None, ('dp', 'fsdp'))
- grad_bias_out: float32 [768], P(('dp', 'fsdp'))
- grad_ln2_gain: float32 [768], P(('dp', 'fsdp'))
- grad_ln2_bias: float32 [768], P(('dp', 'fsdp'))
- grad_w_fc1: float32 [768, 3072], P(None, ('dp', 'fsdp'))
- grad_bias_fc1: float32 [3072], P(('dp', 'fsdp'))
- grad_w_fc2: float32 [3072, 768], P(('dp', 'fsdp'))
- grad_bias_fc2: float32 [768], P(('dp', 'fsdp'))
The draws below stay inside these ranges and needn't reach their ends.
Inputs may be any that keep to these rules, and one draw needn't show every extreme that they name: Every image has at least 98 tissue slots. `pair_index`: each text is paired with exactly one image.
All inputs are finite; a program needn't handle non-finite values.
Results may differ from the reference program's by a relative error of at most 0.023.
Values may be sent and summed in bfloat16 or wider, within the bound.
A program may use at most 128 MiB of HBM per device.

```python
import math
from functools import partial
import jax
import jax.numpy as jnp
from jax import lax

D = 768
HEADS = 12
HEAD = 64
FF = 3072
SLOTS = 196
IMG_DEV = 3
IMGS = 96


def draw_tissue(key, part):
    count_key, order_key = jax.random.split(key)
    counts = jax.random.randint(count_key, (IMGS, 1), SLOTS // 2, SLOTS + 1)
    scores = jax.random.randint(order_key, (IMGS, SLOTS), 0, 2 ** 20) * SLOTS + lax.broadcasted_iota(jnp.int32, (IMGS, SLOTS), 1)
    slot_order = jnp.argsort(scores, axis=1)
    slot_rank = jnp.argsort(slot_order, axis=1)
    return (slot_rank < counts).astype(jnp.int32)


def draw_images(key, part):
    key = jax.random.fold_in(key, 5)
    noise_key, offset_key = jax.random.split(key, 2)
    patches = jnp.clip(jax.random.normal(noise_key, (IMGS, SLOTS, D), jnp.float32), -5.0, 5.0)
    offsets = jnp.clip(0.5 * jax.random.normal(offset_key, (IMGS, 1, D), jnp.float32), -2.5, 2.5)
    return (patches + offsets).astype(jnp.bfloat16)


def levels(rng, extent, shards, smallest, largest):
    def one(axis_at, parts):
        draws = jax.random.uniform(jax.random.fold_in(jax.random.fold_in(rng, 6), axis_at), (parts,), jnp.float32, smallest / len(shards), largest / len(shards))
        return jnp.repeat(jnp.exp(draws), extent[axis_at] // parts).reshape((-1,) + (1,) * (len(extent) - axis_at - 1))

    level = one(*shards[0])
    for cut in shards[1:]:
        level = level * one(*cut)
    return level


def normal_values(rng, extent, scale, bound, pieces=(), held_as=jnp.bfloat16):
    values = scale * jax.random.normal(rng, extent, jnp.float32)
    if pieces:
        values = values * levels(rng, extent, pieces, -0.22, 0.18)
    return jnp.clip(values, -bound, bound).astype(held_as)


def setup_inputs(seed: int = 0) -> dict:
    streams_of = jax.random.split(jax.random.key(seed), 19)
    return {
        "images": draw_images(jax.random.fold_in(streams_of[18], 71), 0),
        "tissue": draw_tissue(jax.random.fold_in(streams_of[18], 71), 0),
        "pair_index": jax.random.permutation(streams_of[2], IMGS).astype(jnp.int32),
        "text_embed": normal_values(streams_of[3], (IMGS, D), 0.04, 0.25, ((0, 32),)),
        "logit_scale": jnp.clip(jnp.exp(jax.random.uniform(streams_of[4], (), jnp.float32, math.log(30.0), math.log(80.0))), 30.0, 80.0),
        "ln1_gain": jnp.clip(1.0 + 0.1 * jax.random.normal(streams_of[5], (D,), jnp.float32), 0.5, 1.5).astype(jnp.bfloat16),
        "ln1_bias": normal_values(streams_of[6], (D,), 0.2, 1.25, ((0, 32),)),
        "w_qkv": normal_values(streams_of[7], (D, 3 * D), D ** -0.5, 0.21875, ((1, 32),)),
        "bias_qv": normal_values(streams_of[8], (2 * D,), 0.2, 1.25, ((0, 32),)),
        "w_out": normal_values(streams_of[9], (D, D), (D // 8) ** -0.5, 0.625, ((1, 32),)),
        "bias_out": normal_values(streams_of[10], (D,), 0.2, 1.25, ((0, 32),)),
        "ln2_gain": jnp.clip(1.0 + 0.1 * jax.random.normal(streams_of[11], (D,), jnp.float32), 0.5, 1.5).astype(jnp.bfloat16),
        "ln2_bias": normal_values(streams_of[12], (D,), 0.2, 1.25, ((0, 32),)),
        "w_fc1": normal_values(streams_of[13], (D, FF), D ** -0.5, 0.21875, ((1, 32),)),
        "bias_fc1": normal_values(streams_of[14], (FF,), 0.2, 1.25, ((0, 32),)),
        "w_fc2": normal_values(streams_of[15], (FF, D), (FF // 2) ** -0.5, 0.15625, ((0, 32),)),
        "bias_fc2": normal_values(streams_of[16], (D,), 0.2, 1.25, ((0, 32),)),
        "cotangent": normal_values(streams_of[17], (IMGS, SLOTS, D), 0.01, 0.0625, ((0, 32),)),
    }


@jax.custom_vjp
def low(v):
    return lax.optimization_barrier(v.astype(jnp.bfloat16)).astype(jnp.float32)

@jax.custom_vjp
def low_back(v):
    return v

def low_keep(v):
    return (low(v), None)

def low_pass(kept, grad):
    return (grad,)

def back_keep(v):
    return (v, None)

def back_low(kept, grad):
    return (low(grad),)
low.defvjp(low_keep, low_pass)
low_back.defvjp(back_keep, back_low)

def matmul(left, right):
    return jnp.dot(left, right, precision=lax.Precision.HIGHEST)

def layer_norm(values, gain_vec, shift_vec):
    centered = values - lax.optimization_barrier(jnp.mean(values, -1, keepdims=True))
    variance = lax.optimization_barrier(jnp.mean(centered * centered, -1, keepdims=True))
    return centered * lax.rsqrt(variance + 1e-06) * gain_vec + shift_vec

def unit_rows(values):
    return values * lax.rsqrt(lax.optimization_barrier(jnp.sum(values * values, -1, keepdims=True)) + 1e-06)

def log_sum(values, axis_index):
    row_top = lax.optimization_barrier(jnp.max(values, axis_index, keepdims=True))
    return jnp.squeeze(row_top, axis_index) + jnp.log(lax.optimization_barrier(jnp.sum(jnp.exp(values - row_top), axis_index)))

def layer_group(params, group_item):
    ln1_gain, ln1_bias, w_qkv, bias_qv, w_out, bias_out, ln2_gain, ln2_bias, w_fc1, bias_fc1, w_fc2, bias_fc2 = params
    inputs, image_mask = group_item
    group_count = inputs.shape[0]
    token_rows = inputs.reshape(-1, D)
    normed = low(layer_norm(token_rows, ln1_gain, ln1_bias))
    bias_all = jnp.concatenate([bias_qv[:D], jnp.zeros((D,), jnp.float32), bias_qv[D:]])
    joined_qkv = low(low_back(matmul(normed, low(w_qkv)) + bias_all)).reshape(group_count, SLOTS, 3, HEADS, HEAD)
    queries = joined_qkv[:, :, 0]
    key_heads = joined_qkv[:, :, 1]
    values = joined_qkv[:, :, 2]
    scores = jnp.einsum('gqhd,gkhd->ghqk', queries, key_heads, precision=lax.Precision.HIGHEST) * HEAD ** (-0.5)
    scores = low_back(jnp.where(image_mask[:, None, None, :] > 0, scores, -jnp.inf))
    row_top = lax.optimization_barrier(jnp.max(scores, -1, keepdims=True))
    exp_terms = jnp.exp(scores - row_top)
    attn_probs = exp_terms / lax.optimization_barrier(jnp.sum(exp_terms, -1, keepdims=True))
    attended = jnp.einsum('ghqk,gkhd->gqhd', low(attn_probs), values, precision=lax.Precision.HIGHEST).reshape(-1, D)
    attended = low(low_back(attended))
    hidden = token_rows + low_back(matmul(attended, low(w_out)) + bias_out)
    second = low(layer_norm(hidden, ln2_gain, ln2_bias))
    pre_act = low_back(matmul(second, low(w_fc1)) + bias_fc1)
    activated = low(jax.nn.gelu(pre_act, approximate=False))
    outputs = hidden + low_back(matmul(activated, low(w_fc2)) + bias_fc2)
    return outputs.reshape(group_count, SLOTS, D) * image_mask[:, :, None]

def forward(params, inputs, text_rows, tissue_float, pair_index, logit_scale):
    group_size = 2 * IMG_DEV
    shaped = (inputs.reshape(-1, group_size, SLOTS, D), tissue_float.reshape(-1, group_size, SLOTS))
    outputs = lax.map(jax.checkpoint(partial(layer_group, params)), shaped).reshape(IMGS, SLOTS, D)
    counts = lax.optimization_barrier(jnp.sum(tissue_float, 1))[:, None]
    pooled = lax.optimization_barrier(jnp.sum(outputs, 1)) / counts
    image_unit = low(unit_rows(pooled))
    text_unit = low(unit_rows(text_rows))
    raw_sim = low_back(matmul(image_unit, text_unit.T))
    logits = logit_scale * raw_sim
    pair_match = (lax.broadcasted_iota(jnp.int32, (IMGS, IMGS), 1) == pair_index[:, None]).astype(jnp.float32)
    loss_value = (jnp.sum(log_sum(logits, 1)) + jnp.sum(log_sum(logits, 0)) - 2.0 * jnp.sum(logits * pair_match)) / (2.0 * IMGS)
    return (outputs, loss_value)

def reference(images, tissue, pair_index, text_embed, logit_scale, ln1_gain, ln1_bias, w_qkv, bias_qv, w_out, bias_out, ln2_gain, ln2_bias, w_fc1, bias_fc1, w_fc2, bias_fc2, cotangent):
    params = tuple((param.astype(jnp.float32) for param in (ln1_gain, ln1_bias, w_qkv, bias_qv, w_out, bias_out, ln2_gain, ln2_bias, w_fc1, bias_fc1, w_fc2, bias_fc2)))
    tissue_float = tissue.astype(jnp.float32)
    inputs = images.astype(jnp.float32)
    text_rows = text_embed.astype(jnp.float32)

    def objective(param_set, input_set, text_set):
        return forward(param_set, input_set, text_set, tissue_float, pair_index, logit_scale)
    (outputs, loss_value), pull = jax.vjp(objective, params, inputs, text_rows)
    grad_params, input_grad, text_grad = pull((cotangent.astype(outputs.dtype), jnp.ones_like(loss_value) * IMGS))
    return (outputs.astype(jnp.bfloat16), input_grad, loss_value, text_grad, grad_params[0], grad_params[1], grad_params[2], grad_params[3], grad_params[4], grad_params[5], grad_params[6], grad_params[7], grad_params[8], grad_params[9], grad_params[10], grad_params[11])
```

```python
import functools
import jax
import jax.numpy as jnp
from jax import lax
from jax.experimental import pallas as pl
from jax.experimental.pallas import tpu as pltpu
from jax.sharding import PartitionSpec as P

MESH = pl.DeviceIdType.MESH
MIB = 1024 * 1024
GROUPS = 32
PIECES = (3, 2, 2, 4, 2, 96, 768)

class Pos: pass
def position(F, r):
    p = Pos()
    L = lax.axis_index("dp")*F + lax.axis_index("fsdp")
    g = lax.div(L, r); p.rho = lax.rem(L, r); p.F=F; p.r=r
    p.g=g
    p.c = lax.rem(g,2); p.z = lax.rem(lax.div(g,2),4); p.x = lax.rem(lax.div(g,8),2); p.y = lax.div(g,16)
    p.l = p.y + p.c*(p.x-p.y); p.f = p.x + p.c*(p.y-p.x)
    def dev(y,x,z,c):
        L2 = (((y*2+x)*4+z)*2+c)*r + p.rho
        return (lax.div(L2,F), lax.rem(L2,F))
    c,x,y,z = p.c,p.x,p.y,p.z
    p.dev=dev
    p.sib = dev(y,x,z,1-c)
    p.fn = dev(y + c*(1-2*y), x + (1-c)*(1-2*x), z, c)
    p.ln = dev(y + (1-c)*(1-2*y), x + c*(1-2*x), z, c)
    p.up = dev(y,x,jnp.minimum(z+1,3),c)
    p.dn = dev(y,x,jnp.maximum(z-1,0),c)
    return p

def barrier(p):
    bar = pltpu.get_barrier_semaphore()
    def body(i, _):
        q = lax.rem(lax.div(p.g,2) + i, 16)
        L2 = (q*2+p.c)*p.r + p.rho
        pl.semaphore_signal(bar, inc=1, device_id=(lax.div(L2,p.F), lax.rem(L2,p.F)), device_id_type=MESH)
        return 0
    lax.fori_loop(1, 16, body, 0)
    pl.semaphore_signal(bar, inc=1, device_id=p.sib, device_id_type=MESH)
    pl.semaphore_wait(bar, 16)

class Gather:
    def __init__(s, p, W, m, sems):
        s.p, s.W, s.m = p, W, m
        s.ss, s.rs = sems
    def cp(s, idx, ks, kr, dev):
        ref = s.W.at[(s.m,)+idx]
        return pltpu.make_async_remote_copy(src_ref=ref, dst_ref=ref, send_sem=s.ss.at[s.m, ks], recv_sem=s.rs.at[s.m, kr], device_id=dev, device_id_type=MESH)
    def f(s):
        p=s.p; return s.cp((p.c,p.l,p.z,p.f), 0, 0, p.fn)
    def f_in(s):
        p=s.p; return s.cp((p.c,p.l,p.z,1-p.f), 0, 0, p.fn)
    def fb(s, b):
        return s.p.f + b*(1-2*s.p.f)
    def up(s, zz, b): f=s.fb(b); return s.cp((s.p.c,s.p.l,zz,f), 1+2*zz+b, 1+2*zz+b, s.p.up)
    def dn(s, zz, b): f=s.fb(b); return s.cp((s.p.c,s.p.l,zz,f), 9+2*zz+b, 1+2*zz+b, s.p.dn)
    def ll(s, zz): return s.cp((s.p.c,s.p.l,zz), 17+zz, 9+zz, s.p.ln)
    def l_in(s, zz): return s.cp((s.p.c,1-s.p.l,zz), 17+zz, 9+zz, s.p.ln)
    def d(s, l, zz): return s.cp((s.p.c,l,zz), 21+4*l+zz, 13+4*l+zz, s.p.sib)
    def d_in(s, l, zz): return s.cp((1-s.p.c,l,zz), 21+4*l+zz, 13+4*l+zz, s.p.sib)
    def own(s, b):
        p=s.p
        if b: s.f_in().wait_recv()
        else: s.f().start()
        @pl.when(p.z<3)
        def _(): s.up(p.z,b).start()
        @pl.when(p.z>0)
        def _(): s.dn(p.z,b).start()
        if b:
            s.ll(p.z).start()
            s.d(p.l, p.z).start()
    def stepz(s, h, b):
        p=s.p
        @pl.when(p.z-h>=0)
        def _():
            zz=p.z-h
            s.up(zz,b).wait_recv()
            @pl.when(p.z<3)
            def _(): s.up(zz,b).start()
            if b: s.ll(zz).start(); s.d(p.l,zz).start()
        @pl.when(p.z+h<=3)
        def _():
            zz=p.z+h
            s.dn(zz,b).wait_recv()
            @pl.when(p.z>0)
            def _(): s.dn(zz,b).start()
            if b: s.ll(zz).start(); s.d(p.l,zz).start()
    def stepl(s, h):
        p=s.p
        def one(zz):
            s.l_in(zz).wait_recv(); s.d(1-p.l,zz).start()
        if h==0: one(p.z)
        else:
            @pl.when(p.z-h>=0)
            def _(): one(p.z-h)
            @pl.when(p.z+h<=3)
            def _(): one(p.z+h)
    def finish(s):
        for zz in range(4):
            for l in range(2): s.d_in(l,zz).wait_recv()
    def drain(s):
        p=s.p
        s.f().wait_send()
        for zz in range(4):
            @pl.when((p.z<3) & (zz<=p.z))
            def _(): s.up(zz,0).wait_send(); s.up(zz,1).wait_send()
            @pl.when((p.z>0) & (zz>=p.z))
            def _(): s.dn(zz,0).wait_send(); s.dn(zz,1).wait_send()
            s.ll(zz).wait_send()
            for l in range(2): s.d(l,zz).wait_send()

class Scatter:
    def __init__(s, p, G, m, R, X, sems):
        s.p, s.G, s.m, s.R, s.X = p, G, m, R, X
        s.ss, s.rs = sems
    def cp(s, src, dst, ks, kr, dev):
        return pltpu.make_async_remote_copy(src_ref=src, dst_ref=dst, send_sem=s.ss.at[s.m, ks], recv_sem=s.rs.at[s.m, kr], device_id=dev, device_id_type=MESH)
    def gq(s, c, l): return s.G.at[s.m, c, l]
    def rc(s, l): return s.R.at[l]
    def ra(s, zz): return s.R.at[2, zz]
    def c_cp(s, l): return s.cp(s.gq(1-s.p.c, l), s.rc(l), 1+l, 1+l, s.p.sib)
    def a_cp(s, zz): return s.cp(s.G.at[s.m, s.p.c, 1-s.p.l, zz], s.ra(zz), 3+zz, 3+zz, s.p.ln)
    def fb(s, b): return 1-s.p.f if b==0 else s.p.f
    def zsrc(s, zz, b): return s.G.at[s.m, s.p.c, s.p.l, zz, s.fb(b)]
    def up_far(s, zz, b): return s.cp(s.zsrc(zz,b), s.R.at[3, zz, b], 7+2*zz+b, 7+2*zz+b, s.p.up)
    def up_end(s, zz, b): return s.cp(s.zsrc(zz,b), s.X.at[b], 7+2*zz+b, 15+b, s.p.up)
    def down(s, zz, b): return s.cp(s.zsrc(zz,b), s.R.at[3, zz, b], 15+2*zz+b, 7+2*zz+b, s.p.dn)
    def f_cp(s): return s.cp(s.zsrc(s.p.z, 0), s.X.at[2], 0, 0, s.p.fn)
    def c_send(s, l): s.c_cp(l).start()
    def c_add(s, l):
        s.c_cp(l).wait_recv()
        def body(zz, _):
            for ff in range(2):
                g = s.G.at[s.m, s.p.c, l, zz, ff]
                g[...] = (g[...].astype(jnp.float32) + s.R[l, zz, ff].astype(jnp.float32)).astype(jnp.bfloat16)
            return 0
        lax.fori_loop(0, 4, body, 0)
    def add(s, zz, b, ref):
        g = s.zsrc(zz, b)
        g[...] = (g[...].astype(jnp.float32) + ref[...].astype(jnp.float32)).astype(jnp.bfloat16)
    def by_dist(s, h, fn):
        p=s.p
        if h==0: fn(p.z); return
        @pl.when(p.z+h<=3)
        def _(): fn(p.z+h)
        @pl.when(p.z-h>=0)
        def _(): fn(p.z-h)
    def a_send(s):
        for h in (3,2,1,0): s.by_dist(h, lambda zz: s.a_cp(zz).start())
    def a_add(s, h):
        def one(zz):
            s.a_cp(zz).wait_recv()
            for b in (0,1):
                g = s.zsrc(zz,b)
                g[...] = (g[...].astype(jnp.float32) + s.R[2, zz, s.fb(b)].astype(jnp.float32)).astype(jnp.bfloat16)
        s.by_dist(h, one)
    def z_step(s, h, b):
        p=s.p
        if h>0:
            @pl.when(p.z+h<=3)
            def _():
                zz=p.z+h
                @pl.when(p.z>0)
                def _():
                    s.up_far(zz,b).wait_recv(); s.add(zz,b,s.R.at[3,zz,b])
                if h==1: s.up_end(zz,b).start()
                else: s.up_far(zz,b).start()
            @pl.when(p.z-h>=0)
            def _():
                zz=p.z-h
                @pl.when(p.z<3)
                def _():
                    s.down(zz,b).wait_recv(); s.add(zz,b,s.R.at[3,zz,b])
                s.down(zz,b).start()
        else:
            @pl.when(p.z>0)
            def _():
                s.up_end(p.z,b).wait_recv(); s.add(p.z,b,s.X.at[b])
            @pl.when(p.z<3)
            def _():
                s.down(p.z,b).wait_recv(); s.add(p.z,b,s.R.at[3,p.z,b])
            if b==0: s.f_cp().start()
    def final(s):
        s.f_cp().wait_recv()
        return s.zsrc(s.p.z,1)[...].astype(jnp.float32) + s.X[2].astype(jnp.float32)
    def drain(s):
        p=s.p
        for l in range(2): s.c_cp(l).wait_send()
        for zz in range(4):
            s.a_cp(zz).wait_send()
            @pl.when(zz>p.z)
            def _():
                for b in (0,1): s.up_far(zz,b).wait_send()
            @pl.when(zz<p.z)
            def _():
                for b in (0,1): s.down(zz,b).wait_send()
        s.f_cp().wait_send()


def gather_kernel(F, r, own, w_out, W, ss, rs):
    p = position(F, r)
    for m in range(3):
        W[m, p.c, p.l, p.z, p.f] = own[m]
    barrier(p)
    gs = [Gather(p, W, m, (ss, rs)) for m in range(3)]
    gs[0].own(0); gs[0].own(1)
    for m in range(3):
        g=gs[m]
        g.stepz(1,0); g.stepz(1,1); g.stepl(0)
        g.stepz(2,0); g.stepz(2,1)
        if m<2: gs[m+1].own(0)
        g.stepl(1)
        if m<2: gs[m+1].own(1)
        g.stepz(3,0); g.stepz(3,1); g.stepl(2)
        g.stepl(3)
    for g in gs: g.finish()
    w_out[...] = W[...]
    for g in gs: g.drain()


def scatter_kernel(F, r, g_ref, o_ref, G, R, X, ss, rs):
    p = position(F, r)
    G[...] = g_ref[...]
    barrier(p)
    sc=[Scatter(p, G, m, R.at[m], X.at[m], (ss,rs)) for m in range(3)]
    for m in range(3): sc[m].c_send(1-p.f)
    for m in range(3): sc[m].c_send(p.f)
    for m in range(3):
        s=sc[m]
        s.c_add(1-p.l); s.a_send(); s.c_add(p.l)
    for m in range(3):
        s=sc[m]
        for h in (3,2,1,0):
            s.a_add(h)
            for b in (0,1): s.z_step(h,b)
        o_ref[m] = s.final()
    for s in sc: s.drain()


def swap(block, step):
    return lambda size: lax.ppermute(block, "fsdp", [(i, i ^ step) for i in range(size)])


def pregather(block, F, r):
    step = 1
    while step < r:
        high = (lax.axis_index("fsdp") // step) % 2 == 1
        other = swap(block, step)(F)
        block = jnp.concatenate([jnp.where(high, other, block), jnp.where(high, block, other)], 0)
        step *= 2
    return block


def postscatter(block, F, r):
    step = r // 2
    while step:
        high = (lax.axis_index("fsdp") // step) % 2 == 1
        half = block.shape[0] // 2
        keep = jnp.where(high, block[half:], block[:half])
        send = jnp.where(high, block[:half], block[half:])
        block = keep + swap(send, step)(F)
        step //= 2
    return block


def to_natural(pieces):
    zero = pieces[:, 0].transpose(0, 1, 3, 2, 4, 5)
    one = pieces[:, 1].transpose(0, 3, 1, 2, 4, 5)
    return jnp.stack([zero, one], 4).reshape(3, 32, 96, 768)


def to_pieces(natural):
    both = natural.reshape(3, 2, 2, 4, 2, 96, 768)
    zero = both[:, :, :, :, 0].transpose(0, 1, 3, 2, 4, 5)
    one = both[:, :, :, :, 1].transpose(0, 2, 3, 1, 4, 5)
    return jnp.stack([zero, one], 1)

HEADS = 12

norm_eps = 1e-06


def layer_norm(values, gain_vec, shift_vec):
    centered = values - jnp.mean(values, -1, keepdims=True)
    variance = jnp.mean(centered * centered, -1, keepdims=True)
    return centered * lax.rsqrt(variance + norm_eps) * gain_vec + shift_vec


def unit_rows(values):
    return values * lax.rsqrt(jnp.sum(values * values, -1, keepdims=True) + norm_eps)


def exact_gelu(values):
    return jax.nn.gelu(values, approximate=False)


def split_heads(joined_qkv, image_mask):
    images_here, slot_count = image_mask.shape
    model_width = joined_qkv.shape[1] // 3
    heads_view = joined_qkv.reshape(images_here, slot_count, 3, HEADS, model_width // HEADS)
    return (heads_view[:, :, 0], heads_view[:, :, 1], heads_view[:, :, 2])


def masked_scores(queries, key_heads, image_mask):
    scores = jnp.einsum(
        "gqhd,gkhd->ghqk", queries, key_heads, preferred_element_type=jnp.float32
    ) * queries.shape[-1] ** (-0.5)
    return jnp.where(image_mask[:, None, None, :] > 0, scores, -jnp.inf)


def forward_block(params_full, token_rows, image_mask):
    (
        ln1_gain,
        ln1_bias,
        w_qkv,
        bias_qv,
        w_out,
        bias_out,
        ln2_gain,
        ln2_bias,
        w_fc1,
        bias_fc1,
        w_fc2,
        bias_fc2,
    ) = params_full
    model_width = token_rows.shape[1]
    normed = layer_norm(
        token_rows, ln1_gain.astype(jnp.float32), ln1_bias.astype(jnp.float32)
    ).astype(jnp.bfloat16)
    bias_all = jnp.concatenate(
        [bias_qv[:model_width], jnp.zeros((model_width,), jnp.bfloat16), bias_qv[model_width:]]
    ).astype(jnp.float32)
    joined_qkv = (jnp.dot(normed, w_qkv, preferred_element_type=jnp.float32) + bias_all).astype(
        jnp.bfloat16
    )
    queries, key_heads, values = split_heads(joined_qkv, image_mask)
    scores = masked_scores(queries, key_heads, image_mask)
    row_top = jnp.max(scores, -1, keepdims=True)
    exp_terms = jnp.exp(scores - row_top)
    row_total = jnp.sum(exp_terms, -1, keepdims=True)
    attn_probs = (exp_terms / row_total).astype(jnp.bfloat16)
    log_total = row_top + jnp.log(row_total)
    attended = jnp.einsum("ghqk,gkhd->gqhd", attn_probs, values, preferred_element_type=jnp.float32)
    attended = attended.reshape(-1, model_width).astype(jnp.bfloat16)
    hidden = (
        token_rows
        + jnp.dot(attended, w_out, preferred_element_type=jnp.float32)
        + bias_out.astype(jnp.float32)
    )
    second = layer_norm(hidden, ln2_gain.astype(jnp.float32), ln2_bias.astype(jnp.float32)).astype(
        jnp.bfloat16
    )
    pre_act = jnp.dot(second, w_fc1, preferred_element_type=jnp.float32) + bias_fc1.astype(
        jnp.float32
    )
    activated = exact_gelu(pre_act).astype(jnp.bfloat16)
    outputs = (
        hidden
        + jnp.dot(activated, w_fc2, preferred_element_type=jnp.float32)
        + bias_fc2.astype(jnp.float32)
    ) * image_mask.reshape(-1, 1)
    saved_state = (normed, joined_qkv, log_total, attended, hidden, second, pre_act, activated)
    return (outputs, saved_state)


def backward_block(params_full, token_rows, image_mask, saved_state, grad_out):
    (
        ln1_gain,
        ln1_bias,
        w_qkv,
        bias_qv,
        w_out,
        bias_out,
        ln2_gain,
        ln2_bias,
        w_fc1,
        bias_fc1,
        w_fc2,
        bias_fc2,
    ) = params_full
    normed, joined_qkv, log_total, attended, hidden, second, pre_act, activated = saved_state
    model_width = token_rows.shape[1]
    grad_branch2 = grad_out.astype(jnp.bfloat16)
    grad_w_fc2 = jnp.einsum(
        "nf,nd->fd", activated, grad_branch2, preferred_element_type=jnp.float32
    )
    grad_bias_fc2 = jnp.sum(grad_branch2.astype(jnp.float32), 0)
    grad_act = jnp.einsum("nd,fd->nf", grad_branch2, w_fc2, preferred_element_type=jnp.float32)
    gelu_value, gelu_pull = jax.vjp(exact_gelu, pre_act)
    grad_pre = gelu_pull(grad_act)[0].astype(jnp.bfloat16)
    grad_w_fc1 = jnp.einsum("nd,nf->df", second, grad_pre, preferred_element_type=jnp.float32)
    grad_bias_fc1 = jnp.sum(grad_pre.astype(jnp.float32), 0)
    grad_second = jnp.einsum("nf,df->nd", grad_pre, w_fc1, preferred_element_type=jnp.float32)
    norm_value, norm_pull = jax.vjp(
        layer_norm, hidden, ln2_gain.astype(jnp.float32), ln2_bias.astype(jnp.float32)
    )
    grad_hidden_norm, grad_ln2_gain, grad_ln2_bias = norm_pull(grad_second)
    grad_hidden = grad_out + grad_hidden_norm
    grad_branch1 = grad_hidden.astype(jnp.bfloat16)
    grad_w_out = jnp.einsum("nd,ne->de", attended, grad_branch1, preferred_element_type=jnp.float32)
    grad_bias_out = jnp.sum(grad_branch1.astype(jnp.float32), 0)
    grad_attended = jnp.einsum(
        "ne,de->nd", grad_branch1, w_out, preferred_element_type=jnp.float32
    ).astype(jnp.bfloat16)
    queries, key_heads, values = split_heads(joined_qkv, image_mask)
    grad_attended = grad_attended.reshape(values.shape)
    scores = masked_scores(queries, key_heads, image_mask)
    attn_probs = jnp.exp(scores - log_total)
    grad_values = jnp.einsum(
        "ghqk,gqhd->gkhd",
        attn_probs.astype(jnp.bfloat16),
        grad_attended,
        preferred_element_type=jnp.float32,
    )
    grad_probs = jnp.einsum(
        "gqhd,gkhd->ghqk", grad_attended, values, preferred_element_type=jnp.float32
    )
    inner_sum = jnp.sum(grad_probs * attn_probs, -1, keepdims=True)
    grad_scores = (attn_probs * (grad_probs - inner_sum)).astype(jnp.bfloat16)
    head_scale = queries.shape[-1] ** (-0.5)
    grad_queries = (
        jnp.einsum("ghqk,gkhd->gqhd", grad_scores, key_heads, preferred_element_type=jnp.float32)
        * head_scale
    )
    grad_keys = (
        jnp.einsum("ghqk,gqhd->gkhd", grad_scores, queries, preferred_element_type=jnp.float32)
        * head_scale
    )
    grad_joined = (
        jnp.stack([grad_queries, grad_keys, grad_values], 2)
        .reshape(-1, 3 * model_width)
        .astype(jnp.bfloat16)
    )
    grad_w_qkv = jnp.einsum("nd,nf->df", normed, grad_joined, preferred_element_type=jnp.float32)
    joined_sums = jnp.sum(grad_joined.astype(jnp.float32), 0)
    grad_bias_qv = jnp.concatenate([joined_sums[:model_width], joined_sums[2 * model_width :]])
    grad_normed = jnp.einsum("nf,df->nd", grad_joined, w_qkv, preferred_element_type=jnp.float32)
    first_value, first_pull = jax.vjp(
        layer_norm, token_rows, ln1_gain.astype(jnp.float32), ln1_bias.astype(jnp.float32)
    )
    grad_rows, grad_ln1_gain, grad_ln1_bias = first_pull(grad_normed)
    grad_input = grad_hidden + grad_rows
    grad_list = (
        grad_ln1_gain,
        grad_ln1_bias,
        grad_w_qkv,
        grad_bias_qv,
        grad_w_out,
        grad_bias_out,
        grad_ln2_gain,
        grad_ln2_bias,
        grad_w_fc1,
        grad_bias_fc1,
        grad_w_fc2,
        grad_bias_fc2,
    )
    return (grad_input, grad_list)


def gather_weights(F, r, own):
    return pl.pallas_call(
        functools.partial(gather_kernel, F, r),
        out_shape=jax.ShapeDtypeStruct(PIECES, jnp.bfloat16),
        in_specs=[pl.BlockSpec(memory_space=pltpu.VMEM)],
        out_specs=pl.BlockSpec(memory_space=pltpu.VMEM),
        scratch_shapes=[pltpu.VMEM(PIECES, jnp.bfloat16), pltpu.SemaphoreType.DMA((3, 32)), pltpu.SemaphoreType.DMA((3, 32))],
        compiler_params=pltpu.CompilerParams(collective_id=0, has_side_effects=True, vmem_limit_bytes=60 * MIB),
    )(own)


def scatter_grads(F, r, pieces):
    return pl.pallas_call(
        functools.partial(scatter_kernel, F, r),
        out_shape=jax.ShapeDtypeStruct((3, 96, 768), jnp.float32),
        in_specs=[pl.BlockSpec(memory_space=pltpu.VMEM)],
        out_specs=pl.BlockSpec(memory_space=pltpu.VMEM),
        scratch_shapes=[
            pltpu.VMEM(PIECES, jnp.bfloat16),
            pltpu.VMEM((3, 4, 4, 2, 96, 768), jnp.bfloat16),
            pltpu.VMEM((3, 3, 96, 768), jnp.bfloat16),
            pltpu.SemaphoreType.DMA((3, 32)),
            pltpu.SemaphoreType.DMA((3, 32)),
        ],
        compiler_params=pltpu.CompilerParams(collective_id=1, has_side_effects=True, vmem_limit_bytes=62 * MIB),
    )(pieces)


def per_device(
    F,
    r,
    images,
    tissue,
    pair_index,
    text_embed,
    logit_scale,
    ln1_gain,
    ln1_bias,
    w_qkv,
    bias_qv,
    w_out,
    bias_out,
    ln2_gain,
    ln2_bias,
    w_fc1,
    bias_fc1,
    w_fc2,
    bias_fc2,
    cotangent,
):
    local_images, slot_count, model_width = images.shape
    per_micro = local_images
    MICRO = 1
    own = jnp.stack([jnp.concatenate([pregather(w_qkv.T, F, r), pregather(w_out.T, F, r)], 0), pregather(w_fc1.T, F, r), pregather(w_fc2, F, r)], 0)
    full = to_natural(gather_weights(F, r, own))
    w_qkv_t = full[0, :, :72].reshape(-1, model_width)
    w_out_t = full[0, :, 72:].reshape(-1, model_width)
    w_fc1_t = full[1].reshape(-1, model_width)
    w_fc2_f = full[2].reshape(-1, model_width)
    tissue_float = tissue.astype(jnp.float32)
    saved_all = []
    pooled_parts = []
    mixed_parts = []
    for micro_step in range(MICRO):
        params_full = (
            lax.all_gather(ln1_gain, ("dp", "fsdp"), axis=0, tiled=True),
            lax.all_gather(ln1_bias, ("dp", "fsdp"), axis=0, tiled=True),
            w_qkv_t.T,
            lax.all_gather(bias_qv, ("dp", "fsdp"), axis=0, tiled=True),
            w_out_t.T,
            lax.all_gather(bias_out, ("dp", "fsdp"), axis=0, tiled=True),
            lax.all_gather(ln2_gain, ("dp", "fsdp"), axis=0, tiled=True),
            lax.all_gather(ln2_bias, ("dp", "fsdp"), axis=0, tiled=True),
            w_fc1_t.T,
            lax.all_gather(bias_fc1, ("dp", "fsdp"), axis=0, tiled=True),
            w_fc2_f,
            lax.all_gather(bias_fc2, ("dp", "fsdp"), axis=0, tiled=True),
        )
        first_image = micro_step * per_micro
        token_rows = (
            images[first_image : first_image + per_micro]
            .reshape(-1, model_width)
            .astype(jnp.float32)
        )
        image_mask = tissue_float[first_image : first_image + per_micro]
        outputs, saved_state = forward_block(params_full, token_rows, image_mask)
        saved_all.append(saved_state)
        shaped = outputs.reshape(per_micro, slot_count, model_width)
        mixed_parts.append(shaped.astype(jnp.bfloat16))
        pooled_parts.append(jnp.sum(shaped, 1))
    mixed_out = jnp.concatenate(mixed_parts, 0)
    counts = jnp.sum(tissue_float, 1)[:, None]
    pooled = jnp.concatenate(pooled_parts, 0) / counts
    text_float = text_embed.astype(jnp.float32)
    text_unit = unit_rows(text_float).astype(jnp.bfloat16)
    image_float, unit_pull = jax.vjp(unit_rows, pooled)
    image_unit = image_float.astype(jnp.bfloat16)
    all_texts, all_images = (
        lax.all_gather(text_unit, ("dp", "fsdp"), axis=0, tiled=True),
        lax.all_gather(image_unit, ("dp", "fsdp"), axis=0, tiled=True),
    )
    all_pairs = lax.all_gather(pair_index, ("dp", "fsdp"), axis=0, tiled=True)
    total_texts = all_texts.shape[0]
    own_start = lax.axis_index(("dp", "fsdp")) * local_images
    logits = logit_scale * jnp.einsum(
        "id,jd->ij", image_unit, all_texts, preferred_element_type=jnp.float32
    )
    col_logits = logit_scale * jnp.einsum(
        "id,jd->ij", all_images, text_unit, preferred_element_type=jnp.float32
    )
    row_top = jnp.max(logits, 1, keepdims=True)
    row_lse = row_top[:, 0] + jnp.log(jnp.sum(jnp.exp(logits - row_top), 1))
    col_top = jnp.max(col_logits, 0, keepdims=True)
    col_lse = col_top[0] + jnp.log(jnp.sum(jnp.exp(col_logits - col_top), 0))
    pair_match = (lax.broadcasted_iota(jnp.int32, logits.shape, 1) == pair_index[:, None]).astype(
        jnp.float32
    )
    paired_terms = jnp.sum(logits * pair_match, 1)
    all_row_lse, all_col_lse, all_paired = (
        lax.all_gather(row_lse, ("dp", "fsdp"), axis=0, tiled=True),
        lax.all_gather(col_lse, ("dp", "fsdp"), axis=0, tiled=True),
        lax.all_gather(paired_terms, ("dp", "fsdp"), axis=0, tiled=True),
    )
    loss_value = (jnp.sum(all_row_lse) + jnp.sum(all_col_lse) - 2.0 * jnp.sum(all_paired)) / (
        2.0 * total_texts
    )
    row_grad = (
        0.5 * (jnp.exp(logits - row_lse[:, None]) + jnp.exp(logits - all_col_lse[None, :]))
        - pair_match
    )
    grad_raw = (logit_scale * row_grad).astype(jnp.bfloat16)
    grad_unit = jnp.einsum("ij,jd->id", grad_raw, all_texts, preferred_element_type=jnp.float32)
    own_columns = lax.broadcasted_iota(jnp.int32, col_logits.shape, 1) + own_start
    col_match = (own_columns == all_pairs[:, None]).astype(jnp.float32)
    col_grad = (
        0.5 * (jnp.exp(col_logits - all_row_lse[:, None]) + jnp.exp(col_logits - col_lse[None, :]))
        - col_match
    )
    col_raw = (logit_scale * col_grad).astype(jnp.bfloat16)
    grad_text_unit = jnp.einsum(
        "ij,id->jd", col_raw, all_images, preferred_element_type=jnp.float32
    )
    text_value, text_pull = jax.vjp(unit_rows, text_float)
    text_grad = text_pull(grad_text_unit)[0]
    grad_pooled = unit_pull(grad_unit)[0] / counts
    grad_totals = None
    input_parts = []
    for micro_step in range(MICRO):
        params_full = (
            lax.all_gather(ln1_gain, ("dp", "fsdp"), axis=0, tiled=True),
            lax.all_gather(ln1_bias, ("dp", "fsdp"), axis=0, tiled=True),
            w_qkv_t.T,
            lax.all_gather(bias_qv, ("dp", "fsdp"), axis=0, tiled=True),
            w_out_t.T,
            lax.all_gather(bias_out, ("dp", "fsdp"), axis=0, tiled=True),
            lax.all_gather(ln2_gain, ("dp", "fsdp"), axis=0, tiled=True),
            lax.all_gather(ln2_bias, ("dp", "fsdp"), axis=0, tiled=True),
            w_fc1_t.T,
            lax.all_gather(bias_fc1, ("dp", "fsdp"), axis=0, tiled=True),
            w_fc2_f,
            lax.all_gather(bias_fc2, ("dp", "fsdp"), axis=0, tiled=True),
        )
        first_image = micro_step * per_micro
        token_rows = (
            images[first_image : first_image + per_micro]
            .reshape(-1, model_width)
            .astype(jnp.float32)
        )
        image_mask = tissue_float[first_image : first_image + per_micro]
        grad_block = (
            cotangent[first_image : first_image + per_micro].astype(jnp.float32)
            + grad_pooled[first_image : first_image + per_micro][:, None, :]
        ) * image_mask[:, :, None]
        grad_input, grad_list = backward_block(
            params_full,
            token_rows,
            image_mask,
            saved_all[micro_step],
            grad_block.reshape(-1, model_width),
        )
        input_parts.append(grad_input.reshape(per_micro, slot_count, model_width))
        if grad_totals is None:
            grad_totals = grad_list
        else:
            grad_totals = jax.tree.map(jnp.add, grad_totals, grad_list)
    natural = jnp.stack([jnp.concatenate([grad_totals[2].T.reshape(32, 72, -1), grad_totals[4].T.reshape(32, 24, -1)], 1), grad_totals[8].T.reshape(32, 96, -1), grad_totals[10].reshape(32, 96, -1)], 0)
    mine = scatter_grads(F, r, to_pieces(natural.astype(jnp.bfloat16)))
    shares = (
        lax.psum_scatter(grad_totals[0], ("dp", "fsdp"), scatter_dimension=0, tiled=True),
        lax.psum_scatter(grad_totals[1], ("dp", "fsdp"), scatter_dimension=0, tiled=True),
        postscatter(mine[0, :72], F, r).T,
        lax.psum_scatter(grad_totals[3], ("dp", "fsdp"), scatter_dimension=0, tiled=True),
        postscatter(mine[0, 72:], F, r).T,
        lax.psum_scatter(grad_totals[5], ("dp", "fsdp"), scatter_dimension=0, tiled=True),
        lax.psum_scatter(grad_totals[6], ("dp", "fsdp"), scatter_dimension=0, tiled=True),
        lax.psum_scatter(grad_totals[7], ("dp", "fsdp"), scatter_dimension=0, tiled=True),
        postscatter(mine[1], F, r).T,
        lax.psum_scatter(grad_totals[9], ("dp", "fsdp"), scatter_dimension=0, tiled=True),
        postscatter(mine[2], F, r),
        lax.psum_scatter(grad_totals[11], ("dp", "fsdp"), scatter_dimension=0, tiled=True),
    )
    input_grad = jnp.concatenate(input_parts, 0)
    return (
        mixed_out,
        input_grad,
        loss_value,
        text_grad,
        shares[0],
        shares[1],
        shares[2],
        shares[3],
        shares[4],
        shares[5],
        shares[6],
        shares[7],
        shares[8],
        shares[9],
        shares[10],
        shares[11],
    )


def solution(mesh):
    F = mesh.shape["fsdp"]
    r = mesh.shape["dp"] * F // GROUPS
    in_specs = (
        P(("dp", "fsdp"), None, None),
        P(("dp", "fsdp"), None),
        P(("dp", "fsdp")),
        P(("dp", "fsdp"), None),
        P(),
        P(("dp", "fsdp")),
        P(("dp", "fsdp")),
        P(None, ("dp", "fsdp")),
        P(("dp", "fsdp")),
        P(None, ("dp", "fsdp")),
        P(("dp", "fsdp")),
        P(("dp", "fsdp")),
        P(("dp", "fsdp")),
        P(None, ("dp", "fsdp")),
        P(("dp", "fsdp")),
        P(("dp", "fsdp"), None),
        P(("dp", "fsdp")),
        P(("dp", "fsdp"), None, None),
    )
    out_specs = (
        P(("dp", "fsdp"), None, None),
        P(("dp", "fsdp"), None, None),
        P(),
        P(("dp", "fsdp"), None),
        P(("dp", "fsdp")),
        P(("dp", "fsdp")),
        P(None, ("dp", "fsdp")),
        P(("dp", "fsdp")),
        P(None, ("dp", "fsdp")),
        P(("dp", "fsdp")),
        P(("dp", "fsdp")),
        P(("dp", "fsdp")),
        P(None, ("dp", "fsdp")),
        P(("dp", "fsdp")),
        P(("dp", "fsdp"), None),
        P(("dp", "fsdp")),
    )
    return jax.shard_map(
        functools.partial(per_device, F, r), mesh=mesh, in_specs=in_specs, out_specs=out_specs, check_vma=False
    )
```

```python
import functools
import math

import jax
import jax.numpy as jnp
from jax import lax
from jax.experimental import pallas as pl
from jax.experimental.pallas import tpu as pltpu
from jax.sharding import PartitionSpec as P

MESH = pl.DeviceIdType.MESH
MIB = 1024 * 1024
GROUPS = 32
D = 768
HEADS = 12
PAD = 208
IMG = 3
TOK = IMG * PAD
QKV_ROWS, OUT_ROWS = 72, 24
ROWS = 96
VMEM_LIMIT = 63 * MIB
EPS = 1e-6
BF, F32 = jnp.bfloat16, jnp.float32


def dot(a, b):
    return lax.dot_general(a, b, (((1,), (0,)), ((), ())), preferred_element_type=F32)


def dot_nt(a, b):
    return lax.dot_general(a, b, (((1,), (1,)), ((), ())), preferred_element_type=F32)


def dot_exact(a, b, dims):
    return lax.dot_general(a, b, (dims, ((), ())), preferred_element_type=F32, precision=lax.Precision.HIGHEST)


def iota(shape, dim):
    return lax.broadcasted_iota(jnp.int32, shape, dim)


def split(numbers, by):
    quotient = jnp.floor((numbers.astype(F32) + 0.5) * (1.0 / by)).astype(jnp.int32)
    return quotient, numbers - quotient * by


class Pos:
    def __init__(p, F, r, n):
        p.F, p.r, p.n = F, r, n
        p.index = lax.axis_index("dp") * F + lax.axis_index("fsdp")
        p.g, p.rho = lax.div(p.index, r), lax.rem(p.index, r)
        p.c, p.z = lax.rem(p.g, 2), lax.rem(lax.div(p.g, 2), 4)
        p.x, p.y = lax.rem(lax.div(p.g, 8), 2), lax.div(p.g, 16)
        p.l = p.y + p.c * (p.x - p.y)
        p.f = p.x + p.c * (p.y - p.x)
        c, x, y, z = p.c, p.x, p.y, p.z
        p.sib = p.chip(y, x, z, 1 - c)
        p.fn = p.chip(y + c * (1 - 2 * y), x + (1 - c) * (1 - 2 * x), z, c)
        p.ln = p.chip(y + (1 - c) * (1 - 2 * y), x + c * (1 - 2 * x), z, c)
        p.up = p.chip(y, x, jnp.minimum(z + 1, 3), c)
        p.dn = p.chip(y, x, jnp.maximum(z - 1, 0), c)
        p.plane = lax.div(p.g, 2) * r + p.rho

    def device(p, linear):
        return (lax.div(linear, p.F), lax.rem(linear, p.F))

    def chip(p, y, x, z, c):
        return p.device((((y * 2 + x) * 4 + z) * 2 + c) * p.r + p.rho)

    def in_plane(p, q):
        return p.device((lax.div(q, p.r) * 2 + p.c) * p.r + lax.rem(q, p.r))

    def block(p, l, z, f):
        y, x = l + p.c * (f - l), f + p.c * (l - f)
        return p.chip(y, x, z, p.c)


def group_of(block):
    c = block // 16 if isinstance(block, int) else jnp.where(block >= 16, 1, 0)
    rest = block - c * 16
    if isinstance(block, int):
        l, z, f = rest // 8, rest // 2 % 4, rest % 2
    else:
        l = jnp.where(rest >= 8, 1, 0)
        zf = rest - 8 * l
        z = jnp.where(zf >= 2, 1, 0) + jnp.where(zf >= 4, 1, 0) + jnp.where(zf >= 6, 1, 0)
        f = zf - 2 * z
    y, x = l + c * (f - l), f + c * (l - f)
    return ((y * 2 + x) * 4 + z) * 2 + c


def enter(p):
    bar = pltpu.get_barrier_semaphore()
    half = p.n // 2

    def greet(i, carry):
        pl.semaphore_signal(bar, inc=1, device_id=p.in_plane(lax.rem(p.plane + i, half)), device_id_type=MESH)
        return carry

    lax.fori_loop(1, half, greet, 0)
    pl.semaphore_signal(bar, inc=1, device_id=p.sib, device_id_type=MESH)
    pl.semaphore_wait(bar, half)


class Gather:
    def __init__(s, p, held, send, recv):
        s.p, s.held, s.send, s.recv = p, held, send, recv

    def cp(s, at, ks, kr, dev):
        ref = s.held.at[at]
        return pltpu.make_async_remote_copy(
            src_ref=ref, dst_ref=ref, send_sem=s.send.at[ks], recv_sem=s.recv.at[kr], device_id=dev, device_id_type=MESH
        )

    def first(s):
        p = s.p
        return s.cp((p.c, p.l, p.z, p.f), 0, 0, p.fn)

    def first_in(s):
        p = s.p
        return s.cp((p.c, p.l, p.z, 1 - p.f), 0, 0, p.fn)

    def f_of(s, b):
        return s.p.f + b * (1 - 2 * s.p.f)

    def up(s, zz, b):
        return s.cp((s.p.c, s.p.l, zz, s.f_of(b)), 1 + 2 * zz + b, 1 + 2 * zz + b, s.p.up)

    def dn(s, zz, b):
        return s.cp((s.p.c, s.p.l, zz, s.f_of(b)), 9 + 2 * zz + b, 1 + 2 * zz + b, s.p.dn)

    def last(s, zz):
        return s.cp((s.p.c, s.p.l, zz), 17 + zz, 9 + zz, s.p.ln)

    def last_in(s, zz):
        return s.cp((s.p.c, 1 - s.p.l, zz), 17 + zz, 9 + zz, s.p.ln)

    def core(s, l, zz):
        return s.cp((s.p.c, l, zz), 21 + 4 * l + zz, 13 + 4 * l + zz, s.p.sib)

    def core_in(s, l, zz):
        return s.cp((1 - s.p.c, l, zz), 21 + 4 * l + zz, 13 + 4 * l + zz, s.p.sib)

    def own(s, b):
        p = s.p
        if b:
            s.first_in().wait_recv()
        else:
            s.first().start()

        @pl.when(p.z < 3)
        def _():
            s.up(p.z, b).start()

        @pl.when(p.z > 0)
        def _():
            s.dn(p.z, b).start()

        if b:
            s.last(p.z).start()
            s.core(p.l, p.z).start()

    def line(s, h, b):
        p = s.p

        @pl.when(p.z - h >= 0)
        def _():
            zz = p.z - h
            s.up(zz, b).wait_recv()

            @pl.when(p.z < 3)
            def _():
                s.up(zz, b).start()

            if b:
                s.last(zz).start()
                s.core(p.l, zz).start()

        @pl.when(p.z + h <= 3)
        def _():
            zz = p.z + h
            s.dn(zz, b).wait_recv()

            @pl.when(p.z > 0)
            def _():
                s.dn(zz, b).start()

            if b:
                s.last(zz).start()
                s.core(p.l, zz).start()

    def arrive(s, h):
        p = s.p

        def one(zz):
            s.last_in(zz).wait_recv()
            s.core(1 - p.l, zz).start()

        if h == 0:
            one(p.z)
        else:

            @pl.when(p.z - h >= 0)
            def _():
                one(p.z - h)

            @pl.when(p.z + h <= 3)
            def _():
                one(p.z + h)

    def finish(s):
        for zz in range(4):
            for l in range(2):
                s.core_in(l, zz).wait_recv()

    def drain(s):
        p = s.p
        s.first().wait_send()
        for zz in range(4):

            @pl.when((p.z < 3) & (zz <= p.z))
            def _():
                s.up(zz, 0).wait_send()
                s.up(zz, 1).wait_send()

            @pl.when((p.z > 0) & (zz >= p.z))
            def _():
                s.dn(zz, 0).wait_send()
                s.dn(zz, 1).wait_send()

            s.last(zz).wait_send()
            for l in range(2):
                s.core(l, zz).wait_send()


class Scatter:
    def __init__(s, p, sums, room, ends, send, recv):
        s.p, s.sums, s.room, s.ends, s.send, s.recv = p, sums, room, ends, send, recv

    def cp(s, src, dst, ks, kr, dev):
        return pltpu.make_async_remote_copy(
            src_ref=src, dst_ref=dst, send_sem=s.send.at[ks], recv_sem=s.recv.at[kr], device_id=dev, device_id_type=MESH
        )

    def core_cp(s, l):
        return s.cp(s.sums.at[1 - s.p.c, l], s.room(l), 1 + l, 1 + l, s.p.sib)

    def side_cp(s, zz):
        return s.cp(s.sums.at[s.p.c, 1 - s.p.l, zz], s.room(2).at[zz], 3 + zz, 3 + zz, s.p.ln)

    def f_of(s, b):
        return 1 - s.p.f if b == 0 else s.p.f

    def here(s, zz, b):
        return s.sums.at[s.p.c, s.p.l, zz, s.f_of(b)]

    def up_far(s, zz, b):
        return s.cp(s.here(zz, b), s.room(3).at[zz, b], 7 + 2 * zz + b, 7 + 2 * zz + b, s.p.up)

    def up_end(s, zz, b):
        return s.cp(s.here(zz, b), s.ends.at[b], 7 + 2 * zz + b, 15 + b, s.p.up)

    def down(s, zz, b):
        return s.cp(s.here(zz, b), s.room(3).at[zz, b], 15 + 2 * zz + b, 7 + 2 * zz + b, s.p.dn)

    def last_cp(s):
        return s.cp(s.here(s.p.z, 0), s.ends.at[2], 0, 0, s.p.fn)

    def core_send(s, l):
        s.core_cp(l).start()

    def core_add(s, l):
        s.core_cp(l).wait_recv()
        room = s.room(l)

        def body(zz, carry):
            for f in range(2):
                ref = s.sums.at[s.p.c, l, zz, f]
                ref[...] = (ref[...].astype(F32) + room[zz, f].astype(F32)).astype(BF)
            return carry

        lax.fori_loop(0, 4, body, 0)

    def add(s, zz, b, ref):
        total = s.here(zz, b)
        total[...] = (total[...].astype(F32) + ref[...].astype(F32)).astype(BF)

    def by_distance(s, h, fn):
        p = s.p
        if h == 0:
            fn(p.z)
            return

        @pl.when(p.z + h <= 3)
        def _():
            fn(p.z + h)

        @pl.when(p.z - h >= 0)
        def _():
            fn(p.z - h)

    def side_send(s):
        for h in (3, 2, 1, 0):
            s.by_distance(h, lambda zz: s.side_cp(zz).start())

    def side_add(s, h):
        def one(zz):
            s.side_cp(zz).wait_recv()
            for f in (0, 1):
                total = s.sums.at[s.p.c, s.p.l, zz, f]
                total[...] = (total[...].astype(F32) + s.room(2)[zz, f].astype(F32)).astype(BF)

        s.by_distance(h, one)

    def line(s, h, b):
        p = s.p
        if h > 0:

            @pl.when(p.z + h <= 3)
            def _():
                zz = p.z + h

                @pl.when(p.z > 0)
                def _():
                    s.up_far(zz, b).wait_recv()
                    s.add(zz, b, s.room(3).at[zz, b])

                if h == 1:
                    s.up_end(zz, b).start()
                else:
                    s.up_far(zz, b).start()

            @pl.when(p.z - h >= 0)
            def _():
                zz = p.z - h

                @pl.when(p.z < 3)
                def _():
                    s.down(zz, b).wait_recv()
                    s.add(zz, b, s.room(3).at[zz, b])

                s.down(zz, b).start()

        else:

            @pl.when(p.z > 0)
            def _():
                s.up_end(p.z, b).wait_recv()
                s.add(p.z, b, s.ends.at[b])

            @pl.when(p.z < 3)
            def _():
                s.down(p.z, b).wait_recv()
                s.add(p.z, b, s.room(3).at[p.z, b])

            if b == 0:
                s.last_cp().start()

    def final(s):
        s.last_cp().wait_recv()
        return s.here(s.p.z, 1)[...].astype(F32) + s.ends[2].astype(F32)

    def drain(s):
        p = s.p
        for l in range(2):
            s.core_cp(l).wait_send()
        for zz in range(4):
            s.side_cp(zz).wait_send()

            @pl.when(zz > p.z)
            def _():
                s.up_far(zz, 0).wait_send()
                s.up_far(zz, 1).wait_send()

            @pl.when(zz < p.z)
            def _():
                s.down(zz, 0).wait_send()
                s.down(zz, 1).wait_send()

        s.last_cp().wait_send()


def qkv_runs(start, stop):
    runs, row = [], start
    while row < stop:
        chip, inside = divmod(row, 2 * QKV_ROWS)
        z, x, y = chip % 4, chip // 4 % 2, chip // 8
        first = inside < ROWS
        until = min(stop, chip * 2 * QKV_ROWS + (ROWS if first else 2 * QKV_ROWS))
        low = inside if first else inside - ROWS
        at = (0, y, z, x) if first else (1, x, z, y)
        runs.append((at, low, low + until - row))
        row = until
    return runs


def out_runs(start, stop):
    runs, row = [], start
    while row < stop:
        chip, inside = divmod(row, 2 * OUT_ROWS)
        z, x, y = chip % 4, chip // 4 % 2, chip // 8
        until = min(stop, (chip + 1) * 2 * OUT_ROWS)
        low = inside + 2 * (QKV_ROWS - OUT_ROWS) // 2
        runs.append(((1, x, z, y), low, low + until - row))
        row = until
    return runs


def load_runs(ref, runs, lanes=slice(None)):
    return jnp.concatenate([ref[at + (slice(a, b), lanes)] for at, a, b in runs], 0)


def store_runs(ref, runs, value):
    row = 0
    for at, a, b in runs:
        ref[at + (slice(a, b), slice(None))] = value[row : row + b - a]
        row += b - a


def slabs(ref, first, count):
    return jnp.concatenate([ref[first + k] for k in range(count)], 1)


def norm_parts(values):
    centered = values - jnp.mean(values, -1, keepdims=True)
    inverse = lax.rsqrt(jnp.mean(centered * centered, -1, keepdims=True) + EPS)
    return centered * inverse, inverse


def norm_grad(grad, gain, normalized, inverse):
    h = grad * gain
    return (h - jnp.mean(h, -1, keepdims=True) - normalized * jnp.mean(h * normalized, -1, keepdims=True)) * inverse


def gelu_parts(x):
    z = jnp.abs(x) * math.sqrt(0.5)
    under = 1.0 + 0.3275911 * z
    t = pl.reciprocal(under, approx=True)
    t = t * (2.0 - under * t)
    bell = jnp.exp(-0.5 * x * x)
    poly = ((((1.061405429 * t - 1.453152027) * t + 1.421413741) * t - 0.284496736) * t + 0.254829592) * t
    tail = 0.5 * poly * bell
    cdf = jnp.where(x >= 0, 1.0 - tail, tail)
    return x * cdf, cdf + x * bell * (1.0 / math.sqrt(2.0 * math.pi))


CUTS = ((0, 48), (48, 48), (96, 48), (144, 64))


def by_rows(fn):
    def body(i, carry):
        for start, size in CUTS:
            fn(i, pl.ds(pl.multiple_of(i * PAD + start, 16), size))
        return carry

    lax.fori_loop(0, IMG, body, 0)


def layer_kernel(
    F,
    r,
    n,
    qo_ref,
    f1_ref,
    f2_ref,
    small_ref,
    img_ref,
    cot_ref,
    mask_ref,
    text_ref,
    scale_ref,
    mix_ref,
    res_ref,
    loss_ref,
    tg_ref,
    dqo_ref,
    df1_ref,
    df2_ref,
    dvec_ref,
    W,
    G,
    room,
    ends,
    small,
    swap_grad,
    norm1,
    qkv,
    att,
    lse,
    sec,
    act,
    slope,
    grad2,
    temp,
    vec,
    vec_grad,
    pooled,
    row_grad,
    pair_rows,
    units,
    vec_out,
    vec_core,
    vec_in,
    g_send,
    g_recv,
    s_send,
    s_recv,
    misc,
    credit,
):
    p = Pos(F, r, n)
    half = n // 2
    total = IMG * n
    per_group = IMG * r
    small_rows = small.shape[4]
    qo_g, f1_g, f2_g = (Gather(p, W.at[m], g_send.at[m], g_recv.at[m]) for m in range(3))
    sm_g = Gather(p, small, g_send.at[3], g_recv.at[3])

    def remote(src, dst, k, dev):
        return pltpu.make_async_remote_copy(
            src_ref=src, dst_ref=dst, send_sem=misc.at[2 * k], recv_sem=misc.at[2 * k + 1], device_id=dev, device_id_type=MESH
        )

    W[1, p.c, p.l, p.z, p.f] = f1_ref[...]
    W[2, p.c, p.l, p.z, p.f] = f2_ref[...]
    small[p.c, p.l, p.z, p.f] = small_ref[...]
    vec_grad[...] = jnp.zeros(vec_grad.shape, F32)
    enter(p)
    swap_copy = remote(qo_ref.at[1 - p.c], G.at[0, 0, 0, 0, 0], 0, p.sib)
    swap_copy.start()
    sm_g.own(0)
    f1_early = False
    swap_copy.wait_recv()
    W[0, p.c, p.l, p.z, p.f] = (qo_ref[p.c].astype(F32) + G[0, 0, 0, 0, 0].astype(F32)).astype(BF)
    qo_g.own(0)
    sm_g.own(1)
    qo_g.own(1)
    sm_g.line(1, 0)
    sm_g.line(1, 1)
    sm_g.arrive(0)
    qo_g.line(1, 0)
    sm_g.line(2, 0)
    sm_g.line(2, 1)
    sm_g.arrive(1)
    qo_g.line(1, 1)
    qo_g.arrive(0)
    sm_g.line(3, 0)
    sm_g.line(3, 1)
    sm_g.arrive(2)
    sm_g.arrive(3)
    sm_g.finish()


    def picked(k):
        source, target = iota((GROUPS, GROUPS * small_rows), 1), iota((GROUPS, GROUPS * small_rows), 0)
        return dot(jnp.where(source == target * small_rows + k, 1.0, 0.0).astype(BF), small[...].reshape(GROUPS * small_rows, 128)).astype(BF)

    table = [(0, 0, 24, 0), (0, 24, 24, 0), (0, 48, 24, 0), (0, 72, 24, 0), (0, 96, 24, 0), (1, 0, 24, 0), (1, 24, 48, 0), (1, 24, 48, D)]
    table += [(2, 0, 96, D * q) for q in range(4)]

    def spread(k, offset, width, base):
        owner, inside = split(iota((1, D), 1) + base, width)
        names = iota((GROUPS, 1), 0)
        names = names if k == 2 else group_of(names)
        mask = jnp.where(names == owner, 1.0, 0.0)
        places = jnp.where(iota((128, D), 0) == inside + offset, 1.0, 0.0)
        return mask, places

    @pl.when(p.index >= 0)
    def _():
      message_rows = [picked(k) for k in range(3)]
      for row, (k, offset, width, base) in enumerate(table):
        mask, places = spread(k, offset, width, base)
        vec[row : row + 1, :] = jnp.sum(mask * dot(message_rows[k], places.astype(BF)), 0, keepdims=True)

    def first_norm(i, rows):
        normalized, _ = norm_parts(img_ref[rows].astype(F32))
        norm1[rows] = (normalized * vec[0:1] + vec[1:2]).astype(BF)

    by_rows(first_norm)
    qo_g.line(2, 0)
    qo_g.line(2, 1)
    f1_g.own(0)
    qo_g.arrive(1)
    f1_g.own(1)
    qo_g.line(3, 0)
    qo_g.line(3, 1)
    qo_g.arrive(2)
    qo_g.arrive(3)
    qo_g.finish()

    for j in range(9):
        part = dot_nt(norm1[...], load_runs(W.at[0], qkv_runs(256 * j, 256 * j + 256)))
        if j < 3:
            part = part + vec[6:7, 256 * j : 256 * j + 256]
        elif j >= 6:
            part = part + vec[7:8, 256 * (j - 6) : 256 * (j - 6) + 256]
        part = part.astype(BF)
        qkv[2 * j] = part[:, :128]
        qkv[2 * j + 1] = part[:, 128:]
        if j == 2:
            f1_g.line(1, 0)
            f1_g.line(1, 1)
            f1_g.arrive(0)
        if j == 6:
            f1_g.line(2, 0)
            f1_g.line(2, 1)
            f2_g.own(0)
            f1_g.arrive(1)
            f2_g.own(1)

    low = iota((1, 128), 1) < 64

    def halves(value):
        zero = jnp.zeros_like(value)
        return jnp.where(low, value, zero), jnp.where(low, zero, value)

    def head_pair(i, pair):
        rows = pl.ds(pl.multiple_of(i * PAD, 16), PAD)
        return rows, qkv[pair, rows], qkv[6 + pair, rows], qkv[12 + pair, rows]

    def attend(it, carry):
        i, pair = lax.div(it, 6), lax.rem(it, 6)
        rows, q, k, v = head_pair(i, pair)
        v_t = v.T
        bars = jnp.concatenate([jnp.where(mask_ref[rows] > 0, 0.0, -1e30)] * 2, 1)[:, :PAD]
        parts = []
        for h, k_h in enumerate(halves(k * jnp.asarray(0.125, BF))):
            scores = dot_nt(k_h, q) + bars
            top = jnp.max(scores, 0, keepdims=True)
            terms = jnp.exp(scores - top)
            amount = jnp.sum(terms, 0, keepdims=True)
            lse[it * 2 + h] = top + jnp.log(amount)
            parts.append(dot(v_t[64 * h : 64 * h + 64], terms.astype(BF)) * (1.0 / amount))
        att[pair, rows] = jnp.concatenate(parts, 0).T.astype(BF)
        return carry

    lax.fori_loop(0, 4, attend, 0)
    f1_g.line(3, 0)
    f1_g.line(3, 1)
    f1_g.arrive(2)
    lax.fori_loop(4, 8, attend, 0)
    f1_g.arrive(3)
    f2_g.line(1, 0)
    f2_g.line(1, 1)
    f2_g.arrive(0)
    lax.fori_loop(8, 14, attend, 0)
    f2_g.line(2, 0)
    f2_g.line(2, 1)
    f2_g.arrive(1)
    lax.fori_loop(14, 18, attend, 0)

    attended = slabs(att, 0, 6)
    for j in range(3):
        lanes = slice(256 * j, 256 * j + 256)
        part = dot_nt(attended, load_runs(W.at[0], out_runs(256 * j, 256 * j + 256)))
        res_ref[:, lanes] = img_ref[:, lanes].astype(F32) + part + vec[2:3, lanes]

    def second_norm(i, rows):
        normalized, _ = norm_parts(res_ref[rows])
        value = (normalized * vec[3:4] + vec[4:5]).astype(BF)
        for k in range(6):
            sec[k, rows] = value[:, 128 * k : 128 * k + 128]

    by_rows(second_norm)
    f1_g.finish()

    def image_rows(i):
        return pl.ds(pl.multiple_of(i * PAD, 16), PAD)

    def expand(it, carry):
        q, rows = lax.div(it, IMG), image_rows(lax.rem(it, IMG))
        left = jnp.concatenate([sec[k, rows] for k in range(6)], 1)
        pre = dot_nt(left, W[1, lax.div(q, 2), lax.rem(q, 2)].reshape(D, D)) + vec[pl.ds(8 + q, 1), :]
        value, derivative = gelu_parts(pre)
        act[q, rows] = value.astype(BF)
        slope[q, rows] = derivative.astype(BF)
        return carry

    lax.fori_loop(0, 3, expand, 0)
    f2_g.line(3, 0)
    f2_g.line(3, 1)
    f2_g.arrive(2)
    lax.fori_loop(3, 9, expand, 0)
    f2_g.arrive(3)
    lax.fori_loop(9, 12, expand, 0)
    f2_g.finish()

    def contract(hidden_units, m):
        def body(i, carry):
            rows = image_rows(i)
            for j in range(3):
                lanes = slice(256 * j, 256 * j + 256)
                left = jnp.concatenate([hidden_units[q, rows] for q in range(4)], 1)
                temp[rows, lanes] = dot(left, W[m, :, :, :, :, :, lanes].reshape(4 * D, 256))
            return carry

        lax.fori_loop(0, IMG, body, 0)

    contract(act, 2)

    def wide(column):
        return jnp.concatenate([column] * 6, 1)

    pooled[...] = jnp.zeros(pooled.shape, F32)
    for i in range(IMG):
        sums, count = jnp.zeros((1, D), F32), jnp.zeros((1, 128), F32)
        for start, size in CUTS:
            rows = pl.ds(i * PAD + start, size)
            mask = mask_ref[rows]
            outputs = (res_ref[rows] + temp[rows] + vec[5:6]) * wide(mask)
            mix_ref[rows] = outputs.astype(BF)
            sums = sums + jnp.sum(outputs, 0, keepdims=True)
            count = count + jnp.sum(mask, 0, keepdims=True)
        pooled[i : i + 1, :] = sums / wide(count)
        pooled[8 + i : 9 + i, :] = wide(count)

    def unit(values):
        inverse = lax.rsqrt(jnp.sum(values * values, -1, keepdims=True) + EPS)
        return values * inverse, inverse

    def unit_grad(grad, values, inverse):
        return inverse * grad - inverse * inverse * inverse * values * jnp.sum(values * grad, -1, keepdims=True)

    own_pooled = pooled[0:8]
    image_unit, image_inverse = unit(own_pooled)
    image_unit = image_unit.astype(BF)
    message = jnp.zeros((32, 128), F32)
    for k in range(6):
        at = jnp.where((iota((32, 8), 0) == iota((32, 8), 1) + IMG * k) & (iota((32, 8), 1) < IMG), 1.0, 0.0).astype(BF)
        message = message + dot(at, image_unit[:, 128 * k : 128 * k + 128])
    units[p.c, p.plane] = message.astype(BF)

    def push(i, carry):
        q = lax.rem(p.plane + i, half)
        remote(units.at[p.c, p.plane], units.at[p.c, p.plane], 1, p.in_plane(q)).start()
        return carry

    lax.fori_loop(1, half, push, 0)
    all_but_own = remote(units.at[p.c, pl.ds(0, half - 1)], units.at[p.c, pl.ds(0, half - 1)], 1, p.sib)

    def gathered(source_chunks, chunk_rows, row_of, tiles, base):
        results = []
        for k in range(tiles):
            value = jnp.zeros((total, 128), F32)
            for number, chunk in source_chunks:
                owner, inside = split(iota((1, chunk_rows), 1), base)
                target = row_of(owner, inside, number, k)
                value = value + dot(jnp.where(iota((total, chunk_rows), 0) == target, 1.0, 0.0).astype(BF), chunk)
            results.append(value)
        return results

    def text_row(owner, inside, number, k):
        at = inside - 3 - per_group * k
        group = group_of(owner + 8 * number)
        return jnp.where((at >= 0) & (at < per_group), group * per_group + at, -1)

    chunks = [(2 * c + l, small[c, l].reshape(8 * small_rows, 128)) for c in range(2) for l in range(2)]
    tiles = gathered(chunks, 8 * small_rows, text_row, 7, small_rows)
    for b in range(r):
        for k in range(6):
            G[1, b // 16, b // 8 % 2, b // 2 % 4, b % 2, :, 128 * k : 128 * k + 128] = tiles[k][ROWS * b : ROWS * b + ROWS].astype(BF)

    def texts():
        return jnp.concatenate([G[1, b // 16, b // 8 % 2, b // 2 % 4, b % 2] for b in range(r)], 0)

    pair_rows[...] = tiles[6]

    all_but_own.wait_recv()
    share = remote(units.at[p.c], units.at[p.c], 2, p.sib)
    share.start()
    remote(units.at[1 - p.c], units.at[1 - p.c], 2, p.sib).wait_recv()

    for k in range(6):

        def add_chunk(number, value, k=k):
            c, at = lax.div(number * 16, half), lax.rem(number * 16, half)
            owner, inside = split(iota((1, 512), 1), 32)
            q = owner + at
            t = inside - IMG * k
            if r == 1:
                linear = 2 * q + c
            else:
                chip, rho = split(q, r)
                linear = (2 * chip + c) * r + rho
            target = jnp.where((t >= 0) & (t < IMG), linear * IMG + t, -1)
            pick = jnp.where(iota((total, 512), 0) == target, 1.0, 0.0).astype(BF)
            return value + dot(pick, units[c, pl.ds(at, 16)].reshape(512, 128))

        value = lax.fori_loop(0, n // 16, add_chunk, jnp.zeros((total, 128), F32)).astype(BF)
        for b in range(r):
            G[2, b // 16, b // 8 % 2, b // 2 % 4, b % 2, :, 128 * k : 128 * k + 128] = value[ROWS * b : ROWS * b + ROWS]

    def block(m, b):
        return G[m, lax.div(b, 16), lax.rem(lax.div(b, 8), 2), lax.rem(lax.div(b, 2), 4), lax.rem(b, 2)]

    scale = scale_ref[0:1, 0:1]
    row = jnp.zeros((1, total), F32)

    def similar(b, col_top):
        rows = pl.ds(pl.multiple_of(b * ROWS, ROWS), ROWS)
        part = dot_nt(block(2, b), texts()) * scale
        temp[rows, :total] = part
        return jnp.maximum(col_top, jnp.max(part, 0, keepdims=True))

    col_top = lax.fori_loop(0, r, similar, row - jnp.inf)

    def by_blocks(fn):
        def body(b, carry):
            rows = pl.ds(pl.multiple_of(b * ROWS, ROWS), ROWS)
            part = temp[rows, :total]
            top = jnp.max(part, 1, keepdims=True)
            row_lse = top + jnp.log(jnp.sum(jnp.exp(part - top), 1, keepdims=True))
            match = jnp.where(iota((ROWS, total), 1) == pair_of(rows), 1.0, 0.0)
            return fn(b, part, row_lse, match, carry)

        return body

    def pair_of(rows):
        column = pair_rows[rows]
        return (column[:, 0:1] * 256.0 + column[:, 1:2]).astype(jnp.int32)

    def sums(b, part, row_lse, match, carry):
        col_sum, loss = carry
        paired = jnp.sum(jnp.sum(part * match, 1, keepdims=True), 0, keepdims=True)
        return col_sum + jnp.sum(jnp.exp(part - col_top), 0, keepdims=True), loss + jnp.sum(row_lse, 0, keepdims=True) - 2.0 * paired

    col_sum, loss = lax.fori_loop(0, r, by_blocks(sums), (row, jnp.zeros((1, 1), F32)))
    col_lse = col_top + jnp.log(col_sum)
    loss = (loss + jnp.sum(col_lse, 1, keepdims=True)) / (2.0 * total)
    loss_ref[...] = jnp.broadcast_to(loss, (8, 128))

    def own_of(places):
        return jnp.where((places == iota(places.shape, 0) + IMG * p.index) & (iota(places.shape, 0) < IMG), 1.0, 0.0).astype(BF)

    own = own_of(iota((8, total), 1))

    def similar_grad(b, part, row_lse, match, carry):
        grad_rows, grad_text = carry
        grad = 0.5 * (jnp.exp(part - row_lse) + jnp.exp(part - col_lse)) - match
        grad = (scale * grad).astype(BF)
        own_rows = own_of(iota((8, ROWS), 1) + b * ROWS)
        return grad_rows + dot(own_rows, grad), grad_text + dot(dot_nt(own, grad).astype(BF), block(2, b))

    grad_rows, grad_text = lax.fori_loop(0, r, by_blocks(similar_grad), (jnp.zeros((8, total), F32), jnp.zeros((8, D), F32)))
    grad_unit = dot(grad_rows.astype(BF), texts())
    row_grad[...] = unit_grad(grad_unit, own_pooled, image_inverse) / jnp.maximum(pooled[8:16], 1.0)
    text_rows = text_ref[...]
    _, text_inverse = unit(text_rows)
    tg_ref[...] = unit_grad(grad_text, text_rows, text_inverse)

    sc0, sc1, sc2 = (
        Scatter(p, G.at[m], area, ends.at[1 if m == 1 else 0], s_send.at[m], s_recv.at[m])
        for m, area in (
            (0, lambda k: room.at[k]),
            (1, lambda k: W.at[2, k // 2, k % 2] if isinstance(k, int) else W.at[2, 0, k]),
            (2, lambda k: room.at[k]),
        )
    )

    def out_grad(i, rows):
        return wide(mask_ref[rows]) * (cot_ref[rows].astype(F32) + row_grad[pl.ds(i, 1), :])

    def first_round(i, rows):
        value = out_grad(i, rows).astype(BF)
        grad2[rows] = value
        vec_grad[5:6] += jnp.sum(value.astype(F32), 0, keepdims=True)

    by_rows(first_round)
    order = ((1 - p.c, 1 - p.f), (p.c, 1 - p.l), (1 - p.c, p.f), (p.c, p.l))

    def weight_grad(m, at, left, right):
        left = left.T
        for j in range(3):
            lanes = slice(256 * j, 256 * j + 256)
            G[(m,) + at + (slice(None), slice(None), slice(None), lanes)] = (
                dot(left, right[:, lanes]).astype(BF).reshape(4, 2, ROWS, 256)
            )

    for step, at in enumerate(order):
        weight_grad(2, at, act[2 * at[0] + at[1]], grad2[...])
        if step == 0:
            sc2.core_send(1 - p.f)
        if step == 1:
            sc2.core_add(1 - p.l)
            sc2.side_send()
        if step == 2:
            sc2.core_send(p.f)
    sc2.core_add(p.l)
    sc2.side_add(3)
    sc2.line(3, 0)
    sc2.line(3, 1)
    for q in range(4):

        def back(i, carry, q=q):
            rows = image_rows(i)
            value = dot_nt(grad2[rows], W[2, q // 2, q % 2].reshape(D, D)) * slope[q, rows].astype(F32)
            value = value.astype(BF)
            slope[q, rows] = value
            vec_grad[8 + q : 9 + q] += jnp.sum(value.astype(F32), 0, keepdims=True)
            return carry

        lax.fori_loop(0, IMG, back, 0)
        if q == 1:
            sc2.side_add(2)
            sc2.line(2, 0)
            sc2.line(2, 1)
    f2_g.drain()
    line_up, line_down = p.z < 3, p.z > 0

    def give(k):
        pl.semaphore_signal(credit.at[k], inc=1, device_id=p.sib, device_id_type=MESH)
        pl.semaphore_signal(credit.at[k + 1], inc=1, device_id=p.ln, device_id_type=MESH)
        pl.semaphore_signal(credit.at[k + 4], inc=1, device_id=p.fn, device_id_type=MESH)

        @pl.when(line_down)
        def _():
            pl.semaphore_signal(credit.at[k + 2], inc=1, device_id=p.dn, device_id_type=MESH)

        @pl.when(line_up)
        def _():
            pl.semaphore_signal(credit.at[k + 3], inc=1, device_id=p.up, device_id_type=MESH)

    def take_line(k):
        pl.semaphore_wait(credit.at[k + 4], 1)

        @pl.when(line_up)
        def _():
            pl.semaphore_wait(credit.at[k + 2], 1)

        @pl.when(line_down)
        def _():
            pl.semaphore_wait(credit.at[k + 3], 1)

    give(0)
    for step, at in enumerate(order):
        weight_grad(1, at, slope[2 * at[0] + at[1]], slabs(sec, 0, 6))
        if step == 0:
            pl.semaphore_wait(credit.at[0], 1)
            sc1.core_send(1 - p.f)
            sc2.side_add(1)
            sc2.line(1, 0)
            sc2.line(1, 1)
        if step == 1:
            sc1.core_add(1 - p.l)
            pl.semaphore_wait(credit.at[1], 1)
            sc1.side_send()
        if step == 2:
            sc1.core_send(p.f)
    sc1.core_add(p.l)
    sc2.side_add(0)
    sc2.line(0, 0)
    sc2.line(0, 1)
    take_line(0)
    sc1.side_add(3)
    sc1.line(3, 0)
    sc1.line(3, 1)
    contract(slope, 1)
    df2_ref[...] = sc2.final()
    give(5)

    def second_back(i, rows):
        grad = temp[rows]
        normalized, inverse = norm_parts(res_ref[rows])
        total_grad = out_grad(i, rows) + norm_grad(grad, vec[3:4], normalized, inverse)
        res_ref[rows] = total_grad
        rounded = total_grad.astype(BF)
        grad2[rows] = rounded
        vec_grad[3:4] += jnp.sum(grad * normalized, 0, keepdims=True)
        vec_grad[4:5] += jnp.sum(grad, 0, keepdims=True)
        vec_grad[2:3] += jnp.sum(rounded.astype(F32), 0, keepdims=True)

    by_rows(second_back)
    sc1.side_add(2)
    sc1.line(2, 0)
    sc1.line(2, 1)
    attended = slabs(att, 0, 6)
    for j in range(3):
        lanes = slice(256 * j, 256 * j + 256)
        store_runs(G.at[0], out_runs(256 * j, 256 * j + 256), dot(grad2[:, lanes].T, attended).astype(BF))
    for j in range(3):
        lanes = slice(256 * j, 256 * j + 256)
        part = dot(grad2[...], load_runs(W.at[0], out_runs(0, D), lanes)).astype(BF)
        sec[2 * j] = part[:, :128]
        sec[2 * j + 1] = part[:, 128:]

    def attend_back(it, carry):
        i, pair = lax.div(it, 6), lax.rem(it, 6)
        rows, q, k, v = head_pair(i, pair)
        grad_out = sec[pair, rows]
        q, k = q * jnp.asarray(0.125, BF), k * jnp.asarray(0.125, BF)
        k_t = k.T
        bars = jnp.concatenate([jnp.where(mask_ref[rows] > 0, 0.0, -1e30)] * 2, 1)[:, :PAD]
        q_halves, out_halves, v_halves = halves(q), halves(grad_out), halves(v)
        plain_q = qkv[pair, rows]
        grad_v, grad_k, grad_q = 0.0, 0.0, []
        for h, k_h in enumerate(halves(k)):
            scores = dot_nt(k_h, plain_q) + bars
            probs = jnp.exp(scores - lse[it * 2 + h])
            grad_v = grad_v + dot(probs.astype(BF), out_halves[h])
            grad_probs = dot_nt(v_halves[h], grad_out)
            grad_scores = (probs * (grad_probs - jnp.sum(grad_probs * probs, 0, keepdims=True))).astype(BF)
            grad_k = grad_k + dot(grad_scores, q_halves[h])
            grad_q.append(dot(k_t[64 * h : 64 * h + 64], grad_scores))
        qkv[pair, rows] = jnp.concatenate(grad_q, 0).T.astype(BF)
        qkv[6 + pair, rows] = grad_k.astype(BF)
        qkv[12 + pair, rows] = grad_v.astype(BF)
        return carry

    lax.fori_loop(0, 6, attend_back, 0)
    sc1.side_add(1)
    sc1.line(1, 0)
    sc1.line(1, 1)
    lax.fori_loop(6, 14, attend_back, 0)
    sc1.side_add(0)
    sc1.line(0, 0)
    sc1.line(0, 1)
    lax.fori_loop(14, 18, attend_back, 0)
    for j in range(9):
        left = slabs(qkv, 2 * j, 2)
        store_runs(G.at[0], qkv_runs(256 * j, 256 * j + 256), dot(left.T, norm1[...]).astype(BF))
        if j < 3 or j >= 6:
            row, lanes = (6, slice(256 * j, 256 * j + 256)) if j < 3 else (7, slice(256 * (j - 6), 256 * (j - 6) + 256))
            vec_grad[row : row + 1, lanes] = jnp.sum(left.astype(F32), 0, keepdims=True)
    pl.semaphore_wait(credit.at[5], 1)
    sc0.core_send(1 - p.f)
    sc0.core_send(p.f)
    sc0.core_add(1 - p.l)
    pl.semaphore_wait(credit.at[6], 1)
    sc0.side_send()
    sc0.core_add(p.l)
    df1_ref[...] = sc1.final()
    take_line(5)
    sc0.side_add(3)
    sc0.line(3, 0)
    sc0.line(3, 1)

    def contract_joined(i, carry):
        rows = image_rows(i)
        for j in range(3):
            lanes = slice(256 * j, 256 * j + 256)
            left = jnp.concatenate([qkv[k, rows] for k in range(18)], 1)
            temp[rows, lanes] = dot(left, load_runs(W.at[0], qkv_runs(0, 3 * D), lanes))
        return carry

    lax.fori_loop(0, IMG, contract_joined, 0)
    sc0.side_add(2)
    sc0.line(2, 0)
    sc0.line(2, 1)

    def first_back(i, rows):
        grad = temp[rows]
        normalized, inverse = norm_parts(img_ref[rows].astype(F32))
        res_ref[rows] += norm_grad(grad, vec[0:1], normalized, inverse)
        vec_grad[0:1] += jnp.sum(grad * normalized, 0, keepdims=True)
        vec_grad[1:2] += jnp.sum(grad, 0, keepdims=True)

    by_rows(first_back)
    sc0.side_add(1)
    sc0.line(1, 0)
    sc0.line(1, 1)

    @pl.when(p.index >= 0)
    def _():
      outgoing = jnp.zeros((GROUPS * 8, 128), F32)
      for k in range(3):
          rows_k = jnp.zeros((GROUPS, 128), F32)
          for row, (kk, offset, width, base) in enumerate(table):
              if kk == k:
                  mask, places = spread(k, offset, width, base)
                  rows_k = rows_k + dot_exact(mask * vec_grad[row : row + 1], places, ((1,), (1,)))
          at = jnp.where(iota((GROUPS * 8, GROUPS), 0) == 8 * iota((GROUPS * 8, GROUPS), 1) + k, 1.0, 0.0)
          outgoing = outgoing + dot_exact(at, rows_k, ((1,), (0,)))
      vec_out[...] = outgoing.reshape(2, 16, 8, 128)
    vec_swap = remote(vec_out.at[1 - p.c], vec_core, 3, p.sib)
    vec_swap.start()
    vec_swap.wait_recv()
    vec_out[p.c] += vec_core[...]
    mine = (p.l * 4 + p.z) * 2 + p.f

    def push_vec(i, carry):
        q = lax.rem(mine + i, 16)
        dev = p.block(lax.div(q, 8), lax.rem(lax.div(q, 2), 4), lax.rem(q, 2))
        remote(vec_out.at[p.c, q], vec_in.at[mine], 4, dev).start()
        return carry

    lax.fori_loop(1, 16, push_vec, 0)
    vec_in[mine] = vec_out[p.c, mine]
    sc0.side_add(0)
    sc0.line(0, 0)
    sc0.line(0, 1)
    own_qo = sc0.final()
    dqo_ref[p.c] = own_qo
    qo_back = remote(dqo_ref.at[p.c], swap_grad, 5, p.sib)
    qo_back.start()
    most = remote(vec_out.at[p.c, pl.ds(0, 15)], vec_in.at[pl.ds(0, 15)], 4, p.sib)
    most.wait_recv()
    dvec_ref[...] = jnp.sum(vec_in[...], 0)
    qo_back.wait_recv()
    dqo_ref[1 - p.c] = swap_grad[...]

    swap_copy.wait_send()
    all_but_own.wait_send()
    share.wait_send()
    vec_swap.wait_send()
    most.wait_send()
    qo_back.wait_send()
    for g in (sm_g, qo_g, f1_g):
        g.drain()
    for s in (sc0, sc1, sc2):
        s.drain()


def swap(block, step, size):
    return lax.ppermute(block, "fsdp", [(i, i ^ step) for i in range(size)])


def pregather(block, F, r):
    step = 1
    while step < r:
        high = (lax.axis_index("fsdp") // step) % 2 == 1
        other = swap(block, step, F)
        block = jnp.concatenate([jnp.where(high, other, block), jnp.where(high, block, other)], 0)
        step *= 2
    return block


def postscatter(block, F, r):
    step = r // 2
    while step:
        high = (lax.axis_index("fsdp") // step) % 2 == 1
        middle = block.shape[0] // 2
        keep = jnp.where(high, block[middle:], block[:middle])
        send = jnp.where(high, block[:middle], block[middle:])
        block = keep + swap(send, step, F)
        step //= 2
    return block


def per_device(
    F,
    r,
    n,
    images,
    tissue,
    pair_index,
    text_embed,
    logit_scale,
    ln1_gain,
    ln1_bias,
    w_qkv,
    bias_qv,
    w_out,
    bias_out,
    ln2_gain,
    ln2_bias,
    w_fc1,
    bias_fc1,
    w_fc2,
    bias_fc2,
    cotangent,
):
    slots = images.shape[1]
    core = (lax.axis_index("fsdp") // r) % 2
    gather = lambda block: pregather(block, F, r)
    joined = gather(jnp.concatenate([w_qkv.T, w_out.T], 0).reshape(1, -1, D))
    rows_here = w_qkv.shape[1]
    q_t = joined[:, :rows_here].reshape(-1, D)
    o_t = joined[:, rows_here:].reshape(-1, D)

    def zeros(count):
        return jnp.zeros((count, D), BF)

    gap = QKV_ROWS - OUT_ROWS
    as_zero = jnp.concatenate([q_t, zeros(ROWS - QKV_ROWS), zeros(gap), o_t, zeros(OUT_ROWS)], 0)
    as_one = jnp.concatenate([zeros(QKV_ROWS), q_t, zeros(OUT_ROWS), o_t], 0)
    qo = jnp.where(core == 0, as_zero, as_one).reshape(2, ROWS, D)
    f1 = gather(w_fc1.T)
    f2 = gather(w_fc2)

    text_float = text_embed.astype(F32)
    text_unit = (text_float * lax.rsqrt(jnp.sum(text_float * text_float, -1, keepdims=True) + EPS)).astype(BF)
    vectors = jnp.stack([ln1_gain, ln1_bias, bias_out, ln2_gain, ln2_bias, bias_fc2], 1)
    vectors = gather(vectors)
    qv, first = gather(bias_qv), gather(bias_fc1)
    lanes = lambda v: jnp.pad(v, (0, 128 - v.shape[0])).reshape(1, 128)
    row0 = lanes(vectors[:, :5].T.reshape(-1))
    row1 = lanes(jnp.concatenate([vectors[:, 5], qv]))
    row2 = lanes(first)
    text_all = gather(text_unit).reshape(-1, 6, 128).transpose(1, 0, 2).reshape(-1, 128)
    pair = gather(pair_index)
    pair_rows = jnp.pad(jnp.stack([pair // 256, pair % 256], 1), ((0, 0), (0, 126))).astype(BF)
    small = jnp.concatenate([row0, row1, row2, text_all, pair_rows], 0)
    small_rows = -(-small.shape[0] // 16) * 16
    small = jnp.pad(small, ((0, small_rows - small.shape[0]), (0, 0)))

    def padded(tokens):
        return jnp.pad(tokens, ((0, 0), (0, PAD - slots), (0, 0))).reshape(TOK, D)

    mask = jnp.pad(tissue.astype(F32), ((0, 0), (0, PAD - slots))).reshape(TOK, 1)
    mask = jnp.broadcast_to(mask, (TOK, 128))
    text_in = jnp.pad(text_float, ((0, 8 - IMG), (0, 0)))
    scale = jnp.broadcast_to(logit_scale.reshape(1, 1), (8, 128))
    vmem = pl.BlockSpec(memory_space=pltpu.VMEM)
    shape = jax.ShapeDtypeStruct
    mix, res, loss, text_grad, dqo, df1, df2, dvec = pl.pallas_call(
        functools.partial(layer_kernel, F, r, n),
        out_shape=(
            shape((TOK, D), BF),
            shape((TOK, D), F32),
            shape((8, 128), F32),
            shape((8, D), F32),
            shape((2, ROWS, D), F32),
            shape((ROWS, D), F32),
            shape((ROWS, D), F32),
            shape((8, 128), F32),
        ),
        in_specs=[vmem] * 9,
        out_specs=(vmem,) * 8,
        scratch_shapes=[
            pltpu.VMEM((3, 2, 2, 4, 2, ROWS, D), BF),
            pltpu.VMEM((3, 2, 2, 4, 2, ROWS, D), BF),
            pltpu.VMEM((4, 4, 2, ROWS, D), BF),
            pltpu.VMEM((2, 3, ROWS, D), BF),
            pltpu.VMEM((2, 2, 4, 2, small_rows, 128), BF),
            pltpu.VMEM((ROWS, D), F32),
            pltpu.VMEM((TOK, D), BF),
            pltpu.VMEM((18, TOK, 128), BF),
            pltpu.VMEM((6, TOK, 128), BF),
            pltpu.VMEM((2 * IMG * 6, 1, PAD), F32),
            pltpu.VMEM((6, TOK, 128), BF),
            pltpu.VMEM((4, TOK, D), BF),
            pltpu.VMEM((4, TOK, D), BF),
            pltpu.VMEM((TOK, D), BF),
            pltpu.VMEM((max(TOK, IMG * n), D), F32),
            pltpu.VMEM((16, D), F32),
            pltpu.VMEM((16, D), F32),
            pltpu.VMEM((16, D), F32),
            pltpu.VMEM((8, D), F32),
            pltpu.VMEM((IMG * n, 128), F32),
            pltpu.VMEM((2, n // 2, 32, 128), BF),
            pltpu.VMEM((2, 16, 8, 128), F32),
            pltpu.VMEM((16, 8, 128), F32),
            pltpu.VMEM((16, 8, 128), F32),
            pltpu.SemaphoreType.DMA((4, 32)),
            pltpu.SemaphoreType.DMA((4, 32)),
            pltpu.SemaphoreType.DMA((3, 32)),
            pltpu.SemaphoreType.DMA((3, 32)),
            pltpu.SemaphoreType.DMA((16,)),
            pltpu.SemaphoreType.REGULAR((10,)),
        ],
        compiler_params=pltpu.CompilerParams(collective_id=0, has_side_effects=True, vmem_limit_bytes=VMEM_LIMIT),
    )(qo, f1, f2, small, padded(images), padded(cotangent), mask, text_in, scale)

    def tokens(rows):
        return rows.reshape(IMG, PAD, D)[:, :slots]

    scatter = lambda block: postscatter(block, F, r)
    chip = dqo.reshape(2 * ROWS, D)
    dq = jnp.where(core == 0, chip[:QKV_ROWS], chip[QKV_ROWS : 2 * QKV_ROWS])
    do = jnp.where(core == 0, chip[2 * QKV_ROWS : 2 * QKV_ROWS + OUT_ROWS], chip[2 * QKV_ROWS + OUT_ROWS :])
    thin = [dvec[0, 24 * k : 24 * k + 24] for k in range(5)] + [dvec[1, :24]]
    thin = [scatter(v) for v in thin]
    return (
        tokens(mix),
        tokens(res),
        loss[0, 0],
        text_grad[:IMG],
        thin[0],
        thin[1],
        scatter(dq).T,
        scatter(dvec[1, 24:72]),
        scatter(do).T,
        thin[2],
        thin[3],
        thin[4],
        scatter(df1).T,
        scatter(dvec[2, :96]),
        scatter(df2),
        thin[5],
    )


def solution(mesh):
    F = mesh.shape["fsdp"]
    n = mesh.shape["dp"] * F
    r = n // GROUPS
    both = ("dp", "fsdp")
    rows, columns = P(both), P(None, both)
    in_specs = (
        rows, rows, rows, rows, P(), rows, rows, columns, rows, columns, rows, rows, rows, columns, rows, rows, rows, rows
    )
    out_specs = (
        rows, rows, P(), rows, rows, rows, columns, rows, columns, rows, rows, rows, columns, rows, rows, rows
    )
    return jax.shard_map(
        functools.partial(per_device, F, r, n), mesh=mesh, in_specs=in_specs, out_specs=out_specs, check_vma=False
    )
```

```python
import functools
import math

import jax
import jax.numpy as jnp
from jax import lax
from jax.experimental import pallas as pl
from jax.experimental.pallas import tpu as pltpu
from jax.sharding import PartitionSpec as P

MESH = pl.DeviceIdType.MESH
MIB = 1024 * 1024
GROUPS = 32
D = 768
HEADS = 12
PAD = 208
IMG = 3
TOK = IMG * PAD
QKV_ROWS, OUT_ROWS = 72, 24
ROWS = 96
VMEM_LIMIT = 63 * MIB
EPS = 1e-6
BF, F32 = jnp.bfloat16, jnp.float32


def dot(a, b):
    return lax.dot_general(a, b, (((1,), (0,)), ((), ())), preferred_element_type=F32)


def dot_nt(a, b):
    return lax.dot_general(a, b, (((1,), (1,)), ((), ())), preferred_element_type=F32)


def dot_exact(a, b, dims):
    return lax.dot_general(a, b, (dims, ((), ())), preferred_element_type=F32, precision=lax.Precision.HIGHEST)


def iota(shape, dim):
    return lax.broadcasted_iota(jnp.int32, shape, dim)


def split(numbers, by):
    quotient = jnp.floor((numbers.astype(F32) + 0.5) * (1.0 / by)).astype(jnp.int32)
    return quotient, numbers - quotient * by


class Pos:
    def __init__(p, F, r, n):
        p.F, p.r, p.n = F, r, n
        p.index = lax.axis_index("dp") * F + lax.axis_index("fsdp")
        p.g, p.rho = lax.div(p.index, r), lax.rem(p.index, r)
        p.c, p.z = lax.rem(p.g, 2), lax.rem(lax.div(p.g, 2), 4)
        p.x, p.y = lax.rem(lax.div(p.g, 8), 2), lax.div(p.g, 16)
        p.l = p.y + p.c * (p.x - p.y)
        p.f = p.x + p.c * (p.y - p.x)
        c, x, y, z = p.c, p.x, p.y, p.z
        p.sib = p.chip(y, x, z, 1 - c)
        p.fn = p.chip(y + c * (1 - 2 * y), x + (1 - c) * (1 - 2 * x), z, c)
        p.ln = p.chip(y + (1 - c) * (1 - 2 * y), x + c * (1 - 2 * x), z, c)
        p.up = p.chip(y, x, jnp.minimum(z + 1, 3), c)
        p.dn = p.chip(y, x, jnp.maximum(z - 1, 0), c)
        p.plane = lax.div(p.g, 2) * r + p.rho

    def device(p, linear):
        return (lax.div(linear, p.F), lax.rem(linear, p.F))

    def chip(p, y, x, z, c):
        return p.device((((y * 2 + x) * 4 + z) * 2 + c) * p.r + p.rho)

    def column(p, zz):
        return p.chip(p.y, p.x, zz, p.c)

    def at_distance(p, h, fn):
        if h == 0:
            fn(p.z)
            return

        @pl.when(p.z + h <= 3)
        def _():
            fn(p.z + h)

        @pl.when(p.z - h >= 0)
        def _():
            fn(p.z - h)

    def for_others(p, fn):
        for h in (1, 2, 3):
            p.at_distance(h, fn)

    def in_plane(p, q):
        return p.device((lax.div(q, p.r) * 2 + p.c) * p.r + lax.rem(q, p.r))

    def block(p, l, z, f):
        y, x = l + p.c * (f - l), f + p.c * (l - f)
        return p.chip(y, x, z, p.c)


def group_of(block):
    c = block // 16 if isinstance(block, int) else jnp.where(block >= 16, 1, 0)
    rest = block - c * 16
    if isinstance(block, int):
        l, z, f = rest // 8, rest // 2 % 4, rest % 2
    else:
        l = jnp.where(rest >= 8, 1, 0)
        zf = rest - 8 * l
        z = jnp.where(zf >= 2, 1, 0) + jnp.where(zf >= 4, 1, 0) + jnp.where(zf >= 6, 1, 0)
        f = zf - 2 * z
    y, x = l + c * (f - l), f + c * (l - f)
    return ((y * 2 + x) * 4 + z) * 2 + c


def enter(p):
    bar = pltpu.get_barrier_semaphore()
    for device in (p.sib, p.fn, p.ln):
        pl.semaphore_signal(bar, inc=1, device_id=device, device_id_type=MESH)
    p.for_others(lambda zz: pl.semaphore_signal(bar, inc=1, device_id=p.column(zz), device_id_type=MESH))
    pl.semaphore_wait(bar, 6)


class Gather:
    def __init__(s, p, held, send, recv, line_first=False):
        s.p, s.held, s.send, s.recv, s.line_first = p, held, send, recv, line_first

    def cp(s, at, ks, kr, dev):
        ref = s.held.at[at]
        return pltpu.make_async_remote_copy(
            src_ref=ref, dst_ref=ref, send_sem=s.send.at[ks], recv_sem=s.recv.at[kr], device_id=dev, device_id_type=MESH
        )

    def first(s):
        p = s.p
        return s.cp((p.c, p.l, p.z, p.f), 0, 0, p.fn)

    def first_in(s):
        p = s.p
        return s.cp((p.c, p.l, p.z, 1 - p.f), 0, 0, p.fn)

    def f_of(s, b):
        return s.p.f + b * (1 - 2 * s.p.f)

    def up(s, zz, b):
        return s.cp((s.p.c, s.p.l, zz, s.f_of(b)), 1 + 2 * zz + b, 1 + 2 * zz + b, s.p.up)

    def dn(s, zz, b):
        return s.cp((s.p.c, s.p.l, zz, s.f_of(b)), 9 + 2 * zz + b, 1 + 2 * zz + b, s.p.dn)

    def cross(s, zz):
        return s.cp((s.p.c, s.p.l, zz, s.p.f), 2 + 2 * zz, 2 + 2 * zz, s.p.fn)

    def cross_in(s, zz):
        return s.cp((s.p.c, s.p.l, zz, 1 - s.p.f), 2 + 2 * zz, 2 + 2 * zz, s.p.fn)

    def last(s, zz):
        return s.cp((s.p.c, s.p.l, zz), 17 + zz, 9 + zz, s.p.ln)

    def last_in(s, zz):
        return s.cp((s.p.c, 1 - s.p.l, zz), 17 + zz, 9 + zz, s.p.ln)

    def core(s, l, zz):
        return s.cp((s.p.c, l, zz), 21 + 4 * l + zz, 13 + 4 * l + zz, s.p.sib)

    def core_in(s, l, zz):
        return s.cp((1 - s.p.c, l, zz), 21 + 4 * l + zz, 13 + 4 * l + zz, s.p.sib)

    def own(s, b):
        p = s.p
        if b:
            s.first_in().wait_recv()
        else:
            s.first().start()
        if not (b and s.line_first):

            @pl.when(p.z < 3)
            def _():
                s.up(p.z, b).start()

            @pl.when(p.z > 0)
            def _():
                s.dn(p.z, b).start()

        if b:
            s.last(p.z).start()
            s.core(p.l, p.z).start()

    def line(s, h, b):
        p = s.p

        def one(zz, copy, onward):
            if b and s.line_first:
                s.cross_in(zz).wait_recv()
            else:
                copy(zz, b).wait_recv()

                @pl.when(onward)
                def _():
                    copy(zz, b).start()

                if s.line_first:
                    s.cross(zz).start()
            if b:
                s.last(zz).start()
                s.core(p.l, zz).start()

        @pl.when(p.z - h >= 0)
        def _():
            one(p.z - h, s.up, p.z < 3)

        @pl.when(p.z + h <= 3)
        def _():
            one(p.z + h, s.dn, p.z > 0)

    def arrive(s, h):
        p = s.p

        def one(zz):
            s.last_in(zz).wait_recv()
            s.core(1 - p.l, zz).start()

        if h == 0:
            one(p.z)
        else:

            @pl.when(p.z - h >= 0)
            def _():
                one(p.z - h)

            @pl.when(p.z + h <= 3)
            def _():
                one(p.z + h)

    def finish(s):
        for zz in range(4):
            for l in range(2):
                s.core_in(l, zz).wait_recv()

    def drain(s):
        p = s.p
        s.first().wait_send()
        for zz in range(4):

            @pl.when((p.z < 3) & (zz <= p.z))
            def _():
                s.up(zz, 0).wait_send()
                if not s.line_first:
                    s.up(zz, 1).wait_send()

            @pl.when((p.z > 0) & (zz >= p.z))
            def _():
                s.dn(zz, 0).wait_send()
                if not s.line_first:
                    s.dn(zz, 1).wait_send()

            if s.line_first:

                @pl.when(zz != p.z)
                def _():
                    s.cross(zz).wait_send()

            s.last(zz).wait_send()
            for l in range(2):
                s.core(l, zz).wait_send()


class Scatter:
    def __init__(s, p, sums, room, landing, send, recv, line_last=False):
        s.p, s.sums, s.room, s.landing, s.send, s.recv, s.line_last = p, sums, room, landing, send, recv, line_last

    def cp(s, src, dst, ks, kr, dev):
        return pltpu.make_async_remote_copy(
            src_ref=src, dst_ref=dst, send_sem=s.send.at[ks], recv_sem=s.recv.at[kr], device_id=dev, device_id_type=MESH
        )

    def core_cp(s, l):
        return s.cp(s.sums.at[1 - s.p.c, l], s.room(l), 1 + l, 1 + l, s.p.sib)

    def side_cp(s, zz):
        return s.cp(s.sums.at[s.p.c, 1 - s.p.l, zz], s.room(2).at[zz], 3 + zz, 3 + zz, s.p.ln)

    def f_of(s, b):
        return 1 - s.p.f if b == 0 else s.p.f

    def here(s, zz, b):
        return s.sums.at[s.p.c, s.p.l, zz, s.f_of(b)]

    def up_far(s, zz, b):
        return s.cp(s.here(zz, b), s.room(3).at[zz, b], 7 + 2 * zz + b, 7 + 2 * zz + b, s.p.up)

    def up_end(s, zz, b):
        return s.cp(s.here(zz, b), s.landing.at[b], 7 + 2 * zz + b, 15 + b, s.p.up)

    def down(s, zz, b):
        return s.cp(s.here(zz, b), s.room(3).at[zz, b], 15 + 2 * zz + b, 7 + 2 * zz + b, s.p.dn)

    def last_cp(s):
        return s.cp(s.here(s.p.z, 0), s.landing.at[2], 0, 0, s.p.fn)

    def cross_cp(s, zz):
        return s.cp(s.here(zz, 0), s.room(3).at[zz, 0], 23 + zz, 17 + zz, s.p.fn)

    def cross_send(s, h):
        s.by_distance(h, lambda zz: s.cross_cp(zz).start())

    def cross_add(s, h):
        def one(zz):
            s.cross_cp(zz).wait_recv()
            s.add(zz, 1, s.room(3).at[zz, 0])
            if h > 0:
                s.straight(zz).start()

        s.by_distance(h, one)

    def core_send(s, l):
        s.core_cp(l).start()

    def core_add(s, l):
        s.core_cp(l).wait_recv()
        room = s.room(l)

        def body(zz, carry):
            for f in range(2):
                ref = s.sums.at[s.p.c, l, zz, f]
                ref[...] = (ref[...].astype(F32) + room[zz, f].astype(F32)).astype(BF)
            return carry

        lax.fori_loop(0, 4, body, 0)

    def add(s, zz, b, ref):
        total = s.here(zz, b)
        total[...] = (total[...].astype(F32) + ref[...].astype(F32)).astype(BF)

    def by_distance(s, h, fn):
        s.p.at_distance(h, fn)

    def side_send(s):
        for h in (3, 2, 1, 0):
            s.by_distance(h, lambda zz: s.side_cp(zz).start())

    def side_add(s, h):
        def one(zz):
            s.side_cp(zz).wait_recv()
            for f in (0, 1):
                total = s.sums.at[s.p.c, s.p.l, zz, f]
                total[...] = (total[...].astype(F32) + s.room(2)[zz, f].astype(F32)).astype(BF)

        s.by_distance(h, one)

    def ends(s, h):
        p = s.p

        @pl.when(p.z == 0)
        def _():
            for b in (0, 1):
                (s.up_end if h == 1 else s.up_far)(p.z + h, b).start()

        @pl.when(p.z == 3)
        def _():
            for b in (0, 1):
                s.down(p.z - h, b).start()

    def inner(s, h, upward):
        p = s.p
        if upward:

            @pl.when((p.z == 1) | (p.z == 2) if h == 1 else p.z == 1)
            def _():
                zz = p.z + h
                for b in (0, 1):
                    s.up_far(zz, b).wait_recv()
                    s.add(zz, b, s.room(3).at[zz, b])
                    (s.up_end if h == 1 else s.up_far)(zz, b).start()

        else:

            @pl.when((p.z == 1) | (p.z == 2) if h == 1 else p.z == 2)
            def _():
                zz = p.z - h
                for b in (0, 1):
                    s.down(zz, b).wait_recv()
                    s.add(zz, b, s.room(3).at[zz, b])
                    s.down(zz, b).start()

    def come(s):
        p = s.p
        for b in (0, 1):

            @pl.when(p.z > 0)
            def _():
                s.up_end(p.z, b).wait_recv()
                s.add(p.z, b, s.landing.at[b])

            @pl.when(p.z < 3)
            def _():
                s.down(p.z, b).wait_recv()
                s.add(p.z, b, s.room(3).at[p.z, b])

            if b == 0:
                s.last_cp().start()

    def straight(s, zz):
        return s.cp(s.here(zz, 1), s.room(3).at[s.p.z, 1], 7 + zz, 7 + s.p.z, s.p.column(zz))

    def straight_in(s, zz):
        return s.cp(s.here(zz, 1), s.room(3).at[zz, 1], 7 + zz, 7 + zz, s.p.column(zz))

    def final(s):
        p = s.p
        if s.line_last:

            def one(zz):
                s.straight_in(zz).wait_recv()
                s.add(p.z, 1, s.room(3).at[zz, 1])

            p.for_others(one)
            return s.here(p.z, 1)[...].astype(F32)
        s.last_cp().wait_recv()
        return s.here(p.z, 1)[...].astype(F32) + s.landing[2].astype(F32)

    def drain(s):
        p = s.p
        for l in range(2):
            s.core_cp(l).wait_send()
        for zz in range(4):
            s.side_cp(zz).wait_send()
            if s.line_last:
                s.cross_cp(zz).wait_send()

                @pl.when(zz != p.z)
                def _():
                    s.straight(zz).wait_send()

            else:

                @pl.when(zz > p.z)
                def _():
                    s.up_far(zz, 0).wait_send()
                    s.up_far(zz, 1).wait_send()

                @pl.when(zz < p.z)
                def _():
                    s.down(zz, 0).wait_send()
                    s.down(zz, 1).wait_send()

        if not s.line_last:
            s.last_cp().wait_send()


def qkv_runs(start, stop):
    runs, row = [], start
    while row < stop:
        chip, inside = divmod(row, 2 * QKV_ROWS)
        z, x, y = chip % 4, chip // 4 % 2, chip // 8
        first = inside < ROWS
        until = min(stop, chip * 2 * QKV_ROWS + (ROWS if first else 2 * QKV_ROWS))
        low = inside if first else inside - ROWS
        at = (0, y, z, x) if first else (1, x, z, y)
        runs.append((at, low, low + until - row))
        row = until
    return runs


def out_runs(start, stop):
    runs, row = [], start
    while row < stop:
        chip, inside = divmod(row, 2 * OUT_ROWS)
        z, x, y = chip % 4, chip // 4 % 2, chip // 8
        until = min(stop, (chip + 1) * 2 * OUT_ROWS)
        low = inside + 2 * (QKV_ROWS - OUT_ROWS) // 2
        runs.append(((1, x, z, y), low, low + until - row))
        row = until
    return runs


def load_runs(ref, runs, lanes=slice(None)):
    return jnp.concatenate([ref[at + (slice(a, b), lanes)] for at, a, b in runs], 0)


def store_runs(ref, runs, value):
    row = 0
    for at, a, b in runs:
        ref[at + (slice(a, b), slice(None))] = value[row : row + b - a]
        row += b - a


def slabs(ref, first, count):
    return jnp.concatenate([ref[first + k] for k in range(count)], 1)


def norm_parts(values):
    centered = values - jnp.mean(values, -1, keepdims=True)
    inverse = lax.rsqrt(jnp.mean(centered * centered, -1, keepdims=True) + EPS)
    return centered * inverse, inverse


def norm_grad(grad, gain, normalized, inverse):
    h = grad * gain
    return (h - jnp.mean(h, -1, keepdims=True) - normalized * jnp.mean(h * normalized, -1, keepdims=True)) * inverse


def gelu_parts(x):
    z = jnp.abs(x) * math.sqrt(0.5)
    under = 1.0 + 0.3275911 * z
    t = pl.reciprocal(under, approx=True)
    t = t * (2.0 - under * t)
    bell = jnp.exp(-0.5 * x * x)
    poly = ((((1.061405429 * t - 1.453152027) * t + 1.421413741) * t - 0.284496736) * t + 0.254829592) * t
    tail = 0.5 * poly * bell
    cdf = jnp.where(x >= 0, 1.0 - tail, tail)
    return x * cdf, cdf + x * bell * (1.0 / math.sqrt(2.0 * math.pi))


CUTS = ((0, 48), (48, 48), (96, 48), (144, 64))


def by_rows(fn):
    def body(i, carry):
        for start, size in CUTS:
            fn(i, pl.ds(pl.multiple_of(i * PAD + start, 16), size))
        return carry

    lax.fori_loop(0, IMG, body, 0)


def layer_kernel(
    F,
    r,
    n,
    qo_ref,
    f1_ref,
    f2_ref,
    small_ref,
    img_ref,
    cot_ref,
    mask_ref,
    text_ref,
    scale_ref,
    mix_ref,
    res_ref,
    loss_ref,
    tg_ref,
    dqo_ref,
    df1_ref,
    df2_ref,
    dvec_ref,
    W,
    G,
    room,
    ends,
    small,
    swap_grad,
    norm1,
    qkv,
    att,
    lse,
    sec,
    act,
    slope,
    grad2,
    temp,
    vec,
    vec_grad,
    pooled,
    row_grad,
    pair_rows,
    units,
    vec_out,
    vec_core,
    vec_in,
    g_send,
    g_recv,
    s_send,
    s_recv,
    misc,
    credit,
):
    p = Pos(F, r, n)
    half = n // 2
    total = IMG * n
    per_group = IMG * r
    small_rows = small.shape[4]
    qo_g, f1_g, f2_g = (Gather(p, W.at[m], g_send.at[m], g_recv.at[m], m == 0) for m in range(3))
    sm_g = Gather(p, small, g_send.at[3], g_recv.at[3], True)

    def remote(src, dst, k, dev):
        return pltpu.make_async_remote_copy(
            src_ref=src, dst_ref=dst, send_sem=misc.at[2 * k], recv_sem=misc.at[2 * k + 1], device_id=dev, device_id_type=MESH
        )

    W[1, p.c, p.l, p.z, p.f] = f1_ref[...]
    W[2, p.c, p.l, p.z, p.f] = f2_ref[...]
    small[p.c, p.l, p.z, p.f] = small_ref[...]
    vec_grad[...] = jnp.zeros(vec_grad.shape, F32)
    enter(p)
    swap_copy = remote(qo_ref.at[1 - p.c], G.at[0, 0, 0, 0, 0], 0, p.sib)
    swap_copy.start()
    sm_g.own(0)
    swap_copy.wait_recv()
    W[0, p.c, p.l, p.z, p.f] = (qo_ref[p.c].astype(F32) + G[0, 0, 0, 0, 0].astype(F32)).astype(BF)
    qo_g.own(0)
    f1_g.own(0)
    sm_g.own(1)
    qo_g.own(1)
    for h in (1, 2, 3):
        sm_g.line(h, 0)
        qo_g.line(h, 0)
        sm_g.line(h, 1)
        qo_g.line(h, 1)
        sm_g.arrive(h - 1)
        if h == 1:
            f1_g.own(1)
        if h == 2:
            f1_g.line(1, 0)
        if h == 3:
            f1_g.line(1, 1)
            sm_g.arrive(3)
        qo_g.arrive(h - 1)
    sm_g.finish()


    def picked(k):
        source, target = iota((GROUPS, GROUPS * small_rows), 1), iota((GROUPS, GROUPS * small_rows), 0)
        return dot(jnp.where(source == target * small_rows + k, 1.0, 0.0).astype(BF), small[...].reshape(GROUPS * small_rows, 128)).astype(BF)

    table = [(0, 0, 24, 0), (0, 24, 24, 0), (0, 48, 24, 0), (0, 72, 24, 0), (0, 96, 24, 0), (1, 0, 24, 0), (1, 24, 48, 0), (1, 24, 48, D)]
    table += [(2, 0, 96, D * q) for q in range(4)]

    def spread(k, offset, width, base):
        owner, inside = split(iota((1, D), 1) + base, width)
        names = iota((GROUPS, 1), 0)
        names = names if k == 2 else group_of(names)
        mask = jnp.where(names == owner, 1.0, 0.0)
        places = jnp.where(iota((128, D), 0) == inside + offset, 1.0, 0.0)
        return mask, places

    @pl.when(p.index >= 0)
    def _():
      message_rows = [picked(k) for k in range(3)]
      for row, (k, offset, width, base) in enumerate(table):
        mask, places = spread(k, offset, width, base)
        vec[row : row + 1, :] = jnp.sum(mask * dot(message_rows[k], places.astype(BF)), 0, keepdims=True)

    def first_norm(i, rows):
        normalized, _ = norm_parts(img_ref[rows].astype(F32))
        norm1[rows] = (normalized * vec[0:1] + vec[1:2]).astype(BF)

    by_rows(first_norm)
    f1_g.arrive(0)
    f1_g.line(2, 0)
    f2_g.own(0)
    qo_g.arrive(3)
    qo_g.finish()

    for j in range(9):
        part = dot_nt(norm1[...], load_runs(W.at[0], qkv_runs(256 * j, 256 * j + 256)))
        if j < 3:
            part = part + vec[6:7, 256 * j : 256 * j + 256]
        elif j >= 6:
            part = part + vec[7:8, 256 * (j - 6) : 256 * (j - 6) + 256]
        part = part.astype(BF)
        qkv[2 * j] = part[:, :128]
        qkv[2 * j + 1] = part[:, 128:]
        if j == 4:
            f1_g.line(2, 1)
            f1_g.arrive(1)
            f2_g.own(1)

    def image_rows(i):
        return pl.ds(pl.multiple_of(i * PAD, 16), PAD)

    low = iota((1, 128), 1) < 64

    def halves(value):
        zero = jnp.zeros_like(value)
        return jnp.where(low, value, zero), jnp.where(low, zero, value)

    def head_pair(i, pair):
        rows = pl.ds(pl.multiple_of(i * PAD, 16), PAD)
        return rows, qkv[pair, rows], qkv[6 + pair, rows], qkv[12 + pair, rows]

    PAIRS = 2

    def attend(it, carry):
        i, first = lax.div(it, 6 // PAIRS), lax.rem(it, 6 // PAIRS) * PAIRS
        bars = jnp.concatenate([jnp.where(mask_ref[image_rows(i)] > 0, 0.0, -1e30)] * 2, 1)[:, :PAD]
        results = []
        for step in range(PAIRS):
            rows, q, k, v = head_pair(i, first + step)
            v_t = v.T
            parts = []
            for h, k_h in enumerate(halves(k * jnp.asarray(0.125, BF))):
                scores = dot_nt(k_h, q) + bars
                top = jnp.max(scores, 0, keepdims=True)
                terms = jnp.exp(scores - top)
                amount = jnp.sum(terms, 0, keepdims=True)
                lse[(i * 6 + first + step) * 2 + h] = top + jnp.log(amount)
                parts.append(dot(v_t[64 * h : 64 * h + 64], terms.astype(BF)) * (1.0 / amount))
            results.append(jnp.concatenate(parts, 0).T.astype(BF))
        for step in range(PAIRS):
            att[first + step, rows] = results[step]
        return carry

    lax.fori_loop(0, 3, attend, 0)
    f1_g.line(3, 0)
    f2_g.line(1, 0)
    f1_g.line(3, 1)
    f1_g.arrive(2)
    lax.fori_loop(3, 5, attend, 0)
    f2_g.line(1, 1)
    f1_g.arrive(3)
    f2_g.arrive(0)
    lax.fori_loop(5, 7, attend, 0)
    f2_g.line(2, 0)
    f2_g.line(2, 1)
    f2_g.arrive(1)
    lax.fori_loop(7, 9, attend, 0)

    attended = slabs(att, 0, 6)
    for j in range(3):
        lanes = slice(256 * j, 256 * j + 256)
        part = dot_nt(attended, load_runs(W.at[0], out_runs(256 * j, 256 * j + 256)))
        res_ref[:, lanes] = img_ref[:, lanes].astype(F32) + part + vec[2:3, lanes]

    def second_norm(i, rows):
        normalized, _ = norm_parts(res_ref[rows])
        value = (normalized * vec[3:4] + vec[4:5]).astype(BF)
        for k in range(6):
            sec[k, rows] = value[:, 128 * k : 128 * k + 128]

    by_rows(second_norm)
    f1_g.finish()

    def expand(it, carry):
        q, rows = lax.div(it, IMG), image_rows(lax.rem(it, IMG))
        left = jnp.concatenate([sec[k, rows] for k in range(6)], 1)
        pre = dot_nt(left, W[1, lax.div(q, 2), lax.rem(q, 2)].reshape(D, D)) + vec[pl.ds(8 + q, 1), :]
        value, derivative = gelu_parts(pre)
        act[q, rows] = value.astype(BF)
        slope[q, rows] = derivative.astype(BF)
        return carry

    lax.fori_loop(0, 3, expand, 0)
    f2_g.line(3, 0)
    f2_g.line(3, 1)
    f2_g.arrive(2)
    lax.fori_loop(3, 9, expand, 0)
    f2_g.arrive(3)
    lax.fori_loop(9, 12, expand, 0)
    f2_g.finish()

    def contract(hidden_units, m):
        def body(i, carry):
            rows = image_rows(i)
            for j in range(3):
                lanes = slice(256 * j, 256 * j + 256)
                left = jnp.concatenate([hidden_units[q, rows] for q in range(4)], 1)
                temp[rows, lanes] = dot(left, W[m, :, :, :, :, :, lanes].reshape(4 * D, 256))
            return carry

        lax.fori_loop(0, IMG, body, 0)

    contract(act, 2)

    def wide(column):
        return jnp.concatenate([column] * 6, 1)

    pooled[...] = jnp.zeros(pooled.shape, F32)
    for i in range(IMG):
        sums, count = jnp.zeros((1, D), F32), jnp.zeros((1, 128), F32)
        for start, size in CUTS:
            rows = pl.ds(i * PAD + start, size)
            mask = mask_ref[rows]
            outputs = (res_ref[rows] + temp[rows] + vec[5:6]) * wide(mask)
            mix_ref[rows] = outputs.astype(BF)
            sums = sums + jnp.sum(outputs, 0, keepdims=True)
            count = count + jnp.sum(mask, 0, keepdims=True)
        pooled[i : i + 1, :] = sums / wide(count)
        pooled[8 + i : 9 + i, :] = wide(count)

    def unit(values):
        inverse = lax.rsqrt(jnp.sum(values * values, -1, keepdims=True) + EPS)
        return values * inverse, inverse

    def unit_grad(grad, values, inverse):
        return inverse * grad - inverse * inverse * inverse * values * jnp.sum(values * grad, -1, keepdims=True)

    own_pooled = pooled[0:8]
    image_unit, image_inverse = unit(own_pooled)
    image_unit = image_unit.astype(BF)
    message = jnp.zeros((32, 128), F32)
    for k in range(6):
        at = jnp.where((iota((32, 8), 0) == iota((32, 8), 1) + IMG * k) & (iota((32, 8), 1) < IMG), 1.0, 0.0).astype(BF)
        message = message + dot(at, image_unit[:, 128 * k : 128 * k + 128])
    units[p.c, p.plane] = message.astype(BF)

    def push(i, carry):
        q = lax.rem(p.plane + i, half)
        remote(units.at[p.c, p.plane], units.at[p.c, p.plane], 1, p.in_plane(q)).start()
        return carry

    lax.fori_loop(1, half, push, 0)
    all_but_own = remote(units.at[p.c, pl.ds(0, half - 1)], units.at[p.c, pl.ds(0, half - 1)], 1, p.sib)

    def gathered(source_chunks, chunk_rows, row_of, tiles, base):
        results = []
        for k in range(tiles):
            value = jnp.zeros((total, 128), F32)
            for number, chunk in source_chunks:
                owner, inside = split(iota((1, chunk_rows), 1), base)
                target = row_of(owner, inside, number, k)
                value = value + dot(jnp.where(iota((total, chunk_rows), 0) == target, 1.0, 0.0).astype(BF), chunk)
            results.append(value)
        return results

    def text_row(owner, inside, number, k):
        at = inside - 3 - per_group * k
        group = group_of(owner + 8 * number)
        return jnp.where((at >= 0) & (at < per_group), group * per_group + at, -1)

    chunks = [(2 * c + l, small[c, l].reshape(8 * small_rows, 128)) for c in range(2) for l in range(2)]
    tiles = gathered(chunks, 8 * small_rows, text_row, 7, small_rows)
    for b in range(r):
        for k in range(6):
            G[1, b // 16, b // 8 % 2, b // 2 % 4, b % 2, :, 128 * k : 128 * k + 128] = tiles[k][ROWS * b : ROWS * b + ROWS].astype(BF)

    def texts():
        return jnp.concatenate([G[1, b // 16, b // 8 % 2, b // 2 % 4, b % 2] for b in range(r)], 0)

    pair_rows[...] = tiles[6]

    all_but_own.wait_recv()
    share = remote(units.at[p.c], units.at[p.c], 2, p.sib)
    share.start()
    remote(units.at[1 - p.c], units.at[1 - p.c], 2, p.sib).wait_recv()

    for k in range(6):

        def add_chunk(number, value, k=k):
            c, at = lax.div(number * 16, half), lax.rem(number * 16, half)
            owner, inside = split(iota((1, 512), 1), 32)
            q = owner + at
            t = inside - IMG * k
            if r == 1:
                linear = 2 * q + c
            else:
                chip, rho = split(q, r)
                linear = (2 * chip + c) * r + rho
            target = jnp.where((t >= 0) & (t < IMG), linear * IMG + t, -1)
            pick = jnp.where(iota((total, 512), 0) == target, 1.0, 0.0).astype(BF)
            return value + dot(pick, units[c, pl.ds(at, 16)].reshape(512, 128))

        value = lax.fori_loop(0, n // 16, add_chunk, jnp.zeros((total, 128), F32)).astype(BF)
        for b in range(r):
            G[2, b // 16, b // 8 % 2, b // 2 % 4, b % 2, :, 128 * k : 128 * k + 128] = value[ROWS * b : ROWS * b + ROWS]

    def block(m, b):
        return G[m, lax.div(b, 16), lax.rem(lax.div(b, 8), 2), lax.rem(lax.div(b, 2), 4), lax.rem(b, 2)]

    scale = scale_ref[0:1, 0:1]
    row = jnp.zeros((1, total), F32)

    def similar(b, col_top):
        rows = pl.ds(pl.multiple_of(b * ROWS, ROWS), ROWS)
        part = dot_nt(block(2, b), texts()) * scale
        temp[rows, :total] = part
        return jnp.maximum(col_top, jnp.max(part, 0, keepdims=True))

    col_top = lax.fori_loop(0, r, similar, row - jnp.inf)

    def by_blocks(fn):
        def body(b, carry):
            rows = pl.ds(pl.multiple_of(b * ROWS, ROWS), ROWS)
            part = temp[rows, :total]
            top = jnp.max(part, 1, keepdims=True)
            row_lse = top + jnp.log(jnp.sum(jnp.exp(part - top), 1, keepdims=True))
            match = jnp.where(iota((ROWS, total), 1) == pair_of(rows), 1.0, 0.0)
            return fn(b, part, row_lse, match, carry)

        return body

    def pair_of(rows):
        column = pair_rows[rows]
        return (column[:, 0:1] * 256.0 + column[:, 1:2]).astype(jnp.int32)

    def sums(b, part, row_lse, match, carry):
        col_sum, loss = carry
        paired = jnp.sum(jnp.sum(part * match, 1, keepdims=True), 0, keepdims=True)
        return col_sum + jnp.sum(jnp.exp(part - col_top), 0, keepdims=True), loss + jnp.sum(row_lse, 0, keepdims=True) - 2.0 * paired

    col_sum, loss = lax.fori_loop(0, r, by_blocks(sums), (row, jnp.zeros((1, 1), F32)))
    col_lse = col_top + jnp.log(col_sum)
    loss = (loss + jnp.sum(col_lse, 1, keepdims=True)) / (2.0 * total)
    loss_ref[...] = jnp.broadcast_to(loss, (8, 128))

    def own_of(places):
        return jnp.where((places == iota(places.shape, 0) + IMG * p.index) & (iota(places.shape, 0) < IMG), 1.0, 0.0).astype(BF)

    own = own_of(iota((8, total), 1))

    def similar_grad(b, part, row_lse, match, carry):
        grad_rows, grad_text = carry
        grad = 0.5 * (jnp.exp(part - row_lse) + jnp.exp(part - col_lse)) - match
        grad = (scale * grad).astype(BF)
        own_rows = own_of(iota((8, ROWS), 1) + b * ROWS)
        return grad_rows + dot(own_rows, grad), grad_text + dot(dot_nt(own, grad).astype(BF), block(2, b))

    grad_rows, grad_text = lax.fori_loop(0, r, by_blocks(similar_grad), (jnp.zeros((8, total), F32), jnp.zeros((8, D), F32)))
    grad_unit = dot(grad_rows.astype(BF), texts())
    row_grad[...] = unit_grad(grad_unit, own_pooled, image_inverse) / jnp.maximum(pooled[8:16], 1.0)
    text_rows = text_ref[...]
    _, text_inverse = unit(text_rows)
    tg_ref[...] = unit_grad(grad_text, text_rows, text_inverse)

    sc0, sc1, sc2 = (
        Scatter(p, G.at[m], area, ends.at[1 if m == 1 else 0], s_send.at[m], s_recv.at[m], m == 0)
        for m, area in (
            (0, lambda k: room.at[k]),
            (1, lambda k: W.at[2, k // 2, k % 2] if isinstance(k, int) else W.at[2, 0, k]),
            (2, lambda k: room.at[k]),
        )
    )

    def out_grad(i, rows):
        return wide(mask_ref[rows]) * (cot_ref[rows].astype(F32) + row_grad[pl.ds(i, 1), :])

    def first_round(i, rows):
        value = out_grad(i, rows).astype(BF)
        grad2[rows] = value
        vec_grad[5:6] += jnp.sum(value.astype(F32), 0, keepdims=True)

    by_rows(first_round)
    order = ((1 - p.c, 1 - p.f), (p.c, 1 - p.l), (1 - p.c, p.f), (p.c, p.l))

    def weight_grad(m, at, left, right):
        left = left.T
        for j in range(3):
            lanes = slice(256 * j, 256 * j + 256)
            G[(m,) + at + (slice(None), slice(None), slice(None), lanes)] = (
                dot(left, right[:, lanes]).astype(BF).reshape(4, 2, ROWS, 256)
            )

    for step, at in enumerate(order):
        weight_grad(2, at, act[2 * at[0] + at[1]], grad2[...])
        if step == 0:
            sc2.core_send(1 - p.f)
        if step == 2:
            sc2.core_send(p.f)
    for q in range(4):
        for part in range(2):
            lanes = slice(384 * part, 384 * part + 384)
            value = dot_nt(grad2[...], W[2, q // 2, q % 2, 2 * part : 2 * part + 2].reshape(384, D)) * slope[q, :, lanes].astype(F32)
            value = value.astype(BF)
            slope[q, :, lanes] = value
            vec_grad[8 + q : 9 + q, lanes] = jnp.sum(value.astype(F32), 0, keepdims=True)
        if q == 0:
            sc2.core_add(1 - p.l)
            sc2.side_send()
        if q == 1:
            sc2.core_add(p.l)
    sc2.side_add(3)
    sc2.ends(3)
    f2_g.drain()

    def give(k):
        for at, device in ((0, p.sib), (1, p.ln), (2, p.fn)):
            pl.semaphore_signal(credit.at[k, at], inc=1, device_id=device, device_id_type=MESH)
        p.for_others(lambda zz: pl.semaphore_signal(credit.at[k, 3 + p.z], inc=1, device_id=p.column(zz), device_id_type=MESH))

    def take(k, *which):
        for at in which:
            pl.semaphore_wait(credit.at[k, at], 1)

    def take_column(k):
        p.for_others(lambda zz: pl.semaphore_wait(credit.at[k, 3 + zz], 1))

    give(0)
    for step, at in enumerate(order):
        weight_grad(1, at, slope[2 * at[0] + at[1]], slabs(sec, 0, 6))
        if step == 0:
            take(0, 0)
            sc1.core_send(1 - p.f)
        if step == 2:
            sc1.core_send(p.f)
            sc2.side_add(2)
            sc2.ends(2)
    contract(slope, 1)
    sc1.core_add(1 - p.l)
    take(0, 1)
    sc1.side_send()
    sc1.core_add(p.l)
    sc2.side_add(1)
    sc2.ends(1)
    sc2.side_add(0)

    def second_back(i, rows):
        grad = temp[rows]
        normalized, inverse = norm_parts(res_ref[rows])
        total_grad = out_grad(i, rows) + norm_grad(grad, vec[3:4], normalized, inverse)
        res_ref[rows] = total_grad
        rounded = total_grad.astype(BF)
        grad2[rows] = rounded
        vec_grad[3:4] += jnp.sum(grad * normalized, 0, keepdims=True)
        vec_grad[4:5] += jnp.sum(grad, 0, keepdims=True)
        vec_grad[2:3] += jnp.sum(rounded.astype(F32), 0, keepdims=True)

    by_rows(second_back)
    sc2.inner(2, True)
    sc2.inner(2, False)
    attended = slabs(att, 0, 6)
    for j in range(3):
        lanes = slice(256 * j, 256 * j + 256)
        store_runs(G.at[0], out_runs(256 * j, 256 * j + 256), dot(grad2[:, lanes].T, attended).astype(BF))
    for j in range(3):
        lanes = slice(256 * j, 256 * j + 256)
        part = dot(grad2[...], load_runs(W.at[0], out_runs(0, D), lanes)).astype(BF)
        sec[2 * j] = part[:, :128]
        sec[2 * j + 1] = part[:, 128:]

    def attend_back(it, carry):
        i, first = lax.div(it, 6 // PAIRS), lax.rem(it, 6 // PAIRS) * PAIRS
        bars = jnp.concatenate([jnp.where(mask_ref[image_rows(i)] > 0, 0.0, -1e30)] * 2, 1)[:, :PAD]
        results = []
        for step in range(PAIRS):
            rows, plain_q, k, v = head_pair(i, first + step)
            grad_out = sec[first + step, rows]
            q, k = plain_q * jnp.asarray(0.125, BF), k * jnp.asarray(0.125, BF)
            k_t = k.T
            q_halves, out_halves, v_halves = halves(q), halves(grad_out), halves(v)
            grad_v, grad_k, grad_q = 0.0, 0.0, []
            for h, k_h in enumerate(halves(k)):
                scores = dot_nt(k_h, plain_q) + bars
                probs = jnp.exp(scores - lse[(i * 6 + first + step) * 2 + h])
                grad_v = grad_v + dot(probs.astype(BF), out_halves[h])
                grad_probs = dot_nt(v_halves[h], grad_out)
                grad_scores = (probs * (grad_probs - jnp.sum(grad_probs * probs, 0, keepdims=True))).astype(BF)
                grad_k = grad_k + dot(grad_scores, q_halves[h])
                grad_q.append(dot(k_t[64 * h : 64 * h + 64], grad_scores))
            results.append((jnp.concatenate(grad_q, 0).T.astype(BF), grad_k.astype(BF), grad_v.astype(BF)))
        for step in range(PAIRS):
            for which in range(3):
                qkv[6 * which + first + step, rows] = results[step][which]
        return carry

    take(0, 2)
    take_column(0)
    lax.fori_loop(0, 2, attend_back, 0)
    sc1.side_add(3)
    sc1.ends(3)
    lax.fori_loop(2, 4, attend_back, 0)
    sc2.inner(1, True)
    sc2.inner(1, False)
    sc1.side_add(2)
    sc1.ends(2)
    lax.fori_loop(4, 6, attend_back, 0)
    sc1.side_add(1)
    sc1.ends(1)
    sc1.side_add(0)
    lax.fori_loop(6, 9, attend_back, 0)
    sc2.come()
    for j in range(9):
        left = slabs(qkv, 2 * j, 2)
        store_runs(G.at[0], qkv_runs(256 * j, 256 * j + 256), dot(left.T, norm1[...]).astype(BF))
        if j < 3 or j >= 6:
            row, lanes = (6, slice(256 * j, 256 * j + 256)) if j < 3 else (7, slice(256 * (j - 6), 256 * (j - 6) + 256))
            vec_grad[row : row + 1, lanes] = jnp.sum(left.astype(F32), 0, keepdims=True)
    sc1.inner(2, True)
    sc1.inner(2, False)
    df2_ref[...] = sc2.final()
    give(1)
    take(1, 0)
    sc0.core_send(1 - p.f)
    sc0.core_send(p.f)
    sc0.core_add(1 - p.l)
    take(1, 1)
    sc0.side_send()

    def contract_joined(i, carry):
        rows = image_rows(i)
        for j in range(3):
            lanes = slice(256 * j, 256 * j + 256)
            left = jnp.concatenate([qkv[k, rows] for k in range(18)], 1)
            temp[rows, lanes] = dot(left, load_runs(W.at[0], qkv_runs(0, 3 * D), lanes))
        return carry

    lax.fori_loop(0, IMG, contract_joined, 0)
    sc0.core_add(p.l)
    sc1.inner(1, True)
    sc1.inner(1, False)
    take(1, 2)
    take_column(1)

    def first_back(i, rows):
        grad = temp[rows]
        normalized, inverse = norm_parts(img_ref[rows].astype(F32))
        res_ref[rows] += norm_grad(grad, vec[0:1], normalized, inverse)
        vec_grad[0:1] += jnp.sum(grad * normalized, 0, keepdims=True)
        vec_grad[1:2] += jnp.sum(grad, 0, keepdims=True)

    by_rows(first_back)
    for h in (3, 2):
        sc0.side_add(h)
        sc0.cross_send(h)

    def two_parts(value):
        high = value.astype(BF)
        return jnp.concatenate([high, (value - high.astype(F32)).astype(BF)], 0)

    @pl.when(p.index >= 0)
    def _():
        lines = []
        for k in range(3):
            line = jnp.zeros((2 * GROUPS, 128), F32)
            for row, (kk, offset, width, base) in enumerate(table):
                if kk == k:
                    mask, places = spread(k, offset, width, base)
                    line = line + dot_nt(two_parts(mask * vec_grad[row : row + 1]), places.astype(BF))
            lines.append(line[:GROUPS] + line[GROUPS:])
        shape = (GROUPS * 8, 2 * 3 * GROUPS)
        source, target = iota(shape, 1), iota(shape, 0)
        source = jnp.where(source >= 3 * GROUPS, source - 3 * GROUPS, source)
        k = jnp.where(source >= GROUPS, 1, 0) + jnp.where(source >= 2 * GROUPS, 1, 0)
        at = jnp.where(target == 8 * (source - GROUPS * k) + k, 1.0, 0.0).astype(BF)
        vec_out[...] = dot(at, two_parts(jnp.concatenate(lines, 0))).reshape(2, 16, 8, 128)

    vec_swap = remote(vec_out.at[1 - p.c], vec_core, 3, p.sib)
    vec_swap.start()
    for h in (1, 0):
        sc0.side_add(h)
        sc0.cross_send(h)
    sc0.cross_add(3)
    sc1.come()
    for h in (2, 1, 0):
        sc0.cross_add(h)
    df1_ref[...] = sc1.final()
    own_qo = sc0.final()
    dqo_ref[p.c] = own_qo
    qo_back = remote(dqo_ref.at[p.c], swap_grad, 5, p.sib)
    qo_back.start()
    vec_swap.wait_recv()
    vec_out[p.c] += vec_core[...]
    mine = (p.l * 4 + p.z) * 2 + p.f

    def push_vec(i, carry):
        q = lax.rem(mine + i, 16)
        dev = p.block(lax.div(q, 8), lax.rem(lax.div(q, 2), 4), lax.rem(q, 2))
        remote(vec_out.at[p.c, q], vec_in.at[mine], 4, dev).start()
        return carry

    lax.fori_loop(1, 16, push_vec, 0)
    vec_in[mine] = vec_out[p.c, mine]
    most = remote(vec_out.at[p.c, pl.ds(0, 15)], vec_in.at[pl.ds(0, 15)], 4, p.sib)
    most.wait_recv()
    dvec_ref[...] = jnp.sum(vec_in[...], 0)
    qo_back.wait_recv()
    dqo_ref[1 - p.c] = swap_grad[...]

    swap_copy.wait_send()
    all_but_own.wait_send()
    share.wait_send()
    vec_swap.wait_send()
    most.wait_send()
    qo_back.wait_send()
    for g in (sm_g, qo_g, f1_g):
        g.drain()
    for s in (sc0, sc1, sc2):
        s.drain()


def swap(block, step, size):
    return lax.ppermute(block, "fsdp", [(i, i ^ step) for i in range(size)])


def pregather(block, F, r):
    step = 1
    while step < r:
        high = (lax.axis_index("fsdp") // step) % 2 == 1
        other = swap(block, step, F)
        block = jnp.concatenate([jnp.where(high, other, block), jnp.where(high, block, other)], 0)
        step *= 2
    return block


def postscatter(block, F, r):
    step = r // 2
    while step:
        high = (lax.axis_index("fsdp") // step) % 2 == 1
        middle = block.shape[0] // 2
        keep = jnp.where(high, block[middle:], block[:middle])
        send = jnp.where(high, block[:middle], block[middle:])
        block = keep + swap(send, step, F)
        step //= 2
    return block


def per_device(
    F,
    r,
    n,
    images,
    tissue,
    pair_index,
    text_embed,
    logit_scale,
    ln1_gain,
    ln1_bias,
    w_qkv,
    bias_qv,
    w_out,
    bias_out,
    ln2_gain,
    ln2_bias,
    w_fc1,
    bias_fc1,
    w_fc2,
    bias_fc2,
    cotangent,
):
    slots = images.shape[1]
    core = (lax.axis_index("fsdp") // r) % 2
    gather = lambda block: pregather(block, F, r)
    joined = gather(jnp.concatenate([w_qkv.T, w_out.T], 0).reshape(1, -1, D))
    rows_here = w_qkv.shape[1]
    q_t = joined[:, :rows_here].reshape(-1, D)
    o_t = joined[:, rows_here:].reshape(-1, D)

    def zeros(count):
        return jnp.zeros((count, D), BF)

    gap = QKV_ROWS - OUT_ROWS
    as_zero = jnp.concatenate([q_t, zeros(ROWS - QKV_ROWS), zeros(gap), o_t, zeros(OUT_ROWS)], 0)
    as_one = jnp.concatenate([zeros(QKV_ROWS), q_t, zeros(OUT_ROWS), o_t], 0)
    qo = jnp.where(core == 0, as_zero, as_one).reshape(2, ROWS, D)
    f1 = gather(w_fc1.T)
    f2 = gather(w_fc2)

    text_float = text_embed.astype(F32)
    text_unit = (text_float * lax.rsqrt(jnp.sum(text_float * text_float, -1, keepdims=True) + EPS)).astype(BF)
    vectors = jnp.stack([ln1_gain, ln1_bias, bias_out, ln2_gain, ln2_bias, bias_fc2], 1)
    vectors = gather(vectors)
    qv, first = gather(bias_qv), gather(bias_fc1)
    lanes = lambda v: jnp.pad(v, (0, 128 - v.shape[0])).reshape(1, 128)
    row0 = lanes(vectors[:, :5].T.reshape(-1))
    row1 = lanes(jnp.concatenate([vectors[:, 5], qv]))
    row2 = lanes(first)
    text_all = gather(text_unit).reshape(-1, 6, 128).transpose(1, 0, 2).reshape(-1, 128)
    pair = gather(pair_index)
    pair_rows = jnp.pad(jnp.stack([pair // 256, pair % 256], 1), ((0, 0), (0, 126))).astype(BF)
    small = jnp.concatenate([row0, row1, row2, text_all, pair_rows], 0)
    small_rows = -(-small.shape[0] // 16) * 16
    small = jnp.pad(small, ((0, small_rows - small.shape[0]), (0, 0)))

    def padded(tokens):
        return jnp.pad(tokens, ((0, 0), (0, PAD - slots), (0, 0))).reshape(TOK, D)

    mask = jnp.pad(tissue.astype(F32), ((0, 0), (0, PAD - slots))).reshape(TOK, 1)
    mask = jnp.broadcast_to(mask, (TOK, 128))
    text_in = jnp.pad(text_float, ((0, 8 - IMG), (0, 0)))
    scale = jnp.broadcast_to(logit_scale.reshape(1, 1), (8, 128))
    vmem = pl.BlockSpec(memory_space=pltpu.VMEM)
    shape = jax.ShapeDtypeStruct
    mix, res, loss, text_grad, dqo, df1, df2, dvec = pl.pallas_call(
        functools.partial(layer_kernel, F, r, n),
        out_shape=(
            shape((TOK, D), BF),
            shape((TOK, D), F32),
            shape((8, 128), F32),
            shape((8, D), F32),
            shape((2, ROWS, D), F32),
            shape((ROWS, D), F32),
            shape((ROWS, D), F32),
            shape((8, 128), F32),
        ),
        in_specs=[vmem] * 9,
        out_specs=(vmem,) * 8,
        scratch_shapes=[
            pltpu.VMEM((3, 2, 2, 4, 2, ROWS, D), BF),
            pltpu.VMEM((3, 2, 2, 4, 2, ROWS, D), BF),
            pltpu.VMEM((4, 4, 2, ROWS, D), BF),
            pltpu.VMEM((2, 3, ROWS, D), BF),
            pltpu.VMEM((2, 2, 4, 2, small_rows, 128), BF),
            pltpu.VMEM((ROWS, D), F32),
            pltpu.VMEM((TOK, D), BF),
            pltpu.VMEM((18, TOK, 128), BF),
            pltpu.VMEM((6, TOK, 128), BF),
            pltpu.VMEM((2 * IMG * 6, 1, PAD), F32),
            pltpu.VMEM((6, TOK, 128), BF),
            pltpu.VMEM((4, TOK, D), BF),
            pltpu.VMEM((4, TOK, D), BF),
            pltpu.VMEM((TOK, D), BF),
            pltpu.VMEM((max(TOK, IMG * n), D), F32),
            pltpu.VMEM((16, D), F32),
            pltpu.VMEM((16, D), F32),
            pltpu.VMEM((16, D), F32),
            pltpu.VMEM((8, D), F32),
            pltpu.VMEM((IMG * n, 128), F32),
            pltpu.VMEM((2, n // 2, 32, 128), BF),
            pltpu.VMEM((2, 16, 8, 128), F32),
            pltpu.VMEM((16, 8, 128), F32),
            pltpu.VMEM((16, 8, 128), F32),
            pltpu.SemaphoreType.DMA((4, 32)),
            pltpu.SemaphoreType.DMA((4, 32)),
            pltpu.SemaphoreType.DMA((3, 32)),
            pltpu.SemaphoreType.DMA((3, 32)),
            pltpu.SemaphoreType.DMA((16,)),
            pltpu.SemaphoreType.REGULAR((2, 8)),
        ],
        compiler_params=pltpu.CompilerParams(collective_id=0, has_side_effects=True, vmem_limit_bytes=VMEM_LIMIT),
    )(qo, f1, f2, small, padded(images), padded(cotangent), mask, text_in, scale)

    def tokens(rows):
        return rows.reshape(IMG, PAD, D)[:, :slots]

    scatter = lambda block: postscatter(block, F, r)
    chip = dqo.reshape(2 * ROWS, D)
    dq = jnp.where(core == 0, chip[:QKV_ROWS], chip[QKV_ROWS : 2 * QKV_ROWS])
    do = jnp.where(core == 0, chip[2 * QKV_ROWS : 2 * QKV_ROWS + OUT_ROWS], chip[2 * QKV_ROWS + OUT_ROWS :])
    thin = [dvec[0, 24 * k : 24 * k + 24] for k in range(5)] + [dvec[1, :24]]
    thin = [scatter(v) for v in thin]
    return (
        tokens(mix),
        tokens(res),
        loss[0, 0],
        text_grad[:IMG],
        thin[0],
        thin[1],
        scatter(dq).T,
        scatter(dvec[1, 24:72]),
        scatter(do).T,
        thin[2],
        thin[3],
        thin[4],
        scatter(df1).T,
        scatter(dvec[2, :96]),
        scatter(df2),
        thin[5],
    )


def solution(mesh):
    F = mesh.shape["fsdp"]
    n = mesh.shape["dp"] * F
    r = n // GROUPS
    both = ("dp", "fsdp")
    rows, columns = P(both), P(None, both)
    in_specs = (
        rows, rows, rows, rows, P(), rows, rows, columns, rows, columns, rows, rows, rows, columns, rows, rows, rows, rows
    )
    out_specs = (
        rows, rows, P(), rows, rows, rows, columns, rows, columns, rows, rows, rows, columns, rows, rows, rows
    )
    return jax.shard_map(
        functools.partial(per_device, F, r, n), mesh=mesh, in_specs=in_specs, out_specs=out_specs, check_vma=False
    )
```

```python
import functools
import math

import jax
import jax.numpy as jnp
from jax import lax
from jax.experimental import pallas as pl
from jax.experimental.pallas import tpu as pltpu
from jax.sharding import PartitionSpec as P

MESH = pl.DeviceIdType.MESH
MIB = 1024 * 1024
GROUPS = 32
D = 768
HEADS = 12
PAD = 208
IMG = 3
SLOTS = 196
PAIR_LANE = 72
TOK = IMG * PAD
QKV_ROWS, OUT_ROWS = 72, 24
ROWS = 96
VMEM_LIMIT = 63 * MIB
EPS = 1e-6
BF, F32 = jnp.bfloat16, jnp.float32


def dot(a, b):
    return lax.dot_general(a, b, (((1,), (0,)), ((), ())), preferred_element_type=F32)


def dot_nt(a, b):
    return lax.dot_general(a, b, (((1,), (1,)), ((), ())), preferred_element_type=F32)


def dot_exact(a, b, dims):
    return lax.dot_general(a, b, (dims, ((), ())), preferred_element_type=F32, precision=lax.Precision.HIGHEST)


def iota(shape, dim):
    return lax.broadcasted_iota(jnp.int32, shape, dim)


def split(numbers, by):
    quotient = jnp.floor((numbers.astype(F32) + 0.5) * (1.0 / by)).astype(jnp.int32)
    return quotient, numbers - quotient * by


class Pos:
    def __init__(p, F, r, n):
        p.F, p.r, p.n = F, r, n
        p.index = lax.axis_index("dp") * F + lax.axis_index("fsdp")
        p.g, p.rho = lax.div(p.index, r), lax.rem(p.index, r)
        p.c, p.z = lax.rem(p.g, 2), lax.rem(lax.div(p.g, 2), 4)
        p.x, p.y = lax.rem(lax.div(p.g, 8), 2), lax.div(p.g, 16)
        p.l = p.y + p.c * (p.x - p.y)
        p.f = p.x + p.c * (p.y - p.x)
        c, x, y, z = p.c, p.x, p.y, p.z
        p.sib = p.chip(y, x, z, 1 - c)
        p.fn = p.chip(y + c * (1 - 2 * y), x + (1 - c) * (1 - 2 * x), z, c)
        p.ln = p.chip(y + (1 - c) * (1 - 2 * y), x + c * (1 - 2 * x), z, c)
        p.up = p.chip(y, x, jnp.minimum(z + 1, 3), c)
        p.dn = p.chip(y, x, jnp.maximum(z - 1, 0), c)
        p.plane = lax.div(p.g, 2) * r + p.rho

    def device(p, linear):
        return (lax.div(linear, p.F), lax.rem(linear, p.F))

    def chip(p, y, x, z, c):
        return p.device((((y * 2 + x) * 4 + z) * 2 + c) * p.r + p.rho)

    def column(p, zz):
        return p.chip(p.y, p.x, zz, p.c)

    def at_distance(p, h, fn):
        if h == 0:
            fn(p.z)
            return

        @pl.when(p.z + h <= 3)
        def _():
            fn(p.z + h)

        @pl.when(p.z - h >= 0)
        def _():
            fn(p.z - h)

    def for_others(p, fn):
        for h in (1, 2, 3):
            p.at_distance(h, fn)

    def in_plane(p, q):
        return p.device((lax.div(q, p.r) * 2 + p.c) * p.r + lax.rem(q, p.r))

    def block(p, l, z, f):
        y, x = l + p.c * (f - l), f + p.c * (l - f)
        return p.chip(y, x, z, p.c)


def group_of(block):
    c = block // 16 if isinstance(block, int) else jnp.where(block >= 16, 1, 0)
    rest = block - c * 16
    if isinstance(block, int):
        l, z, f = rest // 8, rest // 2 % 4, rest % 2
    else:
        l = jnp.where(rest >= 8, 1, 0)
        zf = rest - 8 * l
        z = jnp.where(zf >= 2, 1, 0) + jnp.where(zf >= 4, 1, 0) + jnp.where(zf >= 6, 1, 0)
        f = zf - 2 * z
    y, x = l + c * (f - l), f + c * (l - f)
    return ((y * 2 + x) * 4 + z) * 2 + c


def enter(p):
    bar = pltpu.get_barrier_semaphore()
    for device in (p.sib, p.fn, p.ln):
        pl.semaphore_signal(bar, inc=1, device_id=device, device_id_type=MESH)
    p.for_others(lambda zz: pl.semaphore_signal(bar, inc=1, device_id=p.column(zz), device_id_type=MESH))
    pl.semaphore_wait(bar, 6)


class Gather:
    def __init__(s, p, held, send, recv, line_first=False):
        s.p, s.held, s.send, s.recv, s.line_first = p, held, send, recv, line_first

    def cp(s, at, ks, kr, dev):
        ref = s.held.at[at]
        return pltpu.make_async_remote_copy(
            src_ref=ref, dst_ref=ref, send_sem=s.send.at[ks], recv_sem=s.recv.at[kr], device_id=dev, device_id_type=MESH
        )

    def first(s):
        p = s.p
        return s.cp((p.c, p.l, p.z, p.f), 0, 0, p.fn)

    def first_in(s):
        p = s.p
        return s.cp((p.c, p.l, p.z, 1 - p.f), 0, 0, p.fn)

    def f_of(s, b):
        return s.p.f + b * (1 - 2 * s.p.f)

    def up(s, zz, b):
        return s.cp((s.p.c, s.p.l, zz, s.f_of(b)), 1 + 2 * zz + b, 1 + 2 * zz + b, s.p.up)

    def dn(s, zz, b):
        return s.cp((s.p.c, s.p.l, zz, s.f_of(b)), 9 + 2 * zz + b, 1 + 2 * zz + b, s.p.dn)

    def cross(s, zz):
        return s.cp((s.p.c, s.p.l, zz, s.p.f), 2 + 2 * zz, 2 + 2 * zz, s.p.fn)

    def cross_in(s, zz):
        return s.cp((s.p.c, s.p.l, zz, 1 - s.p.f), 2 + 2 * zz, 2 + 2 * zz, s.p.fn)

    def last(s, zz):
        return s.cp((s.p.c, s.p.l, zz), 17 + zz, 9 + zz, s.p.ln)

    def last_in(s, zz):
        return s.cp((s.p.c, 1 - s.p.l, zz), 17 + zz, 9 + zz, s.p.ln)

    def core(s, l, zz):
        return s.cp((s.p.c, l, zz), 21 + 4 * l + zz, 13 + 4 * l + zz, s.p.sib)

    def core_in(s, l, zz):
        return s.cp((1 - s.p.c, l, zz), 21 + 4 * l + zz, 13 + 4 * l + zz, s.p.sib)

    def own(s, b):
        p = s.p
        if b:
            s.first_in().wait_recv()
        else:
            s.first().start()
        if not (b and s.line_first):

            @pl.when(p.z < 3)
            def _():
                s.up(p.z, b).start()

            @pl.when(p.z > 0)
            def _():
                s.dn(p.z, b).start()

        if b:
            s.last(p.z).start()
            s.core(p.l, p.z).start()

    def line(s, h, b):
        p = s.p

        def one(zz, copy, onward):
            if b and s.line_first:
                s.cross_in(zz).wait_recv()
            else:
                copy(zz, b).wait_recv()

                @pl.when(onward)
                def _():
                    copy(zz, b).start()

                if s.line_first:
                    s.cross(zz).start()
            if b:
                s.last(zz).start()
                s.core(p.l, zz).start()

        @pl.when(p.z - h >= 0)
        def _():
            one(p.z - h, s.up, p.z < 3)

        @pl.when(p.z + h <= 3)
        def _():
            one(p.z + h, s.dn, p.z > 0)

    def arrive(s, h):
        p = s.p

        def one(zz):
            s.last_in(zz).wait_recv()
            s.core(1 - p.l, zz).start()

        if h == 0:
            one(p.z)
        else:

            @pl.when(p.z - h >= 0)
            def _():
                one(p.z - h)

            @pl.when(p.z + h <= 3)
            def _():
                one(p.z + h)

    def finish(s):
        for zz in range(4):
            for l in range(2):
                s.core_in(l, zz).wait_recv()

    def drain(s):
        p = s.p
        s.first().wait_send()
        for zz in range(4):

            @pl.when((p.z < 3) & (zz <= p.z))
            def _():
                s.up(zz, 0).wait_send()
                if not s.line_first:
                    s.up(zz, 1).wait_send()

            @pl.when((p.z > 0) & (zz >= p.z))
            def _():
                s.dn(zz, 0).wait_send()
                if not s.line_first:
                    s.dn(zz, 1).wait_send()

            if s.line_first:

                @pl.when(zz != p.z)
                def _():
                    s.cross(zz).wait_send()

            s.last(zz).wait_send()
            for l in range(2):
                s.core(l, zz).wait_send()


class Scatter:
    def __init__(s, p, sums, room, landing, send, recv, line_last=False):
        s.p, s.sums, s.room, s.landing, s.send, s.recv, s.line_last = p, sums, room, landing, send, recv, line_last

    def cp(s, src, dst, ks, kr, dev):
        return pltpu.make_async_remote_copy(
            src_ref=src, dst_ref=dst, send_sem=s.send.at[ks], recv_sem=s.recv.at[kr], device_id=dev, device_id_type=MESH
        )

    def core_cp(s, l):
        return s.cp(s.sums.at[1 - s.p.c, l], s.room(l), 1 + l, 1 + l, s.p.sib)

    def side_cp(s, zz):
        return s.cp(s.sums.at[s.p.c, 1 - s.p.l, zz], s.room(2).at[zz], 3 + zz, 3 + zz, s.p.ln)

    def f_of(s, b):
        return 1 - s.p.f if b == 0 else s.p.f

    def here(s, zz, b):
        return s.sums.at[s.p.c, s.p.l, zz, s.f_of(b)]

    def up_far(s, zz, b):
        return s.cp(s.here(zz, b), s.room(3).at[zz, b], 7 + 2 * zz + b, 7 + 2 * zz + b, s.p.up)

    def up_end(s, zz, b):
        return s.cp(s.here(zz, b), s.landing.at[b], 7 + 2 * zz + b, 15 + b, s.p.up)

    def down(s, zz, b):
        return s.cp(s.here(zz, b), s.room(3).at[zz, b], 15 + 2 * zz + b, 7 + 2 * zz + b, s.p.dn)

    def last_cp(s):
        return s.cp(s.here(s.p.z, 0), s.landing.at[2], 0, 0, s.p.fn)

    def cross_cp(s, zz):
        return s.cp(s.here(zz, 0), s.room(3).at[zz, 0], 23 + zz, 17 + zz, s.p.fn)

    def cross_send(s, h):
        s.by_distance(h, lambda zz: s.cross_cp(zz).start())

    def cross_add(s, h):
        def one(zz):
            s.cross_cp(zz).wait_recv()
            s.add(zz, 1, s.room(3).at[zz, 0])
            if h > 0:
                s.straight(zz).start()

        s.by_distance(h, one)

    def core_send(s, l):
        s.core_cp(l).start()

    def core_add(s, l):
        s.core_cp(l).wait_recv()
        room = s.room(l)

        def body(zz, carry):
            for f in range(2):
                ref = s.sums.at[s.p.c, l, zz, f]
                ref[...] = (ref[...].astype(F32) + room[zz, f].astype(F32)).astype(BF)
            return carry

        lax.fori_loop(0, 4, body, 0)

    def add(s, zz, b, ref):
        total = s.here(zz, b)
        total[...] = (total[...].astype(F32) + ref[...].astype(F32)).astype(BF)

    def by_distance(s, h, fn):
        s.p.at_distance(h, fn)

    def side_send(s):
        for h in (3, 2, 1, 0):
            s.by_distance(h, lambda zz: s.side_cp(zz).start())

    def side_add(s, h):
        def one(zz):
            s.side_cp(zz).wait_recv()
            for f in (0, 1):
                total = s.sums.at[s.p.c, s.p.l, zz, f]
                total[...] = (total[...].astype(F32) + s.room(2)[zz, f].astype(F32)).astype(BF)

        s.by_distance(h, one)

    def ends(s, h):
        p = s.p

        @pl.when(p.z == 0)
        def _():
            for b in (0, 1):
                (s.up_end if h == 1 else s.up_far)(p.z + h, b).start()

        @pl.when(p.z == 3)
        def _():
            for b in (0, 1):
                s.down(p.z - h, b).start()

    def inner(s, h, upward):
        p = s.p
        if upward:

            @pl.when((p.z == 1) | (p.z == 2) if h == 1 else p.z == 1)
            def _():
                zz = p.z + h
                for b in (0, 1):
                    s.up_far(zz, b).wait_recv()
                    s.add(zz, b, s.room(3).at[zz, b])
                    (s.up_end if h == 1 else s.up_far)(zz, b).start()

        else:

            @pl.when((p.z == 1) | (p.z == 2) if h == 1 else p.z == 2)
            def _():
                zz = p.z - h
                for b in (0, 1):
                    s.down(zz, b).wait_recv()
                    s.add(zz, b, s.room(3).at[zz, b])
                    s.down(zz, b).start()

    def come(s):
        p = s.p
        for b in (0, 1):

            @pl.when(p.z > 0)
            def _():
                s.up_end(p.z, b).wait_recv()
                s.add(p.z, b, s.landing.at[b])

            @pl.when(p.z < 3)
            def _():
                s.down(p.z, b).wait_recv()
                s.add(p.z, b, s.room(3).at[p.z, b])

            if b == 0:
                s.last_cp().start()

    def straight(s, zz):
        return s.cp(s.here(zz, 1), s.room(3).at[s.p.z, 1], 7 + zz, 7 + s.p.z, s.p.column(zz))

    def straight_in(s, zz):
        return s.cp(s.here(zz, 1), s.room(3).at[zz, 1], 7 + zz, 7 + zz, s.p.column(zz))

    def final(s):
        p = s.p
        if s.line_last:

            def one(zz):
                s.straight_in(zz).wait_recv()
                s.add(p.z, 1, s.room(3).at[zz, 1])

            p.for_others(one)
            return s.here(p.z, 1)[...].astype(F32)
        s.last_cp().wait_recv()
        return s.here(p.z, 1)[...].astype(F32) + s.landing[2].astype(F32)

    def drain(s):
        p = s.p
        for l in range(2):
            s.core_cp(l).wait_send()
        for zz in range(4):
            s.side_cp(zz).wait_send()
            if s.line_last:
                s.cross_cp(zz).wait_send()

                @pl.when(zz != p.z)
                def _():
                    s.straight(zz).wait_send()

            else:

                @pl.when(zz > p.z)
                def _():
                    s.up_far(zz, 0).wait_send()
                    s.up_far(zz, 1).wait_send()

                @pl.when(zz < p.z)
                def _():
                    s.down(zz, 0).wait_send()
                    s.down(zz, 1).wait_send()

        if not s.line_last:
            s.last_cp().wait_send()


def qkv_runs(start, stop):
    runs, row = [], start
    while row < stop:
        chip, inside = divmod(row, 2 * QKV_ROWS)
        z, x, y = chip % 4, chip // 4 % 2, chip // 8
        first = inside < ROWS
        until = min(stop, chip * 2 * QKV_ROWS + (ROWS if first else 2 * QKV_ROWS))
        low = inside if first else inside - ROWS
        at = (0, y, z, x) if first else (1, x, z, y)
        runs.append((at, low, low + until - row))
        row = until
    return runs


def out_runs(start, stop):
    runs, row = [], start
    while row < stop:
        chip, inside = divmod(row, 2 * OUT_ROWS)
        z, x, y = chip % 4, chip // 4 % 2, chip // 8
        until = min(stop, (chip + 1) * 2 * OUT_ROWS)
        low = inside + 2 * (QKV_ROWS - OUT_ROWS) // 2
        runs.append(((1, x, z, y), low, low + until - row))
        row = until
    return runs


def load_runs(ref, runs, lanes=slice(None)):
    return jnp.concatenate([ref[at + (slice(a, b), lanes)] for at, a, b in runs], 0)


def store_runs(ref, runs, value):
    row = 0
    for at, a, b in runs:
        ref[at + (slice(a, b), slice(None))] = value[row : row + b - a]
        row += b - a


def slabs(ref, first, count):
    return jnp.concatenate([ref[first + k] for k in range(count)], 1)


def norm_parts(values):
    centered = values - jnp.mean(values, -1, keepdims=True)
    inverse = lax.rsqrt(jnp.mean(centered * centered, -1, keepdims=True) + EPS)
    return centered * inverse, inverse


def norm_grad(grad, gain, normalized, inverse):
    h = grad * gain
    return (h - jnp.mean(h, -1, keepdims=True) - normalized * jnp.mean(h * normalized, -1, keepdims=True)) * inverse


def gelu_parts(x):
    z = jnp.abs(x) * math.sqrt(0.5)
    under = 1.0 + 0.3275911 * z
    t = pl.reciprocal(under, approx=True)
    t = t * (2.0 - under * t)
    bell = jnp.exp(-0.5 * x * x)
    poly = ((((1.061405429 * t - 1.453152027) * t + 1.421413741) * t - 0.284496736) * t + 0.254829592) * t
    tail = 0.5 * poly * bell
    cdf = jnp.where(x >= 0, 1.0 - tail, tail)
    return x * cdf, cdf + x * bell * (1.0 / math.sqrt(2.0 * math.pi))


CUTS = ((0, 48), (48, 48), (96, 48), (144, SLOTS - 144))


def by_rows(fn):
    def body(i, carry):
        for start, size in CUTS:
            fn((i, slice(start, start + size)), pl.ds(pl.multiple_of(i * PAD + start, 16), size))
        return carry

    lax.fori_loop(0, IMG, body, 0)


def layer_kernel(
    F,
    r,
    n,
    wq_ref,
    wo_ref,
    f1_ref,
    f2_ref,
    thin_ref,
    group_ref,
    img_ref,
    cot_ref,
    tissue_ref,
    text_ref,
    scale_ref,
    mix_ref,
    res_ref,
    loss_ref,
    tg_ref,
    dq_ref,
    do_ref,
    df1_ref,
    df2_ref,
    dvec_ref,
    W,
    G,
    room,
    ends,
    small,
    mask_ref,
    mask_line,
    text_rows,
    swap_grad,
    norm1,
    qkv,
    att,
    lse,
    sec,
    act,
    slope,
    grad2,
    temp,
    vec,
    vec_grad,
    pooled,
    row_grad,
    pair_rows,
    units,
    vec_out,
    vec_core,
    vec_in,
    g_send,
    g_recv,
    s_send,
    s_recv,
    misc,
    credit,
):
    p = Pos(F, r, n)
    half = n // 2
    total = IMG * n
    per_group = IMG * r
    small_rows = small.shape[4]
    qo_g, f1_g, f2_g = (Gather(p, W.at[m], g_send.at[m], g_recv.at[m], m == 0) for m in range(3))
    sm_g = Gather(p, small, g_send.at[3], g_recv.at[3], True)

    def remote(src, dst, k, dev):
        return pltpu.make_async_remote_copy(
            src_ref=src, dst_ref=dst, send_sem=misc.at[2 * k], recv_sem=misc.at[2 * k + 1], device_id=dev, device_id_type=MESH
        )

    first_core = p.c == 0
    q_t, o_t = wq_ref[...].astype(F32), wo_ref[...].astype(F32)

    def empty(rows):
        return jnp.zeros((rows, D), F32)

    gap = QKV_ROWS - OUT_ROWS
    to_zero = (
        jnp.concatenate([q_t, empty(ROWS - QKV_ROWS)], 0),
        jnp.concatenate([empty(QKV_ROWS), q_t[: ROWS - QKV_ROWS]], 0),
    )
    to_one = (
        jnp.concatenate([empty(gap), o_t, empty(OUT_ROWS)], 0),
        jnp.concatenate([q_t[ROWS - QKV_ROWS :], empty(OUT_ROWS), o_t], 0),
    )
    W[0, p.c, p.l, p.z, p.f] = jnp.where(first_core, to_zero[0], to_one[1]).astype(BF)
    G[0, 0, 0, 0, 1] = jnp.where(first_core, to_one[0], to_zero[1]).astype(BF)
    enter(p)
    swap_copy = remote(G.at[0, 0, 0, 0, 1], G.at[0, 0, 0, 0, 0], 0, p.sib)
    swap_copy.start()

    def unit(values):
        inverse = lax.rsqrt(jnp.sum(values * values, -1, keepdims=True) + EPS)
        return values * inverse, inverse

    text_rows[...] = jnp.zeros(text_rows.shape, F32)
    text_rows[0:per_group] = group_ref[...].astype(F32)
    group_units = unit(text_rows[...])[0].astype(BF)
    own_small = jnp.zeros((small_rows, 128), F32)
    for k in range(6):
        shape = (small_rows, group_units.shape[0])
        at = (iota(shape, 0) == iota(shape, 1) + 3 + per_group * k) & (iota(shape, 1) < per_group)
        own_small = own_small + dot(jnp.where(at, 1.0, 0.0).astype(BF), group_units[:, 128 * k : 128 * k + 128])
    at = jnp.where(iota((small_rows, 8), 0) == iota((small_rows, 8), 1), 1.0, 0.0)
    thin = jnp.where(iota((8, 128), 0) < 3, jnp.concatenate([thin_ref[...].astype(F32)] + [jnp.zeros((5, 128), F32)], 0), 0.0)
    small[p.c, p.l, p.z, p.f] = (own_small + dot(at.astype(BF), thin.astype(BF))).astype(BF)
    sm_g.own(0)
    W[1, p.c, p.l, p.z, p.f] = f1_ref[...]
    swap_copy.wait_recv()
    own_block = W.at[0, p.c, p.l, p.z, p.f]
    own_block[...] = (own_block[...].astype(F32) + G[0, 0, 0, 0, 0].astype(F32)).astype(BF)
    qo_g.own(0)
    f1_g.own(0)
    W[2, p.c, p.l, p.z, p.f] = f2_ref[...]
    vec_grad[...] = jnp.zeros(vec_grad.shape, F32)
    mask_line[...] = jnp.zeros(mask_line.shape, F32)
    mask_line[0:IMG, 0:SLOTS] = tissue_ref[...].astype(F32)
    for i in range(IMG):
        tail = slice(i * PAD + SLOTS // 16 * 16, (i + 1) * PAD)
        nothing = jnp.zeros((PAD - SLOTS // 16 * 16, D), BF)
        norm1[tail] = nothing
        grad2[tail] = nothing
        for k in range(6):
            sec[k, tail] = nothing[:, :128]
        line = jnp.broadcast_to(mask_line[i : i + 1], (128, 256))
        mask_ref[i * PAD : i * PAD + PAD] = line.T[:PAD]
    sm_g.own(1)
    qo_g.own(1)
    for h in (1, 2, 3):
        sm_g.line(h, 0)
        qo_g.line(h, 0)
        sm_g.line(h, 1)
        qo_g.line(h, 1)
        sm_g.arrive(h - 1)
        if h == 1:
            f1_g.own(1)
        if h == 2:
            f1_g.line(1, 0)
        if h == 3:
            f1_g.line(1, 1)
            sm_g.arrive(3)
        qo_g.arrive(h - 1)
    sm_g.finish()


    def picked(k):
        source, target = iota((GROUPS, GROUPS * small_rows), 1), iota((GROUPS, GROUPS * small_rows), 0)
        return dot(jnp.where(source == target * small_rows + k, 1.0, 0.0).astype(BF), small[...].reshape(GROUPS * small_rows, 128)).astype(BF)

    table = [(0, 0, 24, 0), (0, 24, 24, 0), (0, 48, 24, 0), (0, 72, 24, 0), (0, 96, 24, 0), (1, 0, 24, 0), (1, 24, 48, 0), (1, 24, 48, D)]
    table += [(2, 0, 96, D * q) for q in range(4)]

    def spread(k, offset, width, base):
        owner, inside = split(iota((1, D), 1) + base, width)
        names = iota((GROUPS, 1), 0)
        names = names if k == 2 else group_of(names)
        mask = jnp.where(names == owner, 1.0, 0.0)
        places = jnp.where(iota((128, D), 0) == inside + offset, 1.0, 0.0)
        return mask, places

    @pl.when(p.index >= 0)
    def _():
      message_rows = [picked(k) for k in range(3)]
      for row, (k, offset, width, base) in enumerate(table):
        mask, places = spread(k, offset, width, base)
        vec[row : row + 1, :] = jnp.sum(mask * dot(message_rows[k], places.astype(BF)), 0, keepdims=True)

    def first_norm(slots, rows):
        normalized, _ = norm_parts(img_ref[slots].astype(F32))
        norm1[rows] = (normalized * vec[0:1] + vec[1:2]).astype(BF)

    by_rows(first_norm)
    f1_g.arrive(0)
    f1_g.line(2, 0)
    f2_g.own(0)
    qo_g.arrive(3)
    qo_g.finish()
    swap_copy.wait_send()

    for j in range(9):
        part = dot_nt(norm1[...], load_runs(W.at[0], qkv_runs(256 * j, 256 * j + 256)))
        if j < 3:
            part = part + vec[6:7, 256 * j : 256 * j + 256]
        elif j >= 6:
            part = part + vec[7:8, 256 * (j - 6) : 256 * (j - 6) + 256]
        part = part.astype(BF)
        qkv[2 * j] = part[:, :128]
        qkv[2 * j + 1] = part[:, 128:]
        if j == 4:
            f1_g.line(2, 1)
            f1_g.arrive(1)
            f2_g.own(1)

    def image_rows(i):
        return pl.ds(pl.multiple_of(i * PAD, 16), PAD)

    low = iota((1, 128), 1) < 64

    def halves(value):
        zero = jnp.zeros_like(value)
        return jnp.where(low, value, zero), jnp.where(low, zero, value)

    def head_pair(i, pair):
        rows = pl.ds(pl.multiple_of(i * PAD, 16), PAD)
        return rows, qkv[pair, rows], qkv[6 + pair, rows], qkv[12 + pair, rows]

    PAIRS = 2

    def attend(it, carry):
        i, first = lax.div(it, 6 // PAIRS), lax.rem(it, 6 // PAIRS) * PAIRS
        bars = jnp.concatenate([jnp.where(mask_ref[image_rows(i)] > 0, 0.0, -1e30)] * 2, 1)[:, :PAD]
        results = []
        for step in range(PAIRS):
            rows, q, k, v = head_pair(i, first + step)
            v_t = v.T
            parts = []
            for h, k_h in enumerate(halves(k * jnp.asarray(0.125, BF))):
                scores = dot_nt(k_h, q) + bars
                top = jnp.max(scores, 0, keepdims=True)
                terms = jnp.exp(scores - top)
                amount = jnp.sum(terms, 0, keepdims=True)
                lse[(i * 6 + first + step) * 2 + h] = top + jnp.log(amount)
                parts.append(dot(v_t[64 * h : 64 * h + 64], terms.astype(BF)) * (1.0 / amount))
            results.append(jnp.concatenate(parts, 0).T.astype(BF))
        for step in range(PAIRS):
            att[first + step, rows] = results[step]
        return carry

    lax.fori_loop(0, 3, attend, 0)
    f1_g.line(3, 0)
    f2_g.line(1, 0)
    f1_g.line(3, 1)
    f1_g.arrive(2)
    lax.fori_loop(3, 5, attend, 0)
    f2_g.line(1, 1)
    f1_g.arrive(3)
    f2_g.arrive(0)
    lax.fori_loop(5, 7, attend, 0)
    f2_g.line(2, 0)
    f2_g.line(2, 1)
    f2_g.arrive(1)
    lax.fori_loop(7, 9, attend, 0)

    attended = slabs(att, 0, 6)
    for j in range(3):
        lanes = slice(256 * j, 256 * j + 256)
        part = dot_nt(attended, load_runs(W.at[0], out_runs(256 * j, 256 * j + 256)))
        for i in range(IMG):
            res_ref[i, :, lanes] = img_ref[i, :, lanes].astype(F32) + part[i * PAD : i * PAD + SLOTS] + vec[2:3, lanes]

    def second_norm(slots, rows):
        normalized, _ = norm_parts(res_ref[slots])
        value = (normalized * vec[3:4] + vec[4:5]).astype(BF)
        for k in range(6):
            sec[k, rows] = value[:, 128 * k : 128 * k + 128]

    by_rows(second_norm)
    f1_g.finish()

    def expand(it, carry):
        q, rows = lax.div(it, IMG), image_rows(lax.rem(it, IMG))
        left = jnp.concatenate([sec[k, rows] for k in range(6)], 1)
        pre = dot_nt(left, W[1, lax.div(q, 2), lax.rem(q, 2)].reshape(D, D)) + vec[pl.ds(8 + q, 1), :]
        value, derivative = gelu_parts(pre)
        act[q, rows] = value.astype(BF)
        slope[q, rows] = derivative.astype(BF)
        return carry

    lax.fori_loop(0, 3, expand, 0)
    f2_g.line(3, 0)
    f2_g.line(3, 1)
    f2_g.arrive(2)
    lax.fori_loop(3, 9, expand, 0)
    f2_g.arrive(3)
    lax.fori_loop(9, 12, expand, 0)
    f2_g.finish()

    def contract(hidden_units, m):
        def body(i, carry):
            rows = image_rows(i)
            for j in range(3):
                lanes = slice(256 * j, 256 * j + 256)
                left = jnp.concatenate([hidden_units[q, rows] for q in range(4)], 1)
                temp[rows, lanes] = dot(left, W[m, :, :, :, :, :, lanes].reshape(4 * D, 256))
            return carry

        lax.fori_loop(0, IMG, body, 0)

    contract(act, 2)

    def wide(column):
        return jnp.concatenate([column] * 6, 1)

    pooled[...] = jnp.zeros(pooled.shape, F32)
    for i in range(IMG):
        sums, count = jnp.zeros((1, D), F32), jnp.zeros((1, 128), F32)
        for start, size in CUTS:
            rows = pl.ds(i * PAD + start, size)
            mask = mask_ref[rows]
            slots = (i, slice(start, start + size))
            outputs = (res_ref[slots] + temp[rows] + vec[5:6]) * wide(mask)
            mix_ref[slots] = outputs.astype(BF)
            sums = sums + jnp.sum(outputs, 0, keepdims=True)
            count = count + jnp.sum(mask, 0, keepdims=True)
        pooled[i : i + 1, :] = sums / wide(count)
        pooled[8 + i : 9 + i, :] = wide(count)

    def unit_grad(grad, values, inverse):
        return inverse * grad - inverse * inverse * inverse * values * jnp.sum(values * grad, -1, keepdims=True)

    own_pooled = pooled[0:8]
    image_unit, image_inverse = unit(own_pooled)
    image_unit = image_unit.astype(BF)
    message = jnp.zeros((32, 128), F32)
    for k in range(6):
        at = jnp.where((iota((32, 8), 0) == iota((32, 8), 1) + IMG * k) & (iota((32, 8), 1) < IMG), 1.0, 0.0).astype(BF)
        message = message + dot(at, image_unit[:, 128 * k : 128 * k + 128])
    units[p.c, p.plane] = message.astype(BF)

    def push(i, carry):
        q = lax.rem(p.plane + i, half)
        remote(units.at[p.c, p.plane], units.at[p.c, p.plane], 1, p.in_plane(q)).start()
        return carry

    lax.fori_loop(1, half, push, 0)
    all_but_own = remote(units.at[p.c, pl.ds(0, half - 1)], units.at[p.c, pl.ds(0, half - 1)], 1, p.sib)

    def gathered(source_chunks, chunk_rows, row_of, tiles, base):
        results = []
        for k in range(tiles):
            value = jnp.zeros((total, 128), F32)
            for number, chunk in source_chunks:
                owner, inside = split(iota((1, chunk_rows), 1), base)
                target = row_of(owner, inside, number, k)
                value = value + dot(jnp.where(iota((total, chunk_rows), 0) == target, 1.0, 0.0).astype(BF), chunk)
            results.append(value)
        return results

    def text_row(owner, inside, number, k):
        at = inside - 3 - per_group * k
        group = group_of(owner + 8 * number)
        return jnp.where((at >= 0) & (at < per_group), group * per_group + at, -1)

    chunks = [(2 * c + l, small[c, l].reshape(8 * small_rows, 128)) for c in range(2) for l in range(2)]
    tiles = gathered(chunks, 8 * small_rows, text_row, 6, small_rows)
    for b in range(r):
        for k in range(6):
            G[1, b // 16, b // 8 % 2, b // 2 % 4, b % 2, :, 128 * k : 128 * k + 128] = tiles[k][ROWS * b : ROWS * b + ROWS].astype(BF)

    def texts():
        return jnp.concatenate([G[1, b // 16, b // 8 % 2, b // 2 % 4, b % 2] for b in range(r)], 0)

    owner, inside = split(iota((total, 1), 0), per_group)
    lines = dot(jnp.where(owner == group_of(iota((1, GROUPS), 1)), 1.0, 0.0).astype(BF), picked(1))
    places = iota((1, 128), 1)
    high = jnp.sum(jnp.where(places == inside + PAIR_LANE, lines, 0.0), 1, keepdims=True)
    rest = jnp.sum(jnp.where(places == inside + PAIR_LANE + per_group, lines, 0.0), 1, keepdims=True)
    pair_rows[...] = jnp.broadcast_to(high * 256.0 + rest, (total, 128))

    all_but_own.wait_recv()
    share = remote(units.at[p.c], units.at[p.c], 2, p.sib)
    share.start()
    remote(units.at[1 - p.c], units.at[1 - p.c], 2, p.sib).wait_recv()

    for k in range(6):

        def add_chunk(number, value, k=k):
            c, at = lax.div(number * 16, half), lax.rem(number * 16, half)
            owner, inside = split(iota((1, 512), 1), 32)
            q = owner + at
            t = inside - IMG * k
            if r == 1:
                linear = 2 * q + c
            else:
                chip, rho = split(q, r)
                linear = (2 * chip + c) * r + rho
            target = jnp.where((t >= 0) & (t < IMG), linear * IMG + t, -1)
            pick = jnp.where(iota((total, 512), 0) == target, 1.0, 0.0).astype(BF)
            return value + dot(pick, units[c, pl.ds(at, 16)].reshape(512, 128))

        value = lax.fori_loop(0, n // 16, add_chunk, jnp.zeros((total, 128), F32)).astype(BF)
        for b in range(r):
            G[2, b // 16, b // 8 % 2, b // 2 % 4, b % 2, :, 128 * k : 128 * k + 128] = value[ROWS * b : ROWS * b + ROWS]

    def block(m, b):
        return G[m, lax.div(b, 16), lax.rem(lax.div(b, 8), 2), lax.rem(lax.div(b, 2), 4), lax.rem(b, 2)]

    scale = scale_ref[0, 0]
    row = jnp.zeros((1, total), F32)

    def similar(b, col_top):
        rows = pl.ds(pl.multiple_of(b * ROWS, ROWS), ROWS)
        part = dot_nt(block(2, b), texts()) * scale
        temp[rows, :total] = part
        return jnp.maximum(col_top, jnp.max(part, 0, keepdims=True))

    col_top = lax.fori_loop(0, r, similar, row - jnp.inf)

    def by_blocks(fn):
        def body(b, carry):
            rows = pl.ds(pl.multiple_of(b * ROWS, ROWS), ROWS)
            part = temp[rows, :total]
            top = jnp.max(part, 1, keepdims=True)
            row_lse = top + jnp.log(jnp.sum(jnp.exp(part - top), 1, keepdims=True))
            match = jnp.where(iota((ROWS, total), 1) == pair_of(rows), 1.0, 0.0)
            return fn(b, part, row_lse, match, carry)

        return body

    def pair_of(rows):
        return pair_rows[rows][:, 0:1].astype(jnp.int32)

    def sums(b, part, row_lse, match, carry):
        col_sum, loss = carry
        paired = jnp.sum(jnp.sum(part * match, 1, keepdims=True), 0, keepdims=True)
        return col_sum + jnp.sum(jnp.exp(part - col_top), 0, keepdims=True), loss + jnp.sum(row_lse, 0, keepdims=True) - 2.0 * paired

    col_sum, loss = lax.fori_loop(0, r, by_blocks(sums), (row, jnp.zeros((1, 1), F32)))
    col_lse = col_top + jnp.log(col_sum)
    loss = (loss + jnp.sum(col_lse, 1, keepdims=True)) / (2.0 * total)
    loss_ref[...] = loss

    def own_of(places):
        return jnp.where((places == iota(places.shape, 0) + IMG * p.index) & (iota(places.shape, 0) < IMG), 1.0, 0.0).astype(BF)

    own = own_of(iota((8, total), 1))

    def similar_grad(b, part, row_lse, match, carry):
        grad_rows, grad_text = carry
        grad = 0.5 * (jnp.exp(part - row_lse) + jnp.exp(part - col_lse)) - match
        grad = (scale * grad).astype(BF)
        own_rows = own_of(iota((8, ROWS), 1) + b * ROWS)
        return grad_rows + dot(own_rows, grad), grad_text + dot(dot_nt(own, grad).astype(BF), block(2, b))

    grad_rows, grad_text = lax.fori_loop(0, r, by_blocks(similar_grad), (jnp.zeros((8, total), F32), jnp.zeros((8, D), F32)))
    grad_unit = dot(grad_rows.astype(BF), texts())
    row_grad[...] = unit_grad(grad_unit, own_pooled, image_inverse) / jnp.maximum(pooled[8:16], 1.0)
    own_text = text_ref[...].astype(F32)
    _, text_inverse = unit(own_text)
    tg_ref[...] = unit_grad(grad_text[:IMG], own_text, text_inverse)

    sc0, sc1, sc2 = (
        Scatter(p, G.at[m], area, ends.at[1 if m == 1 else 0], s_send.at[m], s_recv.at[m], m == 0)
        for m, area in (
            (0, lambda k: room.at[k]),
            (1, lambda k: W.at[2, k // 2, k % 2] if isinstance(k, int) else W.at[2, 0, k]),
            (2, lambda k: room.at[k]),
        )
    )

    def out_grad(slots, rows):
        return wide(mask_ref[rows]) * (cot_ref[slots].astype(F32) + row_grad[pl.ds(slots[0], 1), :])

    def first_round(slots, rows):
        value = out_grad(slots, rows).astype(BF)
        grad2[rows] = value
        vec_grad[5:6] += jnp.sum(value.astype(F32), 0, keepdims=True)

    by_rows(first_round)
    order = ((1 - p.c, 1 - p.f), (p.c, 1 - p.l), (1 - p.c, p.f), (p.c, p.l))

    def weight_grad(m, at, left, right):
        left = left.T
        for j in range(3):
            lanes = slice(256 * j, 256 * j + 256)
            G[(m,) + at + (slice(None), slice(None), slice(None), lanes)] = (
                dot(left, right[:, lanes]).astype(BF).reshape(4, 2, ROWS, 256)
            )

    for step, at in enumerate(order):
        weight_grad(2, at, act[2 * at[0] + at[1]], grad2[...])
        if step == 0:
            sc2.core_send(1 - p.f)
        if step == 2:
            sc2.core_send(p.f)
    for q in range(4):
        for part in range(2):
            lanes = slice(384 * part, 384 * part + 384)
            value = dot_nt(grad2[...], W[2, q // 2, q % 2, 2 * part : 2 * part + 2].reshape(384, D)) * slope[q, :, lanes].astype(F32)
            value = value.astype(BF)
            slope[q, :, lanes] = value
            vec_grad[8 + q : 9 + q, lanes] = jnp.sum(value.astype(F32), 0, keepdims=True)
        if q == 0:
            sc2.core_add(1 - p.l)
            sc2.side_send()
        if q == 1:
            sc2.core_add(p.l)
    sc2.side_add(3)
    sc2.ends(3)
    f2_g.drain()

    def give(k):
        for at, device in ((0, p.sib), (1, p.ln), (2, p.fn)):
            pl.semaphore_signal(credit.at[k, at], inc=1, device_id=device, device_id_type=MESH)
        p.for_others(lambda zz: pl.semaphore_signal(credit.at[k, 3 + p.z], inc=1, device_id=p.column(zz), device_id_type=MESH))

    def take(k, *which):
        for at in which:
            pl.semaphore_wait(credit.at[k, at], 1)

    def take_column(k):
        p.for_others(lambda zz: pl.semaphore_wait(credit.at[k, 3 + zz], 1))

    give(0)
    for step, at in enumerate(order):
        weight_grad(1, at, slope[2 * at[0] + at[1]], slabs(sec, 0, 6))
        if step == 0:
            take(0, 0)
            sc1.core_send(1 - p.f)
        if step == 2:
            sc1.core_send(p.f)
            sc2.side_add(2)
            sc2.ends(2)
    contract(slope, 1)
    sc1.core_add(1 - p.l)
    take(0, 1)
    sc1.side_send()
    sc1.core_add(p.l)
    sc2.side_add(1)
    sc2.ends(1)
    sc2.side_add(0)

    def second_back(slots, rows):
        grad = temp[rows]
        normalized, inverse = norm_parts(res_ref[slots])
        total_grad = out_grad(slots, rows) + norm_grad(grad, vec[3:4], normalized, inverse)
        res_ref[slots] = total_grad
        rounded = total_grad.astype(BF)
        grad2[rows] = rounded
        vec_grad[3:4] += jnp.sum(grad * normalized, 0, keepdims=True)
        vec_grad[4:5] += jnp.sum(grad, 0, keepdims=True)
        vec_grad[2:3] += jnp.sum(rounded.astype(F32), 0, keepdims=True)

    by_rows(second_back)
    sc2.inner(2, True)
    sc2.inner(2, False)
    attended = slabs(att, 0, 6)
    for j in range(3):
        lanes = slice(256 * j, 256 * j + 256)
        store_runs(G.at[0], out_runs(256 * j, 256 * j + 256), dot(grad2[:, lanes].T, attended).astype(BF))
    for j in range(3):
        lanes = slice(256 * j, 256 * j + 256)
        part = dot(grad2[...], load_runs(W.at[0], out_runs(0, D), lanes)).astype(BF)
        sec[2 * j] = part[:, :128]
        sec[2 * j + 1] = part[:, 128:]

    def attend_back(it, carry):
        i, first = lax.div(it, 6 // PAIRS), lax.rem(it, 6 // PAIRS) * PAIRS
        bars = jnp.concatenate([jnp.where(mask_ref[image_rows(i)] > 0, 0.0, -1e30)] * 2, 1)[:, :PAD]
        results = []
        for step in range(PAIRS):
            rows, plain_q, k, v = head_pair(i, first + step)
            grad_out = sec[first + step, rows]
            q, k = plain_q * jnp.asarray(0.125, BF), k * jnp.asarray(0.125, BF)
            k_t = k.T
            q_halves, out_halves, v_halves = halves(q), halves(grad_out), halves(v)
            grad_v, grad_k, grad_q = 0.0, 0.0, []
            for h, k_h in enumerate(halves(k)):
                scores = dot_nt(k_h, plain_q) + bars
                probs = jnp.exp(scores - lse[(i * 6 + first + step) * 2 + h])
                grad_v = grad_v + dot(probs.astype(BF), out_halves[h])
                grad_probs = dot_nt(v_halves[h], grad_out)
                grad_scores = (probs * (grad_probs - jnp.sum(grad_probs * probs, 0, keepdims=True))).astype(BF)
                grad_k = grad_k + dot(grad_scores, q_halves[h])
                grad_q.append(dot(k_t[64 * h : 64 * h + 64], grad_scores))
            results.append((jnp.concatenate(grad_q, 0).T.astype(BF), grad_k.astype(BF), grad_v.astype(BF)))
        for step in range(PAIRS):
            for which in range(3):
                qkv[6 * which + first + step, rows] = results[step][which]
        return carry

    take(0, 2)
    take_column(0)
    lax.fori_loop(0, 2, attend_back, 0)
    sc1.side_add(3)
    sc1.ends(3)
    lax.fori_loop(2, 4, attend_back, 0)
    sc2.inner(1, True)
    sc2.inner(1, False)
    sc1.side_add(2)
    sc1.ends(2)
    lax.fori_loop(4, 6, attend_back, 0)
    sc1.side_add(1)
    sc1.ends(1)
    sc1.side_add(0)
    lax.fori_loop(6, 9, attend_back, 0)
    sc2.come()
    for j in range(9):
        left = slabs(qkv, 2 * j, 2)
        store_runs(G.at[0], qkv_runs(256 * j, 256 * j + 256), dot(left.T, norm1[...]).astype(BF))
        if j < 3 or j >= 6:
            row, lanes = (6, slice(256 * j, 256 * j + 256)) if j < 3 else (7, slice(256 * (j - 6), 256 * (j - 6) + 256))
            vec_grad[row : row + 1, lanes] = jnp.sum(left.astype(F32), 0, keepdims=True)
    sc1.inner(2, True)
    sc1.inner(2, False)
    df2_ref[...] = sc2.final()
    give(1)
    take(1, 0)
    sc0.core_send(1 - p.f)
    sc0.core_send(p.f)
    sc0.core_add(1 - p.l)
    take(1, 1)
    sc0.side_send()

    def contract_joined(i, carry):
        rows = image_rows(i)
        for j in range(3):
            lanes = slice(256 * j, 256 * j + 256)
            left = jnp.concatenate([qkv[k, rows] for k in range(18)], 1)
            temp[rows, lanes] = dot(left, load_runs(W.at[0], qkv_runs(0, 3 * D), lanes))
        return carry

    lax.fori_loop(0, IMG, contract_joined, 0)
    sc0.core_add(p.l)
    sc1.inner(1, True)
    sc1.inner(1, False)
    take(1, 2)
    take_column(1)

    def first_back(slots, rows):
        grad = temp[rows]
        normalized, inverse = norm_parts(img_ref[slots].astype(F32))
        res_ref[slots] += norm_grad(grad, vec[0:1], normalized, inverse)
        vec_grad[0:1] += jnp.sum(grad * normalized, 0, keepdims=True)
        vec_grad[1:2] += jnp.sum(grad, 0, keepdims=True)

    by_rows(first_back)
    for h in (3, 2):
        sc0.side_add(h)
        sc0.cross_send(h)

    def two_parts(value):
        high = value.astype(BF)
        return jnp.concatenate([high, (value - high.astype(F32)).astype(BF)], 0)

    @pl.when(p.index >= 0)
    def _():
        lines = []
        for k in range(3):
            line = jnp.zeros((2 * GROUPS, 128), F32)
            for row, (kk, offset, width, base) in enumerate(table):
                if kk == k:
                    mask, places = spread(k, offset, width, base)
                    line = line + dot_nt(two_parts(mask * vec_grad[row : row + 1]), places.astype(BF))
            lines.append(line[:GROUPS] + line[GROUPS:])
        shape = (GROUPS * 8, 2 * 3 * GROUPS)
        source, target = iota(shape, 1), iota(shape, 0)
        source = jnp.where(source >= 3 * GROUPS, source - 3 * GROUPS, source)
        k = jnp.where(source >= GROUPS, 1, 0) + jnp.where(source >= 2 * GROUPS, 1, 0)
        at = jnp.where(target == 8 * (source - GROUPS * k) + k, 1.0, 0.0).astype(BF)
        vec_out[...] = dot(at, two_parts(jnp.concatenate(lines, 0))).reshape(2, 16, 8, 128)

    vec_swap = remote(vec_out.at[1 - p.c], vec_core, 3, p.sib)
    vec_swap.start()
    for h in (1, 0):
        sc0.side_add(h)
        sc0.cross_send(h)
    sc0.cross_add(3)
    sc1.come()
    for h in (2, 1, 0):
        sc0.cross_add(h)
    df1_ref[...] = sc1.final()
    own_qo = sc0.final()
    swap_grad[0] = own_qo
    qo_back = remote(swap_grad.at[0], swap_grad.at[1], 5, p.sib)
    qo_back.start()
    vec_swap.wait_recv()
    vec_out[p.c] += vec_core[...]
    mine = (p.l * 4 + p.z) * 2 + p.f

    def push_vec(i, carry):
        q = lax.rem(mine + i, 16)
        dev = p.block(lax.div(q, 8), lax.rem(lax.div(q, 2), 4), lax.rem(q, 2))
        remote(vec_out.at[p.c, q], vec_in.at[mine], 4, dev).start()
        return carry

    lax.fori_loop(1, 16, push_vec, 0)
    vec_in[mine] = vec_out[p.c, mine]
    most = remote(vec_out.at[p.c, pl.ds(0, 15)], vec_in.at[pl.ds(0, 15)], 4, p.sib)
    most.wait_recv()
    dvec_ref[...] = jnp.sum(vec_in[...], 0)
    qo_back.wait_recv()
    other_qo = swap_grad[1]
    dq_ref[...] = jnp.where(
        first_core, own_qo[:QKV_ROWS], jnp.concatenate([other_qo[QKV_ROWS:], own_qo[:gap]], 0)
    )
    do_ref[...] = jnp.where(first_core, other_qo[gap : gap + OUT_ROWS], own_qo[QKV_ROWS:])

    all_but_own.wait_send()
    share.wait_send()
    vec_swap.wait_send()
    most.wait_send()
    qo_back.wait_send()
    for g in (sm_g, qo_g, f1_g):
        g.drain()
    for s in (sc0, sc1, sc2):
        s.drain()


def swap(block, step, size):
    return lax.ppermute(block, "fsdp", [(i, i ^ step) for i in range(size)])


def pregather(block, F, r):
    step = 1
    while step < r:
        high = (lax.axis_index("fsdp") // step) % 2 == 1
        other = swap(block, step, F)
        block = jnp.concatenate([jnp.where(high, other, block), jnp.where(high, block, other)], 0)
        step *= 2
    return block


def postscatter(block, F, r):
    step = r // 2
    while step:
        high = (lax.axis_index("fsdp") // step) % 2 == 1
        lower, upper = jnp.split(block, 2)
        block = jnp.where(high, upper, lower) + swap(jnp.where(high, lower, upper), step, F)
        step //= 2
    return block


def per_device(
    F,
    r,
    n,
    images,
    tissue,
    pair_index,
    text_embed,
    logit_scale,
    ln1_gain,
    ln1_bias,
    w_qkv,
    bias_qv,
    w_out,
    bias_out,
    ln2_gain,
    ln2_bias,
    w_fc1,
    bias_fc1,
    w_fc2,
    bias_fc2,
    cotangent,
):
    gather = functools.partial(pregather, F=F, r=r)

    pair = gather(pair_index)
    vectors = [gather(v) for v in (ln1_gain, ln1_bias, bias_out, ln2_gain, ln2_bias, bias_fc2, bias_qv, bias_fc1)]
    vectors += [(pair // 256).astype(BF), (pair % 256).astype(BF)]
    pair_at = 128 + PAIR_LANE
    places = (0, 24, 48, 72, 96, 128, 152, 256, pair_at, pair_at + IMG * r)
    thin = sum(jnp.pad(v, (at, 384 - at - v.shape[0])) for v, at in zip(vectors, places)).reshape(3, 128)
    small_rows = -(-(3 + 18 * r) // 16) * 16
    vmem = pl.BlockSpec(memory_space=pltpu.VMEM)
    shape = jax.ShapeDtypeStruct
    mix, res, loss, text_grad, dq, do, df1, df2, dvec = pl.pallas_call(
        functools.partial(layer_kernel, F, r, n),
        out_shape=(
            shape((IMG, SLOTS, D), BF),
            shape((IMG, SLOTS, D), F32),
            shape((1, 1), F32),
            shape((IMG, D), F32),
            shape((QKV_ROWS, D), F32),
            shape((OUT_ROWS, D), F32),
            shape((ROWS, D), F32),
            shape((ROWS, D), F32),
            shape((8, 128), F32),
        ),
        in_specs=[vmem] * 10 + [pl.BlockSpec(memory_space=pltpu.SMEM)],
        out_specs=(vmem,) * 9,
        scratch_shapes=[
            pltpu.VMEM((3, 2, 2, 4, 2, ROWS, D), BF),
            pltpu.VMEM((3, 2, 2, 4, 2, ROWS, D), BF),
            pltpu.VMEM((4, 4, 2, ROWS, D), BF),
            pltpu.VMEM((2, 3, ROWS, D), BF),
            pltpu.VMEM((2, 2, 4, 2, small_rows, 128), BF),
            pltpu.VMEM((TOK, 128), F32),
            pltpu.VMEM((8, 256), F32),
            pltpu.VMEM((-(-IMG * r // 8) * 8, D), F32),
            pltpu.VMEM((2, ROWS, D), F32),
            pltpu.VMEM((TOK, D), BF),
            pltpu.VMEM((18, TOK, 128), BF),
            pltpu.VMEM((6, TOK, 128), BF),
            pltpu.VMEM((2 * IMG * 6, 1, PAD), F32),
            pltpu.VMEM((6, TOK, 128), BF),
            pltpu.VMEM((4, TOK, D), BF),
            pltpu.VMEM((4, TOK, D), BF),
            pltpu.VMEM((TOK, D), BF),
            pltpu.VMEM((max(TOK, IMG * n), D), F32),
            pltpu.VMEM((16, D), F32),
            pltpu.VMEM((16, D), F32),
            pltpu.VMEM((16, D), F32),
            pltpu.VMEM((8, D), F32),
            pltpu.VMEM((IMG * n, 128), F32),
            pltpu.VMEM((2, n // 2, 32, 128), BF),
            pltpu.VMEM((2, 16, 8, 128), F32),
            pltpu.VMEM((16, 8, 128), F32),
            pltpu.VMEM((16, 8, 128), F32),
            pltpu.SemaphoreType.DMA((4, 32)),
            pltpu.SemaphoreType.DMA((4, 32)),
            pltpu.SemaphoreType.DMA((3, 32)),
            pltpu.SemaphoreType.DMA((3, 32)),
            pltpu.SemaphoreType.DMA((16,)),
            pltpu.SemaphoreType.REGULAR((2, 8)),
        ],
        compiler_params=pltpu.CompilerParams(collective_id=0, has_side_effects=True, vmem_limit_bytes=VMEM_LIMIT),
    )(
        gather(w_qkv.T),
        gather(w_out.T),
        gather(w_fc1.T),
        gather(w_fc2),
        thin,
        gather(text_embed),
        images,
        cotangent,
        tissue,
        text_embed,
        logit_scale.reshape(1, 1),
    )
    scatter = functools.partial(postscatter, F=F, r=r)
    vectors = [scatter(dvec[0, 24 * k : 24 * k + 24]) for k in range(5)] + [scatter(dvec[1, :24])]
    return (
        mix,
        res,
        loss.reshape(()),
        text_grad,
        vectors[0],
        vectors[1],
        scatter(dq).T,
        scatter(dvec[1, 24:72]),
        scatter(do).T,
        vectors[2],
        vectors[3],
        vectors[4],
        scatter(df1).T,
        scatter(dvec[2, :96]),
        scatter(df2),
        vectors[5],
    )


def solution(mesh):
    F = mesh.shape["fsdp"]
    n = mesh.shape["dp"] * F
    r = n // GROUPS
    both = ("dp", "fsdp")
    rows, columns = P(both), P(None, both)
    in_specs = (
        rows, rows, rows, rows, P(), rows, rows, columns, rows, columns, rows, rows, rows, columns, rows, rows, rows, rows
    )
    out_specs = (
        rows, rows, P(), rows, rows, rows, columns, rows, columns, rows, rows, rows, columns, rows, rows, rows
    )
    return jax.shard_map(
        functools.partial(per_device, F, r, n), mesh=mesh, in_specs=in_specs, out_specs=out_specs, check_vma=False
    )
```

```python
import functools
import math

import jax
import jax.numpy as jnp
from jax import lax
from jax.experimental import pallas as pl
from jax.experimental.pallas import tpu as pltpu
from jax.sharding import PartitionSpec as P

MESH = pl.DeviceIdType.MESH
MIB = 1024 * 1024
GROUPS = 32
D = 768
HEADS = 12
PAD = 208
IMG = 3
SLOTS = 196
PAIR_LANE = 72
TOK = IMG * PAD
QKV_ROWS, OUT_ROWS = 72, 24
ROWS = 96
VMEM_LIMIT = 63 * MIB
EPS = 1e-6
BF, F32 = jnp.bfloat16, jnp.float32


def dot(a, b):
    return lax.dot_general(a, b, (((1,), (0,)), ((), ())), preferred_element_type=F32)


def dot_nt(a, b):
    return lax.dot_general(a, b, (((1,), (1,)), ((), ())), preferred_element_type=F32)


def dot_exact(a, b, dims):
    return lax.dot_general(a, b, (dims, ((), ())), preferred_element_type=F32, precision=lax.Precision.HIGHEST)


def iota(shape, dim):
    return lax.broadcasted_iota(jnp.int32, shape, dim)


def split(numbers, by):
    quotient = jnp.floor((numbers.astype(F32) + 0.5) * (1.0 / by)).astype(jnp.int32)
    return quotient, numbers - quotient * by


class Pos:
    def __init__(p, F, r, n):
        p.F, p.r, p.n = F, r, n
        p.index = lax.axis_index("dp") * F + lax.axis_index("fsdp")
        p.g, p.rho = lax.div(p.index, r), lax.rem(p.index, r)
        p.c, p.z = lax.rem(p.g, 2), lax.rem(lax.div(p.g, 2), 4)
        p.x, p.y = lax.rem(lax.div(p.g, 8), 2), lax.div(p.g, 16)
        p.l = p.y + p.c * (p.x - p.y)
        p.f = p.x + p.c * (p.y - p.x)
        c, x, y, z = p.c, p.x, p.y, p.z
        p.sib = p.chip(y, x, z, 1 - c)
        p.fn = p.chip(y + c * (1 - 2 * y), x + (1 - c) * (1 - 2 * x), z, c)
        p.ln = p.chip(y + (1 - c) * (1 - 2 * y), x + c * (1 - 2 * x), z, c)
        p.up = p.chip(y, x, jnp.minimum(z + 1, 3), c)
        p.dn = p.chip(y, x, jnp.maximum(z - 1, 0), c)
        p.plane = lax.div(p.g, 2) * r + p.rho

    def device(p, linear):
        return (lax.div(linear, p.F), lax.rem(linear, p.F))

    def chip(p, y, x, z, c):
        return p.device((((y * 2 + x) * 4 + z) * 2 + c) * p.r + p.rho)

    def column(p, zz):
        return p.chip(p.y, p.x, zz, p.c)

    def at_distance(p, h, fn):
        if h == 0:
            fn(p.z)
            return

        @pl.when(p.z + h <= 3)
        def _():
            fn(p.z + h)

        @pl.when(p.z - h >= 0)
        def _():
            fn(p.z - h)

    def for_others(p, fn):
        for h in (1, 2, 3):
            p.at_distance(h, fn)

    def in_plane(p, q):
        return p.device((lax.div(q, p.r) * 2 + p.c) * p.r + lax.rem(q, p.r))

    def block(p, l, z, f):
        y, x = l + p.c * (f - l), f + p.c * (l - f)
        return p.chip(y, x, z, p.c)


def group_of(block):
    c = block // 16 if isinstance(block, int) else jnp.where(block >= 16, 1, 0)
    rest = block - c * 16
    if isinstance(block, int):
        l, z, f = rest // 8, rest // 2 % 4, rest % 2
    else:
        l = jnp.where(rest >= 8, 1, 0)
        zf = rest - 8 * l
        z = jnp.where(zf >= 2, 1, 0) + jnp.where(zf >= 4, 1, 0) + jnp.where(zf >= 6, 1, 0)
        f = zf - 2 * z
    y, x = l + c * (f - l), f + c * (l - f)
    return ((y * 2 + x) * 4 + z) * 2 + c


def enter(p):
    bar = pltpu.get_barrier_semaphore()
    for device in (p.sib, p.fn, p.ln):
        pl.semaphore_signal(bar, inc=1, device_id=device, device_id_type=MESH)
    p.for_others(lambda zz: pl.semaphore_signal(bar, inc=1, device_id=p.column(zz), device_id_type=MESH))
    pl.semaphore_wait(bar, 6)


class Gather:
    def __init__(s, p, held, send, recv, line_first=False):
        s.p, s.held, s.send, s.recv, s.line_first = p, held, send, recv, line_first

    def cp(s, at, ks, kr, dev):
        ref = s.held.at[at]
        return pltpu.make_async_remote_copy(
            src_ref=ref, dst_ref=ref, send_sem=s.send.at[ks], recv_sem=s.recv.at[kr], device_id=dev, device_id_type=MESH
        )

    def first(s):
        p = s.p
        return s.cp((p.c, p.l, p.z, p.f), 0, 0, p.fn)

    def first_in(s):
        p = s.p
        return s.cp((p.c, p.l, p.z, 1 - p.f), 0, 0, p.fn)

    def f_of(s, b):
        return s.p.f + b * (1 - 2 * s.p.f)

    def up(s, zz, b):
        return s.cp((s.p.c, s.p.l, zz, s.f_of(b)), 1 + 2 * zz + b, 1 + 2 * zz + b, s.p.up)

    def dn(s, zz, b):
        return s.cp((s.p.c, s.p.l, zz, s.f_of(b)), 9 + 2 * zz + b, 1 + 2 * zz + b, s.p.dn)

    def cross(s, zz):
        return s.cp((s.p.c, s.p.l, zz, s.p.f), 2 + 2 * zz, 2 + 2 * zz, s.p.fn)

    def cross_in(s, zz):
        return s.cp((s.p.c, s.p.l, zz, 1 - s.p.f), 2 + 2 * zz, 2 + 2 * zz, s.p.fn)

    def last(s, zz):
        return s.cp((s.p.c, s.p.l, zz), 17 + zz, 9 + zz, s.p.ln)

    def last_in(s, zz):
        return s.cp((s.p.c, 1 - s.p.l, zz), 17 + zz, 9 + zz, s.p.ln)

    def core(s, l, zz):
        return s.cp((s.p.c, l, zz), 21 + 4 * l + zz, 13 + 4 * l + zz, s.p.sib)

    def core_in(s, l, zz):
        return s.cp((1 - s.p.c, l, zz), 21 + 4 * l + zz, 13 + 4 * l + zz, s.p.sib)

    def own(s, b):
        p = s.p
        if b:
            s.first_in().wait_recv()
        else:
            s.first().start()
        if not (b and s.line_first):

            @pl.when(p.z < 3)
            def _():
                s.up(p.z, b).start()

            @pl.when(p.z > 0)
            def _():
                s.dn(p.z, b).start()

        if b:
            s.last(p.z).start()
            s.core(p.l, p.z).start()

    def line(s, h, b):
        p = s.p

        def one(zz, copy, onward):
            if b and s.line_first:
                s.cross_in(zz).wait_recv()
            else:
                copy(zz, b).wait_recv()

                @pl.when(onward)
                def _():
                    copy(zz, b).start()

                if s.line_first:
                    s.cross(zz).start()
            if b:
                s.last(zz).start()
                s.core(p.l, zz).start()

        @pl.when(p.z - h >= 0)
        def _():
            one(p.z - h, s.up, p.z < 3)

        @pl.when(p.z + h <= 3)
        def _():
            one(p.z + h, s.dn, p.z > 0)

    def arrive(s, h):
        p = s.p

        def one(zz):
            s.last_in(zz).wait_recv()
            s.core(1 - p.l, zz).start()

        if h == 0:
            one(p.z)
        else:

            @pl.when(p.z - h >= 0)
            def _():
                one(p.z - h)

            @pl.when(p.z + h <= 3)
            def _():
                one(p.z + h)

    def finish(s):
        for zz in range(4):
            for l in range(2):
                s.core_in(l, zz).wait_recv()

    def drain(s):
        p = s.p
        s.first().wait_send()
        for zz in range(4):

            @pl.when((p.z < 3) & (zz <= p.z))
            def _():
                s.up(zz, 0).wait_send()
                if not s.line_first:
                    s.up(zz, 1).wait_send()

            @pl.when((p.z > 0) & (zz >= p.z))
            def _():
                s.dn(zz, 0).wait_send()
                if not s.line_first:
                    s.dn(zz, 1).wait_send()

            if s.line_first:

                @pl.when(zz != p.z)
                def _():
                    s.cross(zz).wait_send()

            s.last(zz).wait_send()
            for l in range(2):
                s.core(l, zz).wait_send()


class Scatter:
    def __init__(s, p, sums, room, landing, send, recv, line_last=False):
        s.p, s.sums, s.room, s.landing, s.send, s.recv, s.line_last = p, sums, room, landing, send, recv, line_last

    def cp(s, src, dst, ks, kr, dev):
        return pltpu.make_async_remote_copy(
            src_ref=src, dst_ref=dst, send_sem=s.send.at[ks], recv_sem=s.recv.at[kr], device_id=dev, device_id_type=MESH
        )

    def core_cp(s, l):
        return s.cp(s.sums.at[1 - s.p.c, l], s.room(l), 1 + l, 1 + l, s.p.sib)

    def side_cp(s, zz):
        return s.cp(s.sums.at[s.p.c, 1 - s.p.l, zz], s.room(2).at[zz], 3 + zz, 3 + zz, s.p.ln)

    def f_of(s, b):
        return 1 - s.p.f if b == 0 else s.p.f

    def here(s, zz, b):
        return s.sums.at[s.p.c, s.p.l, zz, s.f_of(b)]

    def up_far(s, zz, b):
        return s.cp(s.here(zz, b), s.room(3).at[zz, b], 7 + 2 * zz + b, 7 + 2 * zz + b, s.p.up)

    def up_end(s, zz, b):
        return s.cp(s.here(zz, b), s.landing.at[b], 7 + 2 * zz + b, 15 + b, s.p.up)

    def down(s, zz, b):
        return s.cp(s.here(zz, b), s.room(3).at[zz, b], 15 + 2 * zz + b, 7 + 2 * zz + b, s.p.dn)

    def last_cp(s):
        return s.cp(s.here(s.p.z, 0), s.landing.at[2], 0, 0, s.p.fn)

    def cross_cp(s, zz):
        return s.cp(s.here(zz, 0), s.room(3).at[zz, 0], 23 + zz, 17 + zz, s.p.fn)

    def cross_send(s, h):
        s.by_distance(h, lambda zz: s.cross_cp(zz).start())

    def cross_add(s, h):
        def one(zz):
            s.cross_cp(zz).wait_recv()
            s.add(zz, 1, s.room(3).at[zz, 0])
            if h > 0:
                s.straight(zz).start()

        s.by_distance(h, one)

    def core_send(s, l):
        s.core_cp(l).start()

    def core_add(s, l):
        s.core_cp(l).wait_recv()
        room = s.room(l)

        def body(zz, carry):
            for f in range(2):
                ref = s.sums.at[s.p.c, l, zz, f]
                ref[...] = (ref[...].astype(F32) + room[zz, f].astype(F32)).astype(BF)
            return carry

        lax.fori_loop(0, 4, body, 0)

    def add(s, zz, b, ref):
        total = s.here(zz, b)
        total[...] = (total[...].astype(F32) + ref[...].astype(F32)).astype(BF)

    def by_distance(s, h, fn):
        s.p.at_distance(h, fn)

    def side_send(s):
        for h in (3, 2, 1, 0):
            s.by_distance(h, lambda zz: s.side_cp(zz).start())

    def side_add(s, h):
        def one(zz):
            s.side_cp(zz).wait_recv()
            for f in (0, 1):
                total = s.sums.at[s.p.c, s.p.l, zz, f]
                total[...] = (total[...].astype(F32) + s.room(2)[zz, f].astype(F32)).astype(BF)

        s.by_distance(h, one)

    def ends(s, h):
        p = s.p

        @pl.when(p.z == 0)
        def _():
            for b in (0, 1):
                (s.up_end if h == 1 else s.up_far)(p.z + h, b).start()

        @pl.when(p.z == 3)
        def _():
            for b in (0, 1):
                s.down(p.z - h, b).start()

    def inner(s, h, upward):
        p = s.p
        if upward:

            @pl.when((p.z == 1) | (p.z == 2) if h == 1 else p.z == 1)
            def _():
                zz = p.z + h
                for b in (0, 1):
                    s.up_far(zz, b).wait_recv()
                    s.add(zz, b, s.room(3).at[zz, b])
                    (s.up_end if h == 1 else s.up_far)(zz, b).start()

        else:

            @pl.when((p.z == 1) | (p.z == 2) if h == 1 else p.z == 2)
            def _():
                zz = p.z - h
                for b in (0, 1):
                    s.down(zz, b).wait_recv()
                    s.add(zz, b, s.room(3).at[zz, b])
                    s.down(zz, b).start()

    def come(s):
        p = s.p
        for b in (0, 1):

            @pl.when(p.z > 0)
            def _():
                s.up_end(p.z, b).wait_recv()
                s.add(p.z, b, s.landing.at[b])

            @pl.when(p.z < 3)
            def _():
                s.down(p.z, b).wait_recv()
                s.add(p.z, b, s.room(3).at[p.z, b])

            if b == 0:
                s.last_cp().start()

    def straight(s, zz):
        return s.cp(s.here(zz, 1), s.room(3).at[s.p.z, 1], 7 + zz, 7 + s.p.z, s.p.column(zz))

    def straight_in(s, zz):
        return s.cp(s.here(zz, 1), s.room(3).at[zz, 1], 7 + zz, 7 + zz, s.p.column(zz))

    def final(s):
        p = s.p
        if s.line_last:

            def one(zz):
                s.straight_in(zz).wait_recv()
                s.add(p.z, 1, s.room(3).at[zz, 1])

            p.for_others(one)
            return s.here(p.z, 1)[...].astype(F32)
        s.last_cp().wait_recv()
        return s.here(p.z, 1)[...].astype(F32) + s.landing[2].astype(F32)

    def drain(s):
        p = s.p
        for l in range(2):
            s.core_cp(l).wait_send()
        for zz in range(4):
            s.side_cp(zz).wait_send()
            if s.line_last:
                s.cross_cp(zz).wait_send()

                @pl.when(zz != p.z)
                def _():
                    s.straight(zz).wait_send()

            else:

                @pl.when(zz > p.z)
                def _():
                    s.up_far(zz, 0).wait_send()
                    s.up_far(zz, 1).wait_send()

                @pl.when(zz < p.z)
                def _():
                    s.down(zz, 0).wait_send()
                    s.down(zz, 1).wait_send()

        if not s.line_last:
            s.last_cp().wait_send()


def qkv_runs(start, stop):
    runs, row = [], start
    while row < stop:
        chip, inside = divmod(row, 2 * QKV_ROWS)
        z, x, y = chip % 4, chip // 4 % 2, chip // 8
        first = inside < ROWS
        until = min(stop, chip * 2 * QKV_ROWS + (ROWS if first else 2 * QKV_ROWS))
        low = inside if first else inside - ROWS
        at = (0, y, z, x) if first else (1, x, z, y)
        runs.append((at, low, low + until - row))
        row = until
    return runs


def out_runs(start, stop):
    runs, row = [], start
    while row < stop:
        chip, inside = divmod(row, 2 * OUT_ROWS)
        z, x, y = chip % 4, chip // 4 % 2, chip // 8
        until = min(stop, (chip + 1) * 2 * OUT_ROWS)
        low = inside + 2 * (QKV_ROWS - OUT_ROWS) // 2
        runs.append(((1, x, z, y), low, low + until - row))
        row = until
    return runs


def load_runs(ref, runs, lanes=slice(None)):
    return jnp.concatenate([ref[at + (slice(a, b), lanes)] for at, a, b in runs], 0)


def store_runs(ref, runs, value):
    row = 0
    for at, a, b in runs:
        ref[at + (slice(a, b), slice(None))] = value[row : row + b - a]
        row += b - a


def slabs(ref, first, count):
    return jnp.concatenate([ref[first + k] for k in range(count)], 1)


def norm_parts(values):
    centered = values - jnp.mean(values, -1, keepdims=True)
    inverse = lax.rsqrt(jnp.mean(centered * centered, -1, keepdims=True) + EPS)
    return centered * inverse, inverse


def norm_grad(grad, gain, normalized, inverse):
    h = grad * gain
    return (h - jnp.mean(h, -1, keepdims=True) - normalized * jnp.mean(h * normalized, -1, keepdims=True)) * inverse


def gelu_parts(x):
    z = jnp.abs(x) * math.sqrt(0.5)
    under = 1.0 + 0.3275911 * z
    t = pl.reciprocal(under, approx=True)
    t = t * (2.0 - under * t)
    bell = jnp.exp(-0.5 * x * x)
    poly = ((((1.061405429 * t - 1.453152027) * t + 1.421413741) * t - 0.284496736) * t + 0.254829592) * t
    tail = 0.5 * poly * bell
    cdf = jnp.where(x >= 0, 1.0 - tail, tail)
    return x * cdf, cdf + x * bell * (1.0 / math.sqrt(2.0 * math.pi))


CUTS = ((0, 48), (48, 48), (96, 48), (144, SLOTS - 144))


def by_rows(fn):
    def body(i, carry):
        for start, size in CUTS:
            fn((i, slice(start, start + size)), pl.ds(pl.multiple_of(i * PAD + start, 16), size))
        return carry

    lax.fori_loop(0, IMG, body, 0)


def layer_kernel(
    F,
    r,
    n,
    wq_ref,
    wo_ref,
    f1_ref,
    f2_ref,
    thin_ref,
    group_ref,
    img_ref,
    cot_ref,
    tissue_ref,
    text_ref,
    scale_ref,
    mix_ref,
    res_ref,
    loss_ref,
    tg_ref,
    dq_ref,
    do_ref,
    df1_ref,
    df2_ref,
    dvec_ref,
    W,
    G,
    room,
    ends,
    small,
    mask_ref,
    mask_line,
    text_rows,
    swap_grad,
    norm1,
    qkv,
    att,
    lse,
    sec,
    act,
    slope,
    grad2,
    temp,
    vec,
    vec_grad,
    pooled,
    row_grad,
    pair_rows,
    units,
    vec_out,
    vec_core,
    vec_in,
    g_send,
    g_recv,
    s_send,
    s_recv,
    misc,
    credit,
):
    p = Pos(F, r, n)
    half = n // 2
    total = IMG * n
    per_group = IMG * r
    small_rows = small.shape[4]
    qo_g, f1_g, f2_g = (Gather(p, W.at[m], g_send.at[m], g_recv.at[m], m == 0) for m in range(3))
    sm_g = Gather(p, small, g_send.at[3], g_recv.at[3], True)

    def remote(src, dst, k, dev):
        return pltpu.make_async_remote_copy(
            src_ref=src, dst_ref=dst, send_sem=misc.at[2 * k], recv_sem=misc.at[2 * k + 1], device_id=dev, device_id_type=MESH
        )

    first_core = p.c == 0
    q_t, o_t = wq_ref[...].astype(F32), wo_ref[...].astype(F32)

    def empty(rows):
        return jnp.zeros((rows, D), F32)

    gap = QKV_ROWS - OUT_ROWS
    to_zero = (
        jnp.concatenate([q_t, empty(ROWS - QKV_ROWS)], 0),
        jnp.concatenate([empty(QKV_ROWS), q_t[: ROWS - QKV_ROWS]], 0),
    )
    to_one = (
        jnp.concatenate([empty(gap), o_t, empty(OUT_ROWS)], 0),
        jnp.concatenate([q_t[ROWS - QKV_ROWS :], empty(OUT_ROWS), o_t], 0),
    )
    W[0, p.c, p.l, p.z, p.f] = jnp.where(first_core, to_zero[0], to_one[1]).astype(BF)
    G[0, 0, 0, 0, 1] = jnp.where(first_core, to_one[0], to_zero[1]).astype(BF)
    enter(p)
    swap_copy = remote(G.at[0, 0, 0, 0, 1], G.at[0, 0, 0, 0, 0], 0, p.sib)
    swap_copy.start()

    def unit(values):
        inverse = lax.rsqrt(jnp.sum(values * values, -1, keepdims=True) + EPS)
        return values * inverse, inverse

    text_rows[...] = jnp.zeros(text_rows.shape, F32)
    text_rows[0:per_group] = group_ref[...].astype(F32)
    group_units = unit(text_rows[...])[0].astype(BF)
    own_small = jnp.zeros((small_rows, 128), F32)
    for k in range(6):
        shape = (small_rows, group_units.shape[0])
        at = (iota(shape, 0) == iota(shape, 1) + 3 + per_group * k) & (iota(shape, 1) < per_group)
        own_small = own_small + dot(jnp.where(at, 1.0, 0.0).astype(BF), group_units[:, 128 * k : 128 * k + 128])
    at = jnp.where(iota((small_rows, 8), 0) == iota((small_rows, 8), 1), 1.0, 0.0)
    thin = jnp.where(iota((8, 128), 0) < 3, jnp.concatenate([thin_ref[...].astype(F32)] + [jnp.zeros((5, 128), F32)], 0), 0.0)
    small[p.c, p.l, p.z, p.f] = (own_small + dot(at.astype(BF), thin.astype(BF))).astype(BF)
    sm_g.own(0)
    W[1, p.c, p.l, p.z, p.f] = f1_ref[...]
    swap_copy.wait_recv()
    own_block = W.at[0, p.c, p.l, p.z, p.f]
    own_block[...] = (own_block[...].astype(F32) + G[0, 0, 0, 0, 0].astype(F32)).astype(BF)
    qo_g.own(0)
    f1_g.own(0)
    W[2, p.c, p.l, p.z, p.f] = f2_ref[...]
    vec_grad[...] = jnp.zeros(vec_grad.shape, F32)
    mask_line[...] = jnp.zeros(mask_line.shape, F32)
    mask_line[0:IMG, 0:SLOTS] = tissue_ref[...].astype(F32)
    for i in range(IMG):
        tail = slice(i * PAD + SLOTS // 16 * 16, (i + 1) * PAD)
        nothing = jnp.zeros((PAD - SLOTS // 16 * 16, D), BF)
        norm1[tail] = nothing
        grad2[tail] = nothing
        for k in range(6):
            sec[k, tail] = nothing[:, :128]
        line = jnp.broadcast_to(mask_line[i : i + 1], (128, 256))
        mask_ref[i * PAD : i * PAD + PAD] = line.T[:PAD]
    sm_g.own(1)
    qo_g.own(1)
    for h in (1, 2, 3):
        sm_g.line(h, 0)
        qo_g.line(h, 0)
        sm_g.line(h, 1)
        qo_g.line(h, 1)
        sm_g.arrive(h - 1)
        if h == 1:
            f1_g.own(1)
        if h == 2:
            f1_g.line(1, 0)
        if h == 3:
            f1_g.line(1, 1)
            sm_g.arrive(3)
        qo_g.arrive(h - 1)
    qo_g.arrive(3)
    sm_g.finish()


    def picked(k):
        source, target = iota((GROUPS, GROUPS * small_rows), 1), iota((GROUPS, GROUPS * small_rows), 0)
        return dot(jnp.where(source == target * small_rows + k, 1.0, 0.0).astype(BF), small[...].reshape(GROUPS * small_rows, 128)).astype(BF)

    table = [(0, 0, 24, 0), (0, 24, 24, 0), (0, 48, 24, 0), (0, 72, 24, 0), (0, 96, 24, 0), (1, 0, 24, 0), (1, 24, 48, 0), (1, 24, 48, D)]
    table += [(2, 0, 96, D * q) for q in range(4)]

    def spread(k, offset, width, base):
        owner, inside = split(iota((1, D), 1) + base, width)
        names = iota((GROUPS, 1), 0)
        names = names if k == 2 else group_of(names)
        mask = jnp.where(names == owner, 1.0, 0.0)
        places = jnp.where(iota((128, D), 0) == inside + offset, 1.0, 0.0)
        return mask, places

    @pl.when(p.index >= 0)
    def _():
      message_rows = [picked(k) for k in range(3)]
      for row, (k, offset, width, base) in enumerate(table):
        mask, places = spread(k, offset, width, base)
        vec[row : row + 1, :] = jnp.sum(mask * dot(message_rows[k], places.astype(BF)), 0, keepdims=True)

    def first_norm(slots, rows):
        normalized, _ = norm_parts(img_ref[slots].astype(F32))
        norm1[rows] = (normalized * vec[0:1] + vec[1:2]).astype(BF)

    f1_g.arrive(0)
    f1_g.line(2, 0)
    f2_g.own(0)
    by_rows(first_norm)
    qo_g.finish()
    swap_copy.wait_send()

    for j in range(9):
        part = dot_nt(norm1[...], load_runs(W.at[0], qkv_runs(256 * j, 256 * j + 256)))
        if j < 3:
            part = part + vec[6:7, 256 * j : 256 * j + 256]
        elif j >= 6:
            part = part + vec[7:8, 256 * (j - 6) : 256 * (j - 6) + 256]
        part = part.astype(BF)
        qkv[2 * j] = part[:, :128]
        qkv[2 * j + 1] = part[:, 128:]
        if j == 4:
            f1_g.line(2, 1)
            f1_g.arrive(1)
            f2_g.own(1)

    def image_rows(i):
        return pl.ds(pl.multiple_of(i * PAD, 16), PAD)

    low = iota((1, 128), 1) < 64

    def halves(value):
        zero = jnp.zeros_like(value)
        return jnp.where(low, value, zero), jnp.where(low, zero, value)

    def head_pair(i, pair):
        rows = pl.ds(pl.multiple_of(i * PAD, 16), PAD)
        return rows, qkv[pair, rows], qkv[6 + pair, rows], qkv[12 + pair, rows]

    PAIRS = 2

    def attend(it, carry):
        i, first = lax.div(it, 6 // PAIRS), lax.rem(it, 6 // PAIRS) * PAIRS
        bars = jnp.concatenate([jnp.where(mask_ref[image_rows(i)] > 0, 0.0, -1e30)] * 2, 1)[:, :PAD]
        results = []
        for step in range(PAIRS):
            rows, q, k, v = head_pair(i, first + step)
            v_t = v.T
            parts = []
            for h, k_h in enumerate(halves(k * jnp.asarray(0.125, BF))):
                scores = dot_nt(k_h, q) + bars
                top = jnp.max(scores, 0, keepdims=True)
                terms = jnp.exp(scores - top)
                amount = jnp.sum(terms, 0, keepdims=True)
                lse[(i * 6 + first + step) * 2 + h] = top + jnp.log(amount)
                parts.append(dot(v_t[64 * h : 64 * h + 64], terms.astype(BF)) * (1.0 / amount))
            results.append(jnp.concatenate(parts, 0).T.astype(BF))
        for step in range(PAIRS):
            att[first + step, rows] = results[step]
        return carry

    lax.fori_loop(0, 3, attend, 0)
    f1_g.line(3, 0)
    f2_g.line(1, 0)
    f1_g.line(3, 1)
    f1_g.arrive(2)
    lax.fori_loop(3, 5, attend, 0)
    f2_g.line(1, 1)
    f1_g.arrive(3)
    f2_g.arrive(0)
    lax.fori_loop(5, 7, attend, 0)
    f2_g.line(2, 0)
    f2_g.line(2, 1)
    f2_g.arrive(1)
    lax.fori_loop(7, 9, attend, 0)

    attended = slabs(att, 0, 6)
    for j in range(3):
        lanes = slice(256 * j, 256 * j + 256)
        part = dot_nt(attended, load_runs(W.at[0], out_runs(256 * j, 256 * j + 256)))
        for i in range(IMG):
            res_ref[i, :, lanes] = img_ref[i, :, lanes].astype(F32) + part[i * PAD : i * PAD + SLOTS] + vec[2:3, lanes]

    def second_norm(slots, rows):
        normalized, _ = norm_parts(res_ref[slots])
        value = (normalized * vec[3:4] + vec[4:5]).astype(BF)
        for k in range(6):
            sec[k, rows] = value[:, 128 * k : 128 * k + 128]

    by_rows(second_norm)
    f1_g.finish()

    def expand(it, carry):
        q, rows = lax.div(it, IMG), image_rows(lax.rem(it, IMG))
        left = jnp.concatenate([sec[k, rows] for k in range(6)], 1)
        pre = dot_nt(left, W[1, lax.div(q, 2), lax.rem(q, 2)].reshape(D, D)) + vec[pl.ds(8 + q, 1), :]
        value, derivative = gelu_parts(pre)
        act[q, rows] = value.astype(BF)
        slope[q, rows] = derivative.astype(BF)
        return carry

    lax.fori_loop(0, 3, expand, 0)
    f2_g.line(3, 0)
    f2_g.line(3, 1)
    f2_g.arrive(2)
    lax.fori_loop(3, 9, expand, 0)
    f2_g.arrive(3)
    lax.fori_loop(9, 12, expand, 0)
    f2_g.finish()

    def contract(hidden_units, m):
        def body(i, carry):
            rows = image_rows(i)
            for j in range(3):
                lanes = slice(256 * j, 256 * j + 256)
                left = jnp.concatenate([hidden_units[q, rows] for q in range(4)], 1)
                temp[rows, lanes] = dot(left, W[m, :, :, :, :, :, lanes].reshape(4 * D, 256))
            return carry

        lax.fori_loop(0, IMG, body, 0)

    contract(act, 2)

    def wide(column):
        return jnp.concatenate([column] * 6, 1)

    pooled[...] = jnp.zeros(pooled.shape, F32)
    for i in range(IMG):
        sums, count = jnp.zeros((1, D), F32), jnp.zeros((1, 128), F32)
        for start, size in CUTS:
            rows = pl.ds(i * PAD + start, size)
            mask = mask_ref[rows]
            slots = (i, slice(start, start + size))
            outputs = (res_ref[slots] + temp[rows] + vec[5:6]) * wide(mask)
            mix_ref[slots] = outputs.astype(BF)
            sums = sums + jnp.sum(outputs, 0, keepdims=True)
            count = count + jnp.sum(mask, 0, keepdims=True)
        pooled[i : i + 1, :] = sums / wide(count)
        pooled[8 + i : 9 + i, :] = wide(count)

    def unit_grad(grad, values, inverse):
        return inverse * grad - inverse * inverse * inverse * values * jnp.sum(values * grad, -1, keepdims=True)

    own_pooled = pooled[0:8]
    image_unit, image_inverse = unit(own_pooled)
    image_unit = image_unit.astype(BF)
    message = jnp.zeros((32, 128), F32)
    for k in range(6):
        at = jnp.where((iota((32, 8), 0) == iota((32, 8), 1) + IMG * k) & (iota((32, 8), 1) < IMG), 1.0, 0.0).astype(BF)
        message = message + dot(at, image_unit[:, 128 * k : 128 * k + 128])
    units[p.c, p.plane] = message.astype(BF)

    def push(i, carry):
        q = lax.rem(p.plane + i, half)
        remote(units.at[p.c, p.plane], units.at[p.c, p.plane], 1, p.in_plane(q)).start()
        return carry

    lax.fori_loop(1, half, push, 0)
    all_but_own = remote(units.at[p.c, pl.ds(0, half - 1)], units.at[p.c, pl.ds(0, half - 1)], 1, p.sib)

    def gathered(source_chunks, chunk_rows, row_of, tiles, base):
        results = []
        for k in range(tiles):
            value = jnp.zeros((total, 128), F32)
            for number, chunk in source_chunks:
                owner, inside = split(iota((1, chunk_rows), 1), base)
                target = row_of(owner, inside, number, k)
                value = value + dot(jnp.where(iota((total, chunk_rows), 0) == target, 1.0, 0.0).astype(BF), chunk)
            results.append(value)
        return results

    def text_row(owner, inside, number, k):
        at = inside - 3 - per_group * k
        group = group_of(owner + 8 * number)
        return jnp.where((at >= 0) & (at < per_group), group * per_group + at, -1)

    chunks = [(2 * c + l, small[c, l].reshape(8 * small_rows, 128)) for c in range(2) for l in range(2)]
    tiles = gathered(chunks, 8 * small_rows, text_row, 6, small_rows)
    for b in range(r):
        for k in range(6):
            G[1, b // 16, b // 8 % 2, b // 2 % 4, b % 2, :, 128 * k : 128 * k + 128] = tiles[k][ROWS * b : ROWS * b + ROWS].astype(BF)

    def texts():
        return jnp.concatenate([G[1, b // 16, b // 8 % 2, b // 2 % 4, b % 2] for b in range(r)], 0)

    owner, inside = split(iota((total, 1), 0), per_group)
    lines = dot(jnp.where(owner == group_of(iota((1, GROUPS), 1)), 1.0, 0.0).astype(BF), picked(1))
    places = iota((1, 128), 1)
    high = jnp.sum(jnp.where(places == inside + PAIR_LANE, lines, 0.0), 1, keepdims=True)
    rest = jnp.sum(jnp.where(places == inside + PAIR_LANE + per_group, lines, 0.0), 1, keepdims=True)
    pair_rows[...] = jnp.broadcast_to(high * 256.0 + rest, (total, 128))

    all_but_own.wait_recv()
    share = remote(units.at[p.c], units.at[p.c], 2, p.sib)
    share.start()
    remote(units.at[1 - p.c], units.at[1 - p.c], 2, p.sib).wait_recv()

    for k in range(6):

        def add_chunk(number, value, k=k):
            c, at = lax.div(number * 16, half), lax.rem(number * 16, half)
            owner, inside = split(iota((1, 512), 1), 32)
            q = owner + at
            t = inside - IMG * k
            if r == 1:
                linear = 2 * q + c
            else:
                chip, rho = split(q, r)
                linear = (2 * chip + c) * r + rho
            target = jnp.where((t >= 0) & (t < IMG), linear * IMG + t, -1)
            pick = jnp.where(iota((total, 512), 0) == target, 1.0, 0.0).astype(BF)
            return value + dot(pick, units[c, pl.ds(at, 16)].reshape(512, 128))

        value = lax.fori_loop(0, n // 16, add_chunk, jnp.zeros((total, 128), F32)).astype(BF)
        for b in range(r):
            G[2, b // 16, b // 8 % 2, b // 2 % 4, b % 2, :, 128 * k : 128 * k + 128] = value[ROWS * b : ROWS * b + ROWS]

    def block(m, b):
        return G[m, lax.div(b, 16), lax.rem(lax.div(b, 8), 2), lax.rem(lax.div(b, 2), 4), lax.rem(b, 2)]

    scale = scale_ref[0:1, 0:1]
    row = jnp.zeros((1, total), F32)

    def similar(b, col_top):
        rows = pl.ds(pl.multiple_of(b * ROWS, ROWS), ROWS)
        part = dot_nt(block(2, b), texts()) * scale
        temp[rows, :total] = part
        return jnp.maximum(col_top, jnp.max(part, 0, keepdims=True))

    col_top = lax.fori_loop(0, r, similar, row - jnp.inf)

    def by_blocks(fn):
        def body(b, carry):
            rows = pl.ds(pl.multiple_of(b * ROWS, ROWS), ROWS)
            part = temp[rows, :total]
            top = jnp.max(part, 1, keepdims=True)
            row_lse = top + jnp.log(jnp.sum(jnp.exp(part - top), 1, keepdims=True))
            match = jnp.where(iota((ROWS, total), 1) == pair_of(rows), 1.0, 0.0)
            return fn(b, part, row_lse, match, carry)

        return body

    def pair_of(rows):
        return pair_rows[rows][:, 0:1].astype(jnp.int32)

    def sums(b, part, row_lse, match, carry):
        col_sum, loss = carry
        paired = jnp.sum(jnp.sum(part * match, 1, keepdims=True), 0, keepdims=True)
        return col_sum + jnp.sum(jnp.exp(part - col_top), 0, keepdims=True), loss + jnp.sum(row_lse, 0, keepdims=True) - 2.0 * paired

    col_sum, loss = lax.fori_loop(0, r, by_blocks(sums), (row, jnp.zeros((1, 1), F32)))
    col_lse = col_top + jnp.log(col_sum)
    loss = (loss + jnp.sum(col_lse, 1, keepdims=True)) / (2.0 * total)
    loss_ref[...] = jnp.broadcast_to(loss, (8, 128))

    def own_of(places):
        return jnp.where((places == iota(places.shape, 0) + IMG * p.index) & (iota(places.shape, 0) < IMG), 1.0, 0.0).astype(BF)

    own = own_of(iota((8, total), 1))

    def similar_grad(b, part, row_lse, match, carry):
        grad_rows, grad_text = carry
        grad = 0.5 * (jnp.exp(part - row_lse) + jnp.exp(part - col_lse)) - match
        grad = (scale * grad).astype(BF)
        own_rows = own_of(iota((8, ROWS), 1) + b * ROWS)
        return grad_rows + dot(own_rows, grad), grad_text + dot(dot_nt(own, grad).astype(BF), block(2, b))

    grad_rows, grad_text = lax.fori_loop(0, r, by_blocks(similar_grad), (jnp.zeros((8, total), F32), jnp.zeros((8, D), F32)))
    grad_unit = dot(grad_rows.astype(BF), texts())
    row_grad[...] = unit_grad(grad_unit, own_pooled, image_inverse) / jnp.maximum(pooled[8:16], 1.0)
    own_text = text_ref[...].astype(F32)
    _, text_inverse = unit(own_text)
    tg_ref[...] = unit_grad(grad_text[:IMG], own_text, text_inverse)

    sc0, sc1, sc2 = (
        Scatter(p, G.at[m], area, ends.at[1 if m == 1 else 0], s_send.at[m], s_recv.at[m], m == 0)
        for m, area in (
            (0, lambda k: room.at[k]),
            (1, lambda k: W.at[2, k // 2, k % 2] if isinstance(k, int) else W.at[2, 0, k]),
            (2, lambda k: room.at[k]),
        )
    )

    def out_grad(slots, rows):
        return wide(mask_ref[rows]) * (cot_ref[slots].astype(F32) + row_grad[pl.ds(slots[0], 1), :])

    def first_round(slots, rows):
        value = out_grad(slots, rows).astype(BF)
        grad2[rows] = value
        vec_grad[5:6] += jnp.sum(value.astype(F32), 0, keepdims=True)

    by_rows(first_round)
    order = ((1 - p.c, 1 - p.f), (p.c, 1 - p.l), (1 - p.c, p.f), (p.c, p.l))

    def weight_grad(m, at, left, right):
        left = left.T
        for j in range(3):
            lanes = slice(256 * j, 256 * j + 256)
            G[(m,) + at + (slice(None), slice(None), slice(None), lanes)] = (
                dot(left, right[:, lanes]).astype(BF).reshape(4, 2, ROWS, 256)
            )

    for step, at in enumerate(order):
        weight_grad(2, at, act[2 * at[0] + at[1]], grad2[...])
        if step == 0:
            sc2.core_send(1 - p.f)
        if step == 2:
            sc2.core_send(p.f)
    for q in range(4):
        for part in range(2):
            lanes = slice(384 * part, 384 * part + 384)
            value = dot_nt(grad2[...], W[2, q // 2, q % 2, 2 * part : 2 * part + 2].reshape(384, D)) * slope[q, :, lanes].astype(F32)
            value = value.astype(BF)
            slope[q, :, lanes] = value
            vec_grad[8 + q : 9 + q, lanes] = jnp.sum(value.astype(F32), 0, keepdims=True)
        if q == 0:
            sc2.core_add(1 - p.l)
            sc2.side_send()
        if q == 1:
            sc2.core_add(p.l)
    sc2.side_add(3)
    sc2.ends(3)
    f2_g.drain()

    def give(k):
        for at, device in ((0, p.sib), (1, p.ln), (2, p.fn)):
            pl.semaphore_signal(credit.at[k, at], inc=1, device_id=device, device_id_type=MESH)
        p.for_others(lambda zz: pl.semaphore_signal(credit.at[k, 3 + p.z], inc=1, device_id=p.column(zz), device_id_type=MESH))

    def take(k, *which):
        for at in which:
            pl.semaphore_wait(credit.at[k, at], 1)

    def take_column(k):
        p.for_others(lambda zz: pl.semaphore_wait(credit.at[k, 3 + zz], 1))

    give(0)
    for step, at in enumerate(order):
        weight_grad(1, at, slope[2 * at[0] + at[1]], slabs(sec, 0, 6))
        if step == 0:
            take(0, 0)
            sc1.core_send(1 - p.f)
        if step == 2:
            sc1.core_send(p.f)
            sc2.side_add(2)
            sc2.ends(2)
    contract(slope, 1)
    sc1.core_add(1 - p.l)
    take(0, 1)
    sc1.side_send()
    sc1.core_add(p.l)
    sc2.side_add(1)
    sc2.ends(1)
    sc2.side_add(0)

    def second_back(slots, rows):
        grad = temp[rows]
        normalized, inverse = norm_parts(res_ref[slots])
        total_grad = out_grad(slots, rows) + norm_grad(grad, vec[3:4], normalized, inverse)
        res_ref[slots] = total_grad
        rounded = total_grad.astype(BF)
        grad2[rows] = rounded
        vec_grad[3:4] += jnp.sum(grad * normalized, 0, keepdims=True)
        vec_grad[4:5] += jnp.sum(grad, 0, keepdims=True)
        vec_grad[2:3] += jnp.sum(rounded.astype(F32), 0, keepdims=True)

    by_rows(second_back)
    sc2.inner(2, True)
    sc2.inner(2, False)
    attended = slabs(att, 0, 6)
    for j in range(3):
        lanes = slice(256 * j, 256 * j + 256)
        store_runs(G.at[0], out_runs(256 * j, 256 * j + 256), dot(grad2[:, lanes].T, attended).astype(BF))
    for j in range(3):
        lanes = slice(256 * j, 256 * j + 256)
        part = dot(grad2[...], load_runs(W.at[0], out_runs(0, D), lanes)).astype(BF)
        sec[2 * j] = part[:, :128]
        sec[2 * j + 1] = part[:, 128:]

    def attend_back(it, carry):
        i, first = lax.div(it, 6 // PAIRS), lax.rem(it, 6 // PAIRS) * PAIRS
        bars = jnp.concatenate([jnp.where(mask_ref[image_rows(i)] > 0, 0.0, -1e30)] * 2, 1)[:, :PAD]
        results = []
        for step in range(PAIRS):
            rows, plain_q, k, v = head_pair(i, first + step)
            grad_out = sec[first + step, rows]
            q, k = plain_q * jnp.asarray(0.125, BF), k * jnp.asarray(0.125, BF)
            k_t = k.T
            q_halves, out_halves, v_halves = halves(q), halves(grad_out), halves(v)
            grad_v, grad_k, grad_q = 0.0, 0.0, []
            for h, k_h in enumerate(halves(k)):
                scores = dot_nt(k_h, plain_q) + bars
                probs = jnp.exp(scores - lse[(i * 6 + first + step) * 2 + h])
                grad_v = grad_v + dot(probs.astype(BF), out_halves[h])
                grad_probs = dot_nt(v_halves[h], grad_out)
                grad_scores = (probs * (grad_probs - jnp.sum(grad_probs * probs, 0, keepdims=True))).astype(BF)
                grad_k = grad_k + dot(grad_scores, q_halves[h])
                grad_q.append(dot(k_t[64 * h : 64 * h + 64], grad_scores))
            results.append((jnp.concatenate(grad_q, 0).T.astype(BF), grad_k.astype(BF), grad_v.astype(BF)))
        for step in range(PAIRS):
            for which in range(3):
                qkv[6 * which + first + step, rows] = results[step][which]
        return carry

    take(0, 2)
    take_column(0)
    lax.fori_loop(0, 2, attend_back, 0)
    sc1.side_add(3)
    sc1.ends(3)
    lax.fori_loop(2, 4, attend_back, 0)
    sc2.inner(1, True)
    sc2.inner(1, False)
    sc1.side_add(2)
    sc1.ends(2)
    lax.fori_loop(4, 6, attend_back, 0)
    sc1.side_add(1)
    sc1.ends(1)
    sc1.side_add(0)
    lax.fori_loop(6, 9, attend_back, 0)
    sc2.come()
    for j in range(9):
        left = slabs(qkv, 2 * j, 2)
        store_runs(G.at[0], qkv_runs(256 * j, 256 * j + 256), dot(left.T, norm1[...]).astype(BF))
        if j < 3 or j >= 6:
            row, lanes = (6, slice(256 * j, 256 * j + 256)) if j < 3 else (7, slice(256 * (j - 6), 256 * (j - 6) + 256))
            vec_grad[row : row + 1, lanes] = jnp.sum(left.astype(F32), 0, keepdims=True)
    sc1.inner(2, True)
    sc1.inner(2, False)
    df2_ref[...] = sc2.final()
    give(1)
    take(1, 0)
    sc0.core_send(1 - p.f)
    sc0.core_send(p.f)
    sc0.core_add(1 - p.l)
    take(1, 1)
    sc0.side_send()

    def contract_joined(i, carry):
        rows = image_rows(i)
        for j in range(3):
            lanes = slice(256 * j, 256 * j + 256)
            left = jnp.concatenate([qkv[k, rows] for k in range(18)], 1)
            temp[rows, lanes] = dot(left, load_runs(W.at[0], qkv_runs(0, 3 * D), lanes))
        return carry

    lax.fori_loop(0, IMG, contract_joined, 0)
    sc0.core_add(p.l)
    sc1.inner(1, True)
    sc1.inner(1, False)
    take(1, 2)
    take_column(1)

    def first_back(slots, rows):
        grad = temp[rows]
        normalized, inverse = norm_parts(img_ref[slots].astype(F32))
        res_ref[slots] += norm_grad(grad, vec[0:1], normalized, inverse)
        vec_grad[0:1] += jnp.sum(grad * normalized, 0, keepdims=True)
        vec_grad[1:2] += jnp.sum(grad, 0, keepdims=True)

    by_rows(first_back)
    for h in (3, 2):
        sc0.side_add(h)
        sc0.cross_send(h)

    def two_parts(value):
        high = value.astype(BF)
        return jnp.concatenate([high, (value - high.astype(F32)).astype(BF)], 0)

    @pl.when(p.index >= 0)
    def _():
        lines = []
        for k in range(3):
            line = jnp.zeros((2 * GROUPS, 128), F32)
            for row, (kk, offset, width, base) in enumerate(table):
                if kk == k:
                    mask, places = spread(k, offset, width, base)
                    line = line + dot_nt(two_parts(mask * vec_grad[row : row + 1]), places.astype(BF))
            lines.append(line[:GROUPS] + line[GROUPS:])
        shape = (GROUPS * 8, 2 * 3 * GROUPS)
        source, target = iota(shape, 1), iota(shape, 0)
        source = jnp.where(source >= 3 * GROUPS, source - 3 * GROUPS, source)
        k = jnp.where(source >= GROUPS, 1, 0) + jnp.where(source >= 2 * GROUPS, 1, 0)
        at = jnp.where(target == 8 * (source - GROUPS * k) + k, 1.0, 0.0).astype(BF)
        vec_out[...] = dot(at, two_parts(jnp.concatenate(lines, 0))).reshape(2, 16, 8, 128)

    vec_swap = remote(vec_out.at[1 - p.c], vec_core, 3, p.sib)
    vec_swap.start()
    for h in (1, 0):
        sc0.side_add(h)
        sc0.cross_send(h)
    vec_swap.wait_recv()
    vec_out[p.c] += vec_core[...]
    mine = (p.l * 4 + p.z) * 2 + p.f

    def push_vec(i, carry):
        q = lax.rem(mine + i, 16)
        dev = p.block(lax.div(q, 8), lax.rem(lax.div(q, 2), 4), lax.rem(q, 2))
        remote(vec_out.at[p.c, q], vec_in.at[mine], 4, dev).start()
        return carry

    lax.fori_loop(1, 16, push_vec, 0)
    vec_in[mine] = vec_out[p.c, mine]
    sc0.cross_add(3)
    sc1.come()
    for h in (2, 1, 0):
        sc0.cross_add(h)
    df1_ref[...] = sc1.final()
    own_qo = sc0.final()
    swap_grad[0] = own_qo
    qo_back = remote(swap_grad.at[0], swap_grad.at[1], 5, p.sib)
    qo_back.start()
    most = remote(vec_out.at[p.c, pl.ds(0, 15)], vec_in.at[pl.ds(0, 15)], 4, p.sib)
    most.wait_recv()
    dvec_ref[...] = jnp.sum(vec_in[...], 0)
    qo_back.wait_recv()
    other_qo = swap_grad[1]
    dq_ref[...] = jnp.where(
        first_core, own_qo[:QKV_ROWS], jnp.concatenate([other_qo[QKV_ROWS:], own_qo[:gap]], 0)
    )
    do_ref[...] = jnp.where(first_core, other_qo[gap : gap + OUT_ROWS], own_qo[QKV_ROWS:])

    all_but_own.wait_send()
    share.wait_send()
    vec_swap.wait_send()
    most.wait_send()
    qo_back.wait_send()
    for g in (sm_g, qo_g, f1_g):
        g.drain()
    for s in (sc0, sc1, sc2):
        s.drain()


def swap(block, step, size):
    return lax.ppermute(block, "fsdp", [(i, i ^ step) for i in range(size)])


def pregather(block, F, r):
    step = 1
    while step < r:
        high = (lax.axis_index("fsdp") // step) % 2 == 1
        other = swap(block, step, F)
        block = jnp.concatenate([jnp.where(high, other, block), jnp.where(high, block, other)], 0)
        step *= 2
    return block


def postscatter(block, F, r):
    step = r // 2
    while step:
        high = (lax.axis_index("fsdp") // step) % 2 == 1
        lower, upper = jnp.split(block, 2)
        block = jnp.where(high, upper, lower) + swap(jnp.where(high, lower, upper), step, F)
        step //= 2
    return block


def per_device(
    F,
    r,
    n,
    images,
    tissue,
    pair_index,
    text_embed,
    logit_scale,
    ln1_gain,
    ln1_bias,
    w_qkv,
    bias_qv,
    w_out,
    bias_out,
    ln2_gain,
    ln2_bias,
    w_fc1,
    bias_fc1,
    w_fc2,
    bias_fc2,
    cotangent,
):
    gather = functools.partial(pregather, F=F, r=r)

    pair = gather(pair_index)
    vectors = [gather(v) for v in (ln1_gain, ln1_bias, bias_out, ln2_gain, ln2_bias, bias_fc2, bias_qv, bias_fc1)]
    vectors += [(pair // 256).astype(BF), (pair % 256).astype(BF)]
    pair_at = 128 + PAIR_LANE
    places = (0, 24, 48, 72, 96, 128, 152, 256, pair_at, pair_at + IMG * r)
    thin = sum(jnp.pad(v, (at, 384 - at - v.shape[0])) for v, at in zip(vectors, places)).reshape(3, 128)
    small_rows = -(-(3 + 18 * r) // 16) * 16
    vmem = pl.BlockSpec(memory_space=pltpu.VMEM)
    shape = jax.ShapeDtypeStruct
    mix, res, loss, text_grad, dq, do, df1, df2, dvec = pl.pallas_call(
        functools.partial(layer_kernel, F, r, n),
        out_shape=(
            shape((IMG, SLOTS, D), BF),
            shape((IMG, SLOTS, D), F32),
            shape((8, 128), F32),
            shape((IMG, D), F32),
            shape((QKV_ROWS, D), F32),
            shape((OUT_ROWS, D), F32),
            shape((ROWS, D), F32),
            shape((ROWS, D), F32),
            shape((8, 128), F32),
        ),
        in_specs=[vmem] * 11,
        out_specs=(vmem,) * 9,
        scratch_shapes=[
            pltpu.VMEM((3, 2, 2, 4, 2, ROWS, D), BF),
            pltpu.VMEM((3, 2, 2, 4, 2, ROWS, D), BF),
            pltpu.VMEM((4, 4, 2, ROWS, D), BF),
            pltpu.VMEM((2, 3, ROWS, D), BF),
            pltpu.VMEM((2, 2, 4, 2, small_rows, 128), BF),
            pltpu.VMEM((TOK, 128), F32),
            pltpu.VMEM((8, 256), F32),
            pltpu.VMEM((-(-IMG * r // 8) * 8, D), F32),
            pltpu.VMEM((2, ROWS, D), F32),
            pltpu.VMEM((TOK, D), BF),
            pltpu.VMEM((18, TOK, 128), BF),
            pltpu.VMEM((6, TOK, 128), BF),
            pltpu.VMEM((2 * IMG * 6, 1, PAD), F32),
            pltpu.VMEM((6, TOK, 128), BF),
            pltpu.VMEM((4, TOK, D), BF),
            pltpu.VMEM((4, TOK, D), BF),
            pltpu.VMEM((TOK, D), BF),
            pltpu.VMEM((max(TOK, IMG * n), D), F32),
            pltpu.VMEM((16, D), F32),
            pltpu.VMEM((16, D), F32),
            pltpu.VMEM((16, D), F32),
            pltpu.VMEM((8, D), F32),
            pltpu.VMEM((IMG * n, 128), F32),
            pltpu.VMEM((2, n // 2, 32, 128), BF),
            pltpu.VMEM((2, 16, 8, 128), F32),
            pltpu.VMEM((16, 8, 128), F32),
            pltpu.VMEM((16, 8, 128), F32),
            pltpu.SemaphoreType.DMA((4, 32)),
            pltpu.SemaphoreType.DMA((4, 32)),
            pltpu.SemaphoreType.DMA((3, 32)),
            pltpu.SemaphoreType.DMA((3, 32)),
            pltpu.SemaphoreType.DMA((16,)),
            pltpu.SemaphoreType.REGULAR((2, 8)),
        ],
        compiler_params=pltpu.CompilerParams(collective_id=0, has_side_effects=True, vmem_limit_bytes=VMEM_LIMIT),
    )(
        gather(w_qkv.T),
        gather(w_out.T),
        gather(w_fc1.T),
        gather(w_fc2),
        thin,
        gather(text_embed),
        images,
        cotangent,
        tissue,
        text_embed,
        jnp.broadcast_to(logit_scale.reshape(1, 1), (8, 128)),
    )
    scatter = functools.partial(postscatter, F=F, r=r)
    vectors = [scatter(dvec[0, 24 * k : 24 * k + 24]) for k in range(5)] + [scatter(dvec[1, :24])]
    return (
        mix,
        res,
        loss[0, 0],
        text_grad,
        vectors[0],
        vectors[1],
        scatter(dq).T,
        scatter(dvec[1, 24:72]),
        scatter(do).T,
        vectors[2],
        vectors[3],
        vectors[4],
        scatter(df1).T,
        scatter(dvec[2, :96]),
        scatter(df2),
        vectors[5],
    )


def solution(mesh):
    F = mesh.shape["fsdp"]
    n = mesh.shape["dp"] * F
    r = n // GROUPS
    both = ("dp", "fsdp")
    rows, columns = P(both), P(None, both)
    in_specs = (
        rows, rows, rows, rows, P(), rows, rows, columns, rows, columns, rows, rows, rows, columns, rows, rows, rows, rows
    )
    out_specs = (
        rows, rows, P(), rows, rows, rows, columns, rows, columns, rows, rows, rows, columns, rows, rows, rows
    )
    return jax.shard_map(
        functools.partial(per_device, F, r, n), mesh=mesh, in_specs=in_specs, out_specs=out_specs, check_vma=False
    )
```

```python
import functools
import math

import jax
import jax.numpy as jnp
from jax import lax
from jax.experimental import pallas as pl
from jax.experimental.pallas import tpu as pltpu
from jax.sharding import PartitionSpec as P

MESH = pl.DeviceIdType.MESH
MIB = 1024 * 1024
GROUPS = 32
D = 768
HEADS = 12
PAD = 208
IMG = 3
SLOTS = 196
PAIR_LANE = 72
TOK = IMG * PAD
QKV_ROWS, OUT_ROWS = 72, 24
ROWS = 96
VMEM_LIMIT = 63 * MIB
EPS = 1e-6
BF, F32 = jnp.bfloat16, jnp.float32


def dot(a, b):
    return lax.dot_general(a, b, (((1,), (0,)), ((), ())), preferred_element_type=F32)


def dot_nt(a, b):
    return lax.dot_general(a, b, (((1,), (1,)), ((), ())), preferred_element_type=F32)


def dot_exact(a, b, dims):
    return lax.dot_general(a, b, (dims, ((), ())), preferred_element_type=F32, precision=lax.Precision.HIGHEST)


def iota(shape, dim):
    return lax.broadcasted_iota(jnp.int32, shape, dim)


def split(numbers, by):
    quotient = jnp.floor((numbers.astype(F32) + 0.5) * (1.0 / by)).astype(jnp.int32)
    return quotient, numbers - quotient * by


class Pos:
    def __init__(p, F, r, n):
        p.F, p.r, p.n = F, r, n
        p.index = lax.axis_index("dp") * F + lax.axis_index("fsdp")
        p.g, p.rho = lax.div(p.index, r), lax.rem(p.index, r)
        p.c, p.z = lax.rem(p.g, 2), lax.rem(lax.div(p.g, 2), 4)
        p.x, p.y = lax.rem(lax.div(p.g, 8), 2), lax.div(p.g, 16)
        p.l = p.y + p.c * (p.x - p.y)
        p.f = p.x + p.c * (p.y - p.x)
        c, x, y, z = p.c, p.x, p.y, p.z
        p.sib = p.chip(y, x, z, 1 - c)
        p.fn = p.chip(y + c * (1 - 2 * y), x + (1 - c) * (1 - 2 * x), z, c)
        p.ln = p.chip(y + (1 - c) * (1 - 2 * y), x + c * (1 - 2 * x), z, c)
        p.up = p.chip(y, x, jnp.minimum(z + 1, 3), c)
        p.dn = p.chip(y, x, jnp.maximum(z - 1, 0), c)
        p.plane = lax.div(p.g, 2) * r + p.rho

    def device(p, linear):
        return (lax.div(linear, p.F), lax.rem(linear, p.F))

    def chip(p, y, x, z, c):
        return p.device((((y * 2 + x) * 4 + z) * 2 + c) * p.r + p.rho)

    def column(p, zz):
        return p.chip(p.y, p.x, zz, p.c)

    def at_distance(p, h, fn):
        if h == 0:
            fn(p.z)
            return

        @pl.when(p.z + h <= 3)
        def _():
            fn(p.z + h)

        @pl.when(p.z - h >= 0)
        def _():
            fn(p.z - h)

    def for_others(p, fn):
        for h in (1, 2, 3):
            p.at_distance(h, fn)

    def in_plane(p, q):
        return p.device((lax.div(q, p.r) * 2 + p.c) * p.r + lax.rem(q, p.r))

    def block(p, l, z, f):
        y, x = l + p.c * (f - l), f + p.c * (l - f)
        return p.chip(y, x, z, p.c)


def group_of(block):
    c = block // 16 if isinstance(block, int) else jnp.where(block >= 16, 1, 0)
    rest = block - c * 16
    if isinstance(block, int):
        l, z, f = rest // 8, rest // 2 % 4, rest % 2
    else:
        l = jnp.where(rest >= 8, 1, 0)
        zf = rest - 8 * l
        z = jnp.where(zf >= 2, 1, 0) + jnp.where(zf >= 4, 1, 0) + jnp.where(zf >= 6, 1, 0)
        f = zf - 2 * z
    y, x = l + c * (f - l), f + c * (l - f)
    return ((y * 2 + x) * 4 + z) * 2 + c


def enter(p):
    bar = pltpu.get_barrier_semaphore()
    for device in (p.sib, p.fn, p.ln):
        pl.semaphore_signal(bar, inc=1, device_id=device, device_id_type=MESH)
    p.for_others(lambda zz: pl.semaphore_signal(bar, inc=1, device_id=p.column(zz), device_id_type=MESH))
    pl.semaphore_wait(bar, 6)


class Gather:
    def __init__(s, p, held, send, recv, line_first=False):
        s.p, s.held, s.send, s.recv, s.line_first = p, held, send, recv, line_first

    def cp(s, at, ks, kr, dev):
        ref = s.held.at[at]
        return pltpu.make_async_remote_copy(
            src_ref=ref, dst_ref=ref, send_sem=s.send.at[ks], recv_sem=s.recv.at[kr], device_id=dev, device_id_type=MESH
        )

    def first(s):
        p = s.p
        return s.cp((p.c, p.l, p.z, p.f), 0, 0, p.fn)

    def first_in(s):
        p = s.p
        return s.cp((p.c, p.l, p.z, 1 - p.f), 0, 0, p.fn)

    def f_of(s, b):
        return s.p.f + b * (1 - 2 * s.p.f)

    def up(s, zz, b):
        return s.cp((s.p.c, s.p.l, zz, s.f_of(b)), 1 + 2 * zz + b, 1 + 2 * zz + b, s.p.up)

    def dn(s, zz, b):
        return s.cp((s.p.c, s.p.l, zz, s.f_of(b)), 9 + 2 * zz + b, 1 + 2 * zz + b, s.p.dn)

    def cross(s, zz):
        return s.cp((s.p.c, s.p.l, zz, s.p.f), 2 + 2 * zz, 2 + 2 * zz, s.p.fn)

    def cross_in(s, zz):
        return s.cp((s.p.c, s.p.l, zz, 1 - s.p.f), 2 + 2 * zz, 2 + 2 * zz, s.p.fn)

    def last(s, zz):
        return s.cp((s.p.c, s.p.l, zz), 17 + zz, 9 + zz, s.p.ln)

    def last_in(s, zz):
        return s.cp((s.p.c, 1 - s.p.l, zz), 17 + zz, 9 + zz, s.p.ln)

    def core(s, l, zz):
        return s.cp((s.p.c, l, zz), 21 + 4 * l + zz, 13 + 4 * l + zz, s.p.sib)

    def core_in(s, l, zz):
        return s.cp((1 - s.p.c, l, zz), 21 + 4 * l + zz, 13 + 4 * l + zz, s.p.sib)

    def own(s, b):
        p = s.p
        if b:
            s.first_in().wait_recv()
        else:
            s.first().start()
        if not (b and s.line_first):

            @pl.when(p.z < 3)
            def _():
                s.up(p.z, b).start()

            @pl.when(p.z > 0)
            def _():
                s.dn(p.z, b).start()

        if b:
            s.last(p.z).start()
            s.core(p.l, p.z).start()

    def line(s, h, b):
        p = s.p

        def one(zz, copy, onward):
            if b and s.line_first:
                s.cross_in(zz).wait_recv()
            else:
                copy(zz, b).wait_recv()

                @pl.when(onward)
                def _():
                    copy(zz, b).start()

                if s.line_first:
                    s.cross(zz).start()
            if b:
                s.last(zz).start()
                s.core(p.l, zz).start()

        @pl.when(p.z - h >= 0)
        def _():
            one(p.z - h, s.up, p.z < 3)

        @pl.when(p.z + h <= 3)
        def _():
            one(p.z + h, s.dn, p.z > 0)

    def arrive(s, h):
        p = s.p

        def one(zz):
            s.last_in(zz).wait_recv()
            s.core(1 - p.l, zz).start()

        if h == 0:
            one(p.z)
        else:

            @pl.when(p.z - h >= 0)
            def _():
                one(p.z - h)

            @pl.when(p.z + h <= 3)
            def _():
                one(p.z + h)

    def finish(s):
        for zz in range(4):
            for l in range(2):
                s.core_in(l, zz).wait_recv()

    def drain(s):
        p = s.p
        s.first().wait_send()
        for zz in range(4):

            @pl.when((p.z < 3) & (zz <= p.z))
            def _():
                s.up(zz, 0).wait_send()
                if not s.line_first:
                    s.up(zz, 1).wait_send()

            @pl.when((p.z > 0) & (zz >= p.z))
            def _():
                s.dn(zz, 0).wait_send()
                if not s.line_first:
                    s.dn(zz, 1).wait_send()

            if s.line_first:

                @pl.when(zz != p.z)
                def _():
                    s.cross(zz).wait_send()

            s.last(zz).wait_send()
            for l in range(2):
                s.core(l, zz).wait_send()


class Scatter:
    def __init__(s, p, sums, room, landing, send, recv, line_last=False):
        s.p, s.sums, s.room, s.landing, s.send, s.recv, s.line_last = p, sums, room, landing, send, recv, line_last

    def cp(s, src, dst, ks, kr, dev):
        return pltpu.make_async_remote_copy(
            src_ref=src, dst_ref=dst, send_sem=s.send.at[ks], recv_sem=s.recv.at[kr], device_id=dev, device_id_type=MESH
        )

    def core_cp(s, l):
        return s.cp(s.sums.at[1 - s.p.c, l], s.room(l), 1 + l, 1 + l, s.p.sib)

    def side_cp(s, zz):
        return s.cp(s.sums.at[s.p.c, 1 - s.p.l, zz], s.room(2).at[zz], 3 + zz, 3 + zz, s.p.ln)

    def f_of(s, b):
        return 1 - s.p.f if b == 0 else s.p.f

    def here(s, zz, b):
        return s.sums.at[s.p.c, s.p.l, zz, s.f_of(b)]

    def up_far(s, zz, b):
        return s.cp(s.here(zz, b), s.room(3).at[zz, b], 7 + 2 * zz + b, 7 + 2 * zz + b, s.p.up)

    def up_end(s, zz, b):
        return s.cp(s.here(zz, b), s.landing.at[b], 7 + 2 * zz + b, 15 + b, s.p.up)

    def down(s, zz, b):
        return s.cp(s.here(zz, b), s.room(3).at[zz, b], 15 + 2 * zz + b, 7 + 2 * zz + b, s.p.dn)

    def last_cp(s):
        return s.cp(s.here(s.p.z, 0), s.landing.at[2], 0, 0, s.p.fn)

    def cross_cp(s, zz):
        return s.cp(s.here(zz, 0), s.room(3).at[zz, 0], 23 + zz, 17 + zz, s.p.fn)

    def cross_send(s, h):
        s.by_distance(h, lambda zz: s.cross_cp(zz).start())

    def cross_add(s, h):
        def one(zz):
            s.cross_cp(zz).wait_recv()
            s.add(zz, 1, s.room(3).at[zz, 0])
            if h > 0:
                s.straight(zz).start()

        s.by_distance(h, one)

    def core_send(s, l):
        s.core_cp(l).start()

    def core_add(s, l):
        s.core_cp(l).wait_recv()
        room = s.room(l)

        def body(zz, carry):
            for f in range(2):
                ref = s.sums.at[s.p.c, l, zz, f]
                ref[...] = (ref[...].astype(F32) + room[zz, f].astype(F32)).astype(BF)
            return carry

        lax.fori_loop(0, 4, body, 0)

    def add(s, zz, b, ref):
        total = s.here(zz, b)
        total[...] = (total[...].astype(F32) + ref[...].astype(F32)).astype(BF)

    def by_distance(s, h, fn):
        s.p.at_distance(h, fn)

    def side_send(s):
        for h in (3, 2, 1, 0):
            s.by_distance(h, lambda zz: s.side_cp(zz).start())

    def side_add(s, h):
        def one(zz):
            s.side_cp(zz).wait_recv()
            for f in (0, 1):
                total = s.sums.at[s.p.c, s.p.l, zz, f]
                total[...] = (total[...].astype(F32) + s.room(2)[zz, f].astype(F32)).astype(BF)

        s.by_distance(h, one)

    def ends(s, h):
        p = s.p

        @pl.when(p.z == 0)
        def _():
            for b in (0, 1):
                (s.up_end if h == 1 else s.up_far)(p.z + h, b).start()

        @pl.when(p.z == 3)
        def _():
            for b in (0, 1):
                s.down(p.z - h, b).start()

    def inner(s, h, upward):
        p = s.p
        if upward:

            @pl.when((p.z == 1) | (p.z == 2) if h == 1 else p.z == 1)
            def _():
                zz = p.z + h
                for b in (0, 1):
                    s.up_far(zz, b).wait_recv()
                    s.add(zz, b, s.room(3).at[zz, b])
                    (s.up_end if h == 1 else s.up_far)(zz, b).start()

        else:

            @pl.when((p.z == 1) | (p.z == 2) if h == 1 else p.z == 2)
            def _():
                zz = p.z - h
                for b in (0, 1):
                    s.down(zz, b).wait_recv()
                    s.add(zz, b, s.room(3).at[zz, b])
                    s.down(zz, b).start()

    def come(s):
        p = s.p
        for b in (0, 1):

            @pl.when(p.z > 0)
            def _():
                s.up_end(p.z, b).wait_recv()
                s.add(p.z, b, s.landing.at[b])

            @pl.when(p.z < 3)
            def _():
                s.down(p.z, b).wait_recv()
                s.add(p.z, b, s.room(3).at[p.z, b])

            if b == 0:
                s.last_cp().start()

    def straight(s, zz):
        return s.cp(s.here(zz, 1), s.room(3).at[s.p.z, 1], 7 + zz, 7 + s.p.z, s.p.column(zz))

    def straight_in(s, zz):
        return s.cp(s.here(zz, 1), s.room(3).at[zz, 1], 7 + zz, 7 + zz, s.p.column(zz))

    def final(s):
        p = s.p
        if s.line_last:

            def one(zz):
                s.straight_in(zz).wait_recv()
                s.add(p.z, 1, s.room(3).at[zz, 1])

            p.for_others(one)
            return s.here(p.z, 1)[...].astype(F32)
        s.last_cp().wait_recv()
        return s.here(p.z, 1)[...].astype(F32) + s.landing[2].astype(F32)

    def drain(s):
        p = s.p
        for l in range(2):
            s.core_cp(l).wait_send()
        for zz in range(4):
            s.side_cp(zz).wait_send()
            if s.line_last:
                s.cross_cp(zz).wait_send()

                @pl.when(zz != p.z)
                def _():
                    s.straight(zz).wait_send()

            else:

                @pl.when(zz > p.z)
                def _():
                    s.up_far(zz, 0).wait_send()
                    s.up_far(zz, 1).wait_send()

                @pl.when(zz < p.z)
                def _():
                    s.down(zz, 0).wait_send()
                    s.down(zz, 1).wait_send()

        if not s.line_last:
            s.last_cp().wait_send()


def qkv_runs(start, stop):
    runs, row = [], start
    while row < stop:
        chip, inside = divmod(row, 2 * QKV_ROWS)
        z, x, y = chip % 4, chip // 4 % 2, chip // 8
        first = inside < ROWS
        until = min(stop, chip * 2 * QKV_ROWS + (ROWS if first else 2 * QKV_ROWS))
        low = inside if first else inside - ROWS
        at = (0, y, z, x) if first else (1, x, z, y)
        runs.append((at, low, low + until - row))
        row = until
    return runs


def out_runs(start, stop):
    runs, row = [], start
    while row < stop:
        chip, inside = divmod(row, 2 * OUT_ROWS)
        z, x, y = chip % 4, chip // 4 % 2, chip // 8
        until = min(stop, (chip + 1) * 2 * OUT_ROWS)
        low = inside + 2 * (QKV_ROWS - OUT_ROWS) // 2
        runs.append(((1, x, z, y), low, low + until - row))
        row = until
    return runs


def load_runs(ref, runs, lanes=slice(None)):
    return jnp.concatenate([ref[at + (slice(a, b), lanes)] for at, a, b in runs], 0)


def store_runs(ref, runs, value):
    row = 0
    for at, a, b in runs:
        ref[at + (slice(a, b), slice(None))] = value[row : row + b - a]
        row += b - a


def slabs(ref, first, count):
    return jnp.concatenate([ref[first + k] for k in range(count)], 1)


def norm_parts(values):
    centered = values - jnp.mean(values, -1, keepdims=True)
    inverse = lax.rsqrt(jnp.mean(centered * centered, -1, keepdims=True) + EPS)
    return centered * inverse, inverse


def norm_grad(grad, gain, normalized, inverse):
    h = grad * gain
    return (h - jnp.mean(h, -1, keepdims=True) - normalized * jnp.mean(h * normalized, -1, keepdims=True)) * inverse


def gelu_parts(x):
    z = jnp.abs(x) * math.sqrt(0.5)
    under = 1.0 + 0.3275911 * z
    t = pl.reciprocal(under, approx=True)
    t = t * (2.0 - under * t)
    bell = jnp.exp(-0.5 * x * x)
    poly = ((((1.061405429 * t - 1.453152027) * t + 1.421413741) * t - 0.284496736) * t + 0.254829592) * t
    tail = 0.5 * poly * bell
    cdf = jnp.where(x >= 0, 1.0 - tail, tail)
    return x * cdf, cdf + x * bell * (1.0 / math.sqrt(2.0 * math.pi))


CUTS = ((0, 48), (48, 48), (96, 48), (144, SLOTS - 144))


def by_rows(fn):
    def body(i, carry):
        for start, size in CUTS:
            fn((i, slice(start, start + size)), pl.ds(pl.multiple_of(i * PAD + start, 16), size))
        return carry

    lax.fori_loop(0, IMG, body, 0)


def layer_kernel(
    F,
    r,
    n,
    wq_ref,
    wo_ref,
    f1_ref,
    f2_ref,
    thin_ref,
    group_ref,
    img_ref,
    cot_ref,
    tissue_ref,
    text_ref,
    scale_ref,
    mix_ref,
    res_ref,
    loss_ref,
    tg_ref,
    dq_ref,
    do_ref,
    df1_ref,
    df2_ref,
    dvec_ref,
    W,
    G,
    room,
    ends,
    small,
    mask_ref,
    mask_line,
    text_rows,
    swap_grad,
    norm1,
    qkv,
    att,
    lse,
    sec,
    act,
    slope,
    grad2,
    temp,
    vec,
    vec_grad,
    pooled,
    row_grad,
    pair_rows,
    units,
    vec_out,
    vec_core,
    vec_in,
    g_send,
    g_recv,
    s_send,
    s_recv,
    misc,
    credit,
):
    p = Pos(F, r, n)
    half = n // 2
    total = IMG * n
    per_group = IMG * r
    small_rows = small.shape[4]
    qo_g, f1_g, f2_g = (Gather(p, W.at[m], g_send.at[m], g_recv.at[m], m == 0) for m in range(3))
    sm_g = Gather(p, small, g_send.at[3], g_recv.at[3], True)

    def remote(src, dst, k, dev):
        return pltpu.make_async_remote_copy(
            src_ref=src, dst_ref=dst, send_sem=misc.at[2 * k], recv_sem=misc.at[2 * k + 1], device_id=dev, device_id_type=MESH
        )

    first_core = p.c == 0
    q_t, o_t = wq_ref[...].astype(F32), wo_ref[...].astype(F32)

    def empty(rows):
        return jnp.zeros((rows, D), F32)

    gap = QKV_ROWS - OUT_ROWS
    to_zero = (
        jnp.concatenate([q_t, empty(ROWS - QKV_ROWS)], 0),
        jnp.concatenate([empty(QKV_ROWS), q_t[: ROWS - QKV_ROWS]], 0),
    )
    to_one = (
        jnp.concatenate([empty(gap), o_t, empty(OUT_ROWS)], 0),
        jnp.concatenate([q_t[ROWS - QKV_ROWS :], empty(OUT_ROWS), o_t], 0),
    )
    W[0, p.c, p.l, p.z, p.f] = jnp.where(first_core, to_zero[0], to_one[1]).astype(BF)
    G[0, 0, 0, 0, 1] = jnp.where(first_core, to_one[0], to_zero[1]).astype(BF)
    enter(p)
    swap_copy = remote(G.at[0, 0, 0, 0, 1], G.at[0, 0, 0, 0, 0], 0, p.sib)
    swap_copy.start()

    def unit(values):
        inverse = lax.rsqrt(jnp.sum(values * values, -1, keepdims=True) + EPS)
        return values * inverse, inverse

    text_rows[...] = jnp.zeros(text_rows.shape, F32)
    text_rows[0:per_group] = group_ref[...].astype(F32)
    group_units = unit(text_rows[...])[0].astype(BF)
    own_small = jnp.zeros((small_rows, 128), F32)
    for k in range(6):
        shape = (small_rows, group_units.shape[0])
        at = (iota(shape, 0) == iota(shape, 1) + 3 + per_group * k) & (iota(shape, 1) < per_group)
        own_small = own_small + dot(jnp.where(at, 1.0, 0.0).astype(BF), group_units[:, 128 * k : 128 * k + 128])
    at = jnp.where(iota((small_rows, 8), 0) == iota((small_rows, 8), 1), 1.0, 0.0)
    thin = jnp.where(iota((8, 128), 0) < 3, jnp.concatenate([thin_ref[...].astype(F32)] + [jnp.zeros((5, 128), F32)], 0), 0.0)
    small[p.c, p.l, p.z, p.f] = (own_small + dot(at.astype(BF), thin.astype(BF))).astype(BF)
    sm_g.own(0)
    W[1, p.c, p.l, p.z, p.f] = f1_ref[...]
    swap_copy.wait_recv()
    own_block = W.at[0, p.c, p.l, p.z, p.f]
    own_block[...] = (own_block[...].astype(F32) + G[0, 0, 0, 0, 0].astype(F32)).astype(BF)
    qo_g.own(0)
    f1_g.own(0)
    W[2, p.c, p.l, p.z, p.f] = f2_ref[...]
    vec_grad[...] = jnp.zeros(vec_grad.shape, F32)
    mask_line[...] = jnp.zeros(mask_line.shape, F32)
    mask_line[0:IMG, 0:SLOTS] = tissue_ref[...].astype(F32)
    for i in range(IMG):
        tail = slice(i * PAD + SLOTS // 16 * 16, (i + 1) * PAD)
        nothing = jnp.zeros((PAD - SLOTS // 16 * 16, D), BF)
        norm1[tail] = nothing
        grad2[tail] = nothing
        for k in range(6):
            sec[k, tail] = nothing[:, :128]
        line = jnp.broadcast_to(mask_line[i : i + 1], (128, 256))
        mask_ref[i * PAD : i * PAD + PAD] = line.T[:PAD]
    sm_g.own(1)
    qo_g.own(1)
    for h in (1, 2, 3):
        sm_g.line(h, 0)
        qo_g.line(h, 0)
        sm_g.line(h, 1)
        qo_g.line(h, 1)
        sm_g.arrive(h - 1)
        if h == 1:
            f1_g.own(1)
        if h == 2:
            f1_g.line(1, 0)
        if h == 3:
            f1_g.line(1, 1)
            sm_g.arrive(3)
        qo_g.arrive(h - 1)
    qo_g.arrive(3)
    sm_g.finish()


    def picked(k):
        source, target = iota((GROUPS, GROUPS * small_rows), 1), iota((GROUPS, GROUPS * small_rows), 0)
        return dot(jnp.where(source == target * small_rows + k, 1.0, 0.0).astype(BF), small[...].reshape(GROUPS * small_rows, 128)).astype(BF)

    table = [(0, 0, 24, 0), (0, 24, 24, 0), (0, 48, 24, 0), (0, 72, 24, 0), (0, 96, 24, 0), (1, 0, 24, 0), (1, 24, 48, 0), (1, 24, 48, D)]
    table += [(2, 0, 96, D * q) for q in range(4)]

    def spread(k, offset, width, base):
        owner, inside = split(iota((1, D), 1) + base, width)
        names = iota((GROUPS, 1), 0)
        names = names if k == 2 else group_of(names)
        mask = jnp.where(names == owner, 1.0, 0.0)
        places = jnp.where(iota((128, D), 0) == inside + offset, 1.0, 0.0)
        return mask, places

    @pl.when(p.index >= 0)
    def _():
      message_rows = [picked(k) for k in range(3)]
      for row, (k, offset, width, base) in enumerate(table):
        mask, places = spread(k, offset, width, base)
        vec[row : row + 1, :] = jnp.sum(mask * dot(message_rows[k], places.astype(BF)), 0, keepdims=True)

    def first_norm(slots, rows):
        normalized, _ = norm_parts(img_ref[slots].astype(F32))
        norm1[rows] = (normalized * vec[0:1] + vec[1:2]).astype(BF)

    f1_g.arrive(0)
    f1_g.line(2, 0)
    f2_g.own(0)
    by_rows(first_norm)
    qo_g.finish()
    swap_copy.wait_send()

    for j in range(9):
        part = dot_nt(norm1[...], load_runs(W.at[0], qkv_runs(256 * j, 256 * j + 256)))
        if j < 3:
            part = part + vec[6:7, 256 * j : 256 * j + 256]
        elif j >= 6:
            part = part + vec[7:8, 256 * (j - 6) : 256 * (j - 6) + 256]
        part = part.astype(BF)
        qkv[2 * j] = part[:, :128]
        qkv[2 * j + 1] = part[:, 128:]
        if j == 4:
            f1_g.line(2, 1)
            f1_g.arrive(1)
            f2_g.own(1)

    def image_rows(i):
        return pl.ds(pl.multiple_of(i * PAD, 16), PAD)

    low = iota((1, 128), 1) < 64

    def halves(value):
        zero = jnp.zeros_like(value)
        return jnp.where(low, value, zero), jnp.where(low, zero, value)

    def head_pair(i, pair):
        rows = pl.ds(pl.multiple_of(i * PAD, 16), PAD)
        return rows, qkv[pair, rows], qkv[6 + pair, rows], qkv[12 + pair, rows]

    PAIRS = 2

    def attend(it, carry):
        i, first = lax.div(it, 6 // PAIRS), lax.rem(it, 6 // PAIRS) * PAIRS
        bars = jnp.concatenate([jnp.where(mask_ref[image_rows(i)] > 0, 0.0, -1e30)] * 2, 1)[:, :PAD]
        results = []
        for step in range(PAIRS):
            rows, q, k, v = head_pair(i, first + step)
            v_t = v.T
            parts = []
            for h, k_h in enumerate(halves(k * jnp.asarray(0.125, BF))):
                scores = dot_nt(k_h, q) + bars
                top = jnp.max(scores, 0, keepdims=True)
                terms = jnp.exp(scores - top)
                amount = jnp.sum(terms, 0, keepdims=True)
                lse[(i * 6 + first + step) * 2 + h] = top + jnp.log(amount)
                parts.append(dot(v_t[64 * h : 64 * h + 64], terms.astype(BF)) * (1.0 / amount))
            results.append(jnp.concatenate(parts, 0).T.astype(BF))
        for step in range(PAIRS):
            att[first + step, rows] = results[step]
        return carry

    lax.fori_loop(0, 3, attend, 0)
    f1_g.line(3, 0)
    f2_g.line(1, 0)
    f1_g.line(3, 1)
    f1_g.arrive(2)
    lax.fori_loop(3, 5, attend, 0)
    f2_g.line(1, 1)
    f1_g.arrive(3)
    f2_g.arrive(0)
    lax.fori_loop(5, 7, attend, 0)
    f2_g.line(2, 0)
    f2_g.line(2, 1)
    f2_g.arrive(1)
    lax.fori_loop(7, 9, attend, 0)

    attended = slabs(att, 0, 6)
    for j in range(3):
        lanes = slice(256 * j, 256 * j + 256)
        part = dot_nt(attended, load_runs(W.at[0], out_runs(256 * j, 256 * j + 256)))
        for i in range(IMG):
            res_ref[i, :, lanes] = img_ref[i, :, lanes].astype(F32) + part[i * PAD : i * PAD + SLOTS] + vec[2:3, lanes]

    def second_norm(slots, rows):
        normalized, _ = norm_parts(res_ref[slots])
        value = (normalized * vec[3:4] + vec[4:5]).astype(BF)
        for k in range(6):
            sec[k, rows] = value[:, 128 * k : 128 * k + 128]

    by_rows(second_norm)
    f1_g.finish()

    def expand(it, carry):
        q, rows = lax.div(it, IMG), image_rows(lax.rem(it, IMG))
        left = jnp.concatenate([sec[k, rows] for k in range(6)], 1)
        pre = dot_nt(left, W[1, lax.div(q, 2), lax.rem(q, 2)].reshape(D, D)) + vec[pl.ds(8 + q, 1), :]
        value, derivative = gelu_parts(pre)
        act[q, rows] = value.astype(BF)
        slope[q, rows] = derivative.astype(BF)
        return carry

    lax.fori_loop(0, 3, expand, 0)
    f2_g.line(3, 0)
    f2_g.line(3, 1)
    f2_g.arrive(2)
    lax.fori_loop(3, 9, expand, 0)
    f2_g.arrive(3)
    lax.fori_loop(9, 12, expand, 0)
    f2_g.finish()

    def contract(hidden_units, m):
        def body(i, carry):
            rows = image_rows(i)
            for j in range(3):
                lanes = slice(256 * j, 256 * j + 256)
                left = jnp.concatenate([hidden_units[q, rows] for q in range(4)], 1)
                temp[rows, lanes] = dot(left, W[m, :, :, :, :, :, lanes].reshape(4 * D, 256))
            return carry

        lax.fori_loop(0, IMG, body, 0)

    contract(act, 2)

    def wide(column):
        return jnp.concatenate([column] * 6, 1)

    pooled[...] = jnp.zeros(pooled.shape, F32)
    for i in range(IMG):
        sums, count = jnp.zeros((1, D), F32), jnp.zeros((1, 128), F32)
        for start, size in CUTS:
            rows = pl.ds(i * PAD + start, size)
            mask = mask_ref[rows]
            slots = (i, slice(start, start + size))
            outputs = (res_ref[slots] + temp[rows] + vec[5:6]) * wide(mask)
            mix_ref[slots] = outputs.astype(BF)
            sums = sums + jnp.sum(outputs, 0, keepdims=True)
            count = count + jnp.sum(mask, 0, keepdims=True)
        pooled[i : i + 1, :] = sums / wide(count)
        pooled[8 + i : 9 + i, :] = wide(count)

    def unit_grad(grad, values, inverse):
        return inverse * grad - inverse * inverse * inverse * values * jnp.sum(values * grad, -1, keepdims=True)

    own_pooled = pooled[0:8]
    image_unit, image_inverse = unit(own_pooled)
    image_unit = image_unit.astype(BF)
    message = jnp.zeros((32, 128), F32)
    for k in range(6):
        at = jnp.where((iota((32, 8), 0) == iota((32, 8), 1) + IMG * k) & (iota((32, 8), 1) < IMG), 1.0, 0.0).astype(BF)
        message = message + dot(at, image_unit[:, 128 * k : 128 * k + 128])
    units[p.c, p.plane] = message.astype(BF)

    def push(i, carry):
        q = lax.rem(p.plane + i, half)
        remote(units.at[p.c, p.plane], units.at[p.c, p.plane], 1, p.in_plane(q)).start()
        return carry

    lax.fori_loop(1, half, push, 0)
    all_but_own = remote(units.at[p.c, pl.ds(0, half - 1)], units.at[p.c, pl.ds(0, half - 1)], 1, p.sib)

    def gathered(source_chunks, chunk_rows, row_of, tiles, base):
        results = []
        for k in range(tiles):
            value = jnp.zeros((total, 128), F32)
            for number, chunk in source_chunks:
                owner, inside = split(iota((1, chunk_rows), 1), base)
                target = row_of(owner, inside, number, k)
                value = value + dot(jnp.where(iota((total, chunk_rows), 0) == target, 1.0, 0.0).astype(BF), chunk)
            results.append(value)
        return results

    def text_row(owner, inside, number, k):
        at = inside - 3 - per_group * k
        group = group_of(owner + 8 * number)
        return jnp.where((at >= 0) & (at < per_group), group * per_group + at, -1)

    chunks = [(2 * c + l, small[c, l].reshape(8 * small_rows, 128)) for c in range(2) for l in range(2)]
    tiles = gathered(chunks, 8 * small_rows, text_row, 6, small_rows)
    for b in range(r):
        for k in range(6):
            G[1, b // 16, b // 8 % 2, b // 2 % 4, b % 2, :, 128 * k : 128 * k + 128] = tiles[k][ROWS * b : ROWS * b + ROWS].astype(BF)

    def texts():
        return jnp.concatenate([G[1, b // 16, b // 8 % 2, b // 2 % 4, b % 2] for b in range(r)], 0)

    owner, inside = split(iota((total, 1), 0), per_group)
    lines = dot(jnp.where(owner == group_of(iota((1, GROUPS), 1)), 1.0, 0.0).astype(BF), picked(1))
    places = iota((1, 128), 1)
    high = jnp.sum(jnp.where(places == inside + PAIR_LANE, lines, 0.0), 1, keepdims=True)
    rest = jnp.sum(jnp.where(places == inside + PAIR_LANE + per_group, lines, 0.0), 1, keepdims=True)
    pair_rows[...] = jnp.broadcast_to(high * 256.0 + rest, (total, 128))

    all_but_own.wait_recv()
    share = remote(units.at[p.c], units.at[p.c], 2, p.sib)
    share.start()
    remote(units.at[1 - p.c], units.at[1 - p.c], 2, p.sib).wait_recv()

    for k in range(6):

        def add_chunk(number, value, k=k):
            c, at = lax.div(number * 16, half), lax.rem(number * 16, half)
            owner, inside = split(iota((1, 512), 1), 32)
            q = owner + at
            t = inside - IMG * k
            if r == 1:
                linear = 2 * q + c
            else:
                chip, rho = split(q, r)
                linear = (2 * chip + c) * r + rho
            target = jnp.where((t >= 0) & (t < IMG), linear * IMG + t, -1)
            pick = jnp.where(iota((total, 512), 0) == target, 1.0, 0.0).astype(BF)
            return value + dot(pick, units[c, pl.ds(at, 16)].reshape(512, 128))

        value = lax.fori_loop(0, n // 16, add_chunk, jnp.zeros((total, 128), F32)).astype(BF)
        for b in range(r):
            G[2, b // 16, b // 8 % 2, b // 2 % 4, b % 2, :, 128 * k : 128 * k + 128] = value[ROWS * b : ROWS * b + ROWS]

    def block(m, b):
        return G[m, lax.div(b, 16), lax.rem(lax.div(b, 8), 2), lax.rem(lax.div(b, 2), 4), lax.rem(b, 2)]

    scale = scale_ref[0:1, 0:1]
    row = jnp.zeros((1, total), F32)

    def similar(b, col_top):
        rows = pl.ds(pl.multiple_of(b * ROWS, ROWS), ROWS)
        part = dot_nt(block(2, b), texts()) * scale
        temp[rows, :total] = part
        return jnp.maximum(col_top, jnp.max(part, 0, keepdims=True))

    col_top = lax.fori_loop(0, r, similar, row - jnp.inf)

    def by_blocks(fn):
        def body(b, carry):
            rows = pl.ds(pl.multiple_of(b * ROWS, ROWS), ROWS)
            part = temp[rows, :total]
            top = jnp.max(part, 1, keepdims=True)
            row_lse = top + jnp.log(jnp.sum(jnp.exp(part - top), 1, keepdims=True))
            match = jnp.where(iota((ROWS, total), 1) == pair_of(rows), 1.0, 0.0)
            return fn(b, part, row_lse, match, carry)

        return body

    def pair_of(rows):
        return pair_rows[rows][:, 0:1].astype(jnp.int32)

    def sums(b, part, row_lse, match, carry):
        col_sum, loss = carry
        paired = jnp.sum(jnp.sum(part * match, 1, keepdims=True), 0, keepdims=True)
        return col_sum + jnp.sum(jnp.exp(part - col_top), 0, keepdims=True), loss + jnp.sum(row_lse, 0, keepdims=True) - 2.0 * paired

    col_sum, loss = lax.fori_loop(0, r, by_blocks(sums), (row, jnp.zeros((1, 1), F32)))
    col_lse = col_top + jnp.log(col_sum)
    loss = (loss + jnp.sum(col_lse, 1, keepdims=True)) / (2.0 * total)
    loss_ref[...] = jnp.broadcast_to(loss, (8, 128))

    def own_of(places):
        return jnp.where((places == iota(places.shape, 0) + IMG * p.index) & (iota(places.shape, 0) < IMG), 1.0, 0.0).astype(BF)

    own = own_of(iota((8, total), 1))

    def similar_grad(b, part, row_lse, match, carry):
        grad_rows, grad_text = carry
        grad = 0.5 * (jnp.exp(part - row_lse) + jnp.exp(part - col_lse)) - match
        grad = (scale * grad).astype(BF)
        own_rows = own_of(iota((8, ROWS), 1) + b * ROWS)
        return grad_rows + dot(own_rows, grad), grad_text + dot(dot_nt(own, grad).astype(BF), block(2, b))

    grad_rows, grad_text = lax.fori_loop(0, r, by_blocks(similar_grad), (jnp.zeros((8, total), F32), jnp.zeros((8, D), F32)))
    grad_unit = dot(grad_rows.astype(BF), texts())
    row_grad[...] = unit_grad(grad_unit, own_pooled, image_inverse) / jnp.maximum(pooled[8:16], 1.0)
    own_text = text_ref[...].astype(F32)
    _, text_inverse = unit(own_text)
    tg_ref[...] = unit_grad(grad_text[:IMG], own_text, text_inverse)

    sc0, sc1, sc2 = (
        Scatter(p, G.at[m], area, ends.at[1 if m == 1 else 0], s_send.at[m], s_recv.at[m], m == 0)
        for m, area in (
            (0, lambda k: room.at[k]),
            (1, lambda k: W.at[2, k // 2, k % 2] if isinstance(k, int) else W.at[2, 0, k]),
            (2, lambda k: room.at[k]),
        )
    )

    def out_grad(slots, rows):
        return wide(mask_ref[rows]) * (cot_ref[slots].astype(F32) + row_grad[pl.ds(slots[0], 1), :])

    def first_round(slots, rows):
        value = out_grad(slots, rows).astype(BF)
        grad2[rows] = value
        vec_grad[5:6] += jnp.sum(value.astype(F32), 0, keepdims=True)

    by_rows(first_round)
    order = ((1 - p.c, 1 - p.f), (p.c, 1 - p.l), (1 - p.c, p.f), (p.c, p.l))

    def weight_grad(m, at, left, right):
        left = left.T
        for j in range(3):
            lanes = slice(256 * j, 256 * j + 256)
            G[(m,) + at + (slice(None), slice(None), slice(None), lanes)] = (
                dot(left, right[:, lanes]).astype(BF).reshape(4, 2, ROWS, 256)
            )

    for step, at in enumerate(order):
        weight_grad(2, at, act[2 * at[0] + at[1]], grad2[...])
        if step == 0:
            sc2.core_send(1 - p.f)
        if step == 2:
            sc2.core_send(p.f)
    for q in range(4):
        for part in range(2):
            lanes = slice(384 * part, 384 * part + 384)
            value = dot_nt(grad2[...], W[2, q // 2, q % 2, 2 * part : 2 * part + 2].reshape(384, D)) * slope[q, :, lanes].astype(F32)
            value = value.astype(BF)
            slope[q, :, lanes] = value
            vec_grad[8 + q : 9 + q, lanes] = jnp.sum(value.astype(F32), 0, keepdims=True)
        if q == 0:
            sc2.core_add(1 - p.l)
            sc2.side_send()
        if q == 1:
            sc2.core_add(p.l)
    sc2.side_add(3)
    sc2.ends(3)
    f2_g.drain()

    def give(k):
        for at, device in ((0, p.sib), (1, p.ln), (2, p.fn)):
            pl.semaphore_signal(credit.at[k, at], inc=1, device_id=device, device_id_type=MESH)
        p.for_others(lambda zz: pl.semaphore_signal(credit.at[k, 3 + p.z], inc=1, device_id=p.column(zz), device_id_type=MESH))

    def take(k, *which):
        for at in which:
            pl.semaphore_wait(credit.at[k, at], 1)

    def take_column(k):
        p.for_others(lambda zz: pl.semaphore_wait(credit.at[k, 3 + zz], 1))

    give(0)
    for step, at in enumerate(order):
        weight_grad(1, at, slope[2 * at[0] + at[1]], slabs(sec, 0, 6))
        if step == 0:
            take(0, 0)
            sc1.core_send(1 - p.f)
        if step == 2:
            sc1.core_send(p.f)
            sc2.side_add(2)
            sc2.ends(2)
    contract(slope, 1)
    sc1.core_add(1 - p.l)
    take(0, 1)
    sc1.side_send()
    sc1.core_add(p.l)
    sc2.side_add(1)
    sc2.ends(1)
    sc2.side_add(0)

    def second_back(slots, rows):
        grad = temp[rows]
        normalized, inverse = norm_parts(res_ref[slots])
        total_grad = out_grad(slots, rows) + norm_grad(grad, vec[3:4], normalized, inverse)
        res_ref[slots] = total_grad
        rounded = total_grad.astype(BF)
        grad2[rows] = rounded
        vec_grad[3:4] += jnp.sum(grad * normalized, 0, keepdims=True)
        vec_grad[4:5] += jnp.sum(grad, 0, keepdims=True)
        vec_grad[2:3] += jnp.sum(rounded.astype(F32), 0, keepdims=True)

    by_rows(second_back)
    sc2.inner(2, True)
    sc2.inner(2, False)
    attended = slabs(att, 0, 6)
    for j in range(3):
        lanes = slice(256 * j, 256 * j + 256)
        store_runs(G.at[0], out_runs(256 * j, 256 * j + 256), dot(grad2[:, lanes].T, attended).astype(BF))
    for j in range(3):
        lanes = slice(256 * j, 256 * j + 256)
        part = dot(grad2[...], load_runs(W.at[0], out_runs(0, D), lanes)).astype(BF)
        sec[2 * j] = part[:, :128]
        sec[2 * j + 1] = part[:, 128:]

    def attend_back(it, carry):
        i, first = lax.div(it, 6 // PAIRS), lax.rem(it, 6 // PAIRS) * PAIRS
        bars = jnp.concatenate([jnp.where(mask_ref[image_rows(i)] > 0, 0.0, -1e30)] * 2, 1)[:, :PAD]
        results = []
        for step in range(PAIRS):
            rows, plain_q, k, v = head_pair(i, first + step)
            grad_out = sec[first + step, rows]
            q, k = plain_q * jnp.asarray(0.125, BF), k * jnp.asarray(0.125, BF)
            k_t = k.T
            q_halves, out_halves, v_halves = halves(q), halves(grad_out), halves(v)
            grad_v, grad_k, grad_q = 0.0, 0.0, []
            for h, k_h in enumerate(halves(k)):
                scores = dot_nt(k_h, plain_q) + bars
                probs = jnp.exp(scores - lse[(i * 6 + first + step) * 2 + h])
                grad_v = grad_v + dot(probs.astype(BF), out_halves[h])
                grad_probs = dot_nt(v_halves[h], grad_out)
                grad_scores = (probs * (grad_probs - jnp.sum(grad_probs * probs, 0, keepdims=True))).astype(BF)
                grad_k = grad_k + dot(grad_scores, q_halves[h])
                grad_q.append(dot(k_t[64 * h : 64 * h + 64], grad_scores))
            results.append((jnp.concatenate(grad_q, 0).T.astype(BF), grad_k.astype(BF), grad_v.astype(BF)))
        for step in range(PAIRS):
            for which in range(3):
                qkv[6 * which + first + step, rows] = results[step][which]
        return carry

    take(0, 2)
    take_column(0)
    lax.fori_loop(0, 2, attend_back, 0)
    sc1.side_add(3)
    sc1.ends(3)
    lax.fori_loop(2, 4, attend_back, 0)
    sc2.inner(1, True)
    sc2.inner(1, False)
    sc1.side_add(2)
    sc1.ends(2)
    lax.fori_loop(4, 6, attend_back, 0)
    sc1.side_add(1)
    sc1.ends(1)
    sc1.side_add(0)
    lax.fori_loop(6, 9, attend_back, 0)
    sc2.come()
    for j in range(9):
        left = slabs(qkv, 2 * j, 2)
        store_runs(G.at[0], qkv_runs(256 * j, 256 * j + 256), dot(left.T, norm1[...]).astype(BF))
        if j < 3 or j >= 6:
            row, lanes = (6, slice(256 * j, 256 * j + 256)) if j < 3 else (7, slice(256 * (j - 6), 256 * (j - 6) + 256))
            vec_grad[row : row + 1, lanes] = jnp.sum(left.astype(F32), 0, keepdims=True)
    sc1.inner(2, True)
    sc1.inner(2, False)
    df2_ref[...] = sc2.final()
    give(1)
    take(1, 0)
    sc0.core_send(1 - p.f)
    sc0.core_send(p.f)
    sc0.core_add(1 - p.l)
    take(1, 1)
    sc0.side_send()

    def contract_joined(i, carry):
        rows = image_rows(i)
        for j in range(3):
            lanes = slice(256 * j, 256 * j + 256)
            left = jnp.concatenate([qkv[k, rows] for k in range(18)], 1)
            temp[rows, lanes] = dot(left, load_runs(W.at[0], qkv_runs(0, 3 * D), lanes))
        return carry

    lax.fori_loop(0, IMG, contract_joined, 0)
    sc0.core_add(p.l)
    sc1.inner(1, True)
    sc1.inner(1, False)
    take(1, 2)
    take_column(1)

    def first_back(slots, rows):
        grad = temp[rows]
        normalized, inverse = norm_parts(img_ref[slots].astype(F32))
        res_ref[slots] += norm_grad(grad, vec[0:1], normalized, inverse)
        vec_grad[0:1] += jnp.sum(grad * normalized, 0, keepdims=True)
        vec_grad[1:2] += jnp.sum(grad, 0, keepdims=True)

    by_rows(first_back)
    for h in (3, 2):
        sc0.side_add(h)
        sc0.cross_send(h)

    def two_parts(value):
        high = value.astype(BF)
        return jnp.concatenate([high, (value - high.astype(F32)).astype(BF)], 0)

    @pl.when(p.index >= 0)
    def _():
        lines = [jnp.zeros((2 * GROUPS, 128), F32)] * 8
        for row, (k, offset, width, base) in enumerate(table):
            mask, places = spread(k, 0, width, base)
            line = dot_nt(two_parts(mask * vec_grad[row : row + 1]), places.astype(BF))
            line_at = row if row < 6 else 6 if row < 8 else 7
            lines[line_at] = lines[line_at] + line
        lines = [line[:GROUPS] + line[GROUPS:] for line in lines]
        shape = (GROUPS * 8, 8 * GROUPS)
        k, block_at = split(iota(shape, 1), GROUPS)
        at = jnp.where(iota(shape, 0) == 8 * block_at + k, 1.0, 0.0).astype(BF)
        both = two_parts(jnp.concatenate(lines, 0))
        vec_out[...] = (dot(at, both[: 8 * GROUPS]) + dot(at, both[8 * GROUPS :])).reshape(2, 16, 8, 128)

    vec_swap = remote(vec_out.at[1 - p.c], vec_core, 3, p.sib)
    vec_swap.start()
    for h in (1, 0):
        sc0.side_add(h)
        sc0.cross_send(h)
    vec_swap.wait_recv()
    vec_out[p.c] += vec_core[...]
    mine = (p.l * 4 + p.z) * 2 + p.f

    def push_vec(i, carry):
        q = lax.rem(mine + i, 16)
        dev = p.block(lax.div(q, 8), lax.rem(lax.div(q, 2), 4), lax.rem(q, 2))
        remote(vec_out.at[p.c, q], vec_in.at[mine], 4, dev).start()
        return carry

    lax.fori_loop(1, 16, push_vec, 0)
    vec_in[mine] = vec_out[p.c, mine]
    sc0.cross_add(3)
    sc1.come()
    for h in (2, 1, 0):
        sc0.cross_add(h)
    df1_ref[...] = sc1.final()
    own_qo = sc0.final()
    swap_grad[0] = own_qo
    qo_back = remote(swap_grad.at[0], swap_grad.at[1], 5, p.sib)
    qo_back.start()
    most = remote(vec_out.at[p.c, pl.ds(0, 15)], vec_in.at[pl.ds(0, 15)], 4, p.sib)
    most.wait_recv()
    dvec_ref[...] = jnp.sum(vec_in[...], 0)
    qo_back.wait_recv()
    other_qo = swap_grad[1]
    dq_ref[...] = jnp.where(
        first_core, own_qo[:QKV_ROWS], jnp.concatenate([other_qo[QKV_ROWS:], own_qo[:gap]], 0)
    )
    do_ref[...] = jnp.where(first_core, other_qo[gap : gap + OUT_ROWS], own_qo[QKV_ROWS:])

    all_but_own.wait_send()
    share.wait_send()
    vec_swap.wait_send()
    most.wait_send()
    qo_back.wait_send()
    for g in (sm_g, qo_g, f1_g):
        g.drain()
    for s in (sc0, sc1, sc2):
        s.drain()


def results_kernel(*refs):
    sources, results = refs[:9], refs[9:]
    for k in (0, 1, 3, 4, 5, 6, 7):
        results[k][...] = sources[k][...]
    results[2][...] = sources[2][0:1, 0:1]
    for k in range(8):
        results[8 + k][...] = sources[8][k : k + 1, 0 : results[8 + k].shape[1]]


def swap(block, step, size):
    return lax.ppermute(block, "fsdp", [(i, i ^ step) for i in range(size)])


def pregather(block, F, r):
    step = 1
    while step < r:
        high = (lax.axis_index("fsdp") // step) % 2 == 1
        other = swap(block, step, F)
        block = jnp.concatenate([jnp.where(high, other, block), jnp.where(high, block, other)], 0)
        step *= 2
    return block


def postscatter(block, F, r):
    step = r // 2
    while step:
        high = (lax.axis_index("fsdp") // step) % 2 == 1
        lower, upper = jnp.split(block, 2)
        block = jnp.where(high, upper, lower) + swap(jnp.where(high, lower, upper), step, F)
        step //= 2
    return block


def per_device(
    F,
    r,
    n,
    images,
    tissue,
    pair_index,
    text_embed,
    logit_scale,
    ln1_gain,
    ln1_bias,
    w_qkv,
    bias_qv,
    w_out,
    bias_out,
    ln2_gain,
    ln2_bias,
    w_fc1,
    bias_fc1,
    w_fc2,
    bias_fc2,
    cotangent,
):
    gather = functools.partial(pregather, F=F, r=r)

    pair = gather(pair_index)
    vectors = [gather(v) for v in (ln1_gain, ln1_bias, bias_out, ln2_gain, ln2_bias, bias_fc2, bias_qv, bias_fc1)]
    vectors += [(pair // 256).astype(BF), (pair % 256).astype(BF)]
    pair_at = 128 + PAIR_LANE
    places = (0, 24, 48, 72, 96, 128, 152, 256, pair_at, pair_at + IMG * r)
    thin = sum(jnp.pad(v, (at, 384 - at - v.shape[0])) for v, at in zip(vectors, places)).reshape(3, 128)
    small_rows = -(-(3 + 18 * r) // 16) * 16
    vmem = pl.BlockSpec(memory_space=pltpu.VMEM)
    shape = jax.ShapeDtypeStruct
    mix, res, loss, text_grad, dq, do, df1, df2, dvec = pl.pallas_call(
        functools.partial(layer_kernel, F, r, n),
        out_shape=(
            shape((IMG, SLOTS, D), BF),
            shape((IMG, SLOTS, D), F32),
            shape((8, 128), F32),
            shape((IMG, D), F32),
            shape((QKV_ROWS, D), F32),
            shape((OUT_ROWS, D), F32),
            shape((ROWS, D), F32),
            shape((ROWS, D), F32),
            shape((8, 128), F32),
        ),
        in_specs=[vmem] * 11,
        out_specs=(vmem,) * 9,
        scratch_shapes=[
            pltpu.VMEM((3, 2, 2, 4, 2, ROWS, D), BF),
            pltpu.VMEM((3, 2, 2, 4, 2, ROWS, D), BF),
            pltpu.VMEM((4, 4, 2, ROWS, D), BF),
            pltpu.VMEM((2, 3, ROWS, D), BF),
            pltpu.VMEM((2, 2, 4, 2, small_rows, 128), BF),
            pltpu.VMEM((TOK, 128), F32),
            pltpu.VMEM((8, 256), F32),
            pltpu.VMEM((-(-IMG * r // 8) * 8, D), F32),
            pltpu.VMEM((2, ROWS, D), F32),
            pltpu.VMEM((TOK, D), BF),
            pltpu.VMEM((18, TOK, 128), BF),
            pltpu.VMEM((6, TOK, 128), BF),
            pltpu.VMEM((2 * IMG * 6, 1, PAD), F32),
            pltpu.VMEM((6, TOK, 128), BF),
            pltpu.VMEM((4, TOK, D), BF),
            pltpu.VMEM((4, TOK, D), BF),
            pltpu.VMEM((TOK, D), BF),
            pltpu.VMEM((max(TOK, IMG * n), D), F32),
            pltpu.VMEM((16, D), F32),
            pltpu.VMEM((16, D), F32),
            pltpu.VMEM((16, D), F32),
            pltpu.VMEM((8, D), F32),
            pltpu.VMEM((IMG * n, 128), F32),
            pltpu.VMEM((2, n // 2, 32, 128), BF),
            pltpu.VMEM((2, 16, 8, 128), F32),
            pltpu.VMEM((16, 8, 128), F32),
            pltpu.VMEM((16, 8, 128), F32),
            pltpu.SemaphoreType.DMA((4, 32)),
            pltpu.SemaphoreType.DMA((4, 32)),
            pltpu.SemaphoreType.DMA((3, 32)),
            pltpu.SemaphoreType.DMA((3, 32)),
            pltpu.SemaphoreType.DMA((16,)),
            pltpu.SemaphoreType.REGULAR((2, 8)),
        ],
        compiler_params=pltpu.CompilerParams(collective_id=0, has_side_effects=True, vmem_limit_bytes=VMEM_LIMIT),
    )(
        gather(w_qkv.T),
        gather(w_out.T),
        gather(w_fc1.T),
        gather(w_fc2),
        thin,
        gather(text_embed),
        images,
        cotangent,
        tissue,
        text_embed,
        jnp.broadcast_to(logit_scale.reshape(1, 1), (8, 128)),
    )
    widths = (24,) * 6 + (48, 96)
    mix, res, loss, text_grad, dq, do, df1, df2, *vectors = pl.pallas_call(
        results_kernel,
        out_shape=(
            shape((IMG, SLOTS, D), BF),
            shape((IMG, SLOTS, D), F32),
            shape((1, 1), F32),
            shape((IMG, D), F32),
            shape((QKV_ROWS, D), F32),
            shape((OUT_ROWS, D), F32),
            shape((ROWS, D), F32),
            shape((ROWS, D), F32),
        )
        + tuple(shape((1, width), F32) for width in widths),
        in_specs=[vmem] * 9,
        out_specs=(vmem,) * 16,
        compiler_params=pltpu.CompilerParams(vmem_limit_bytes=VMEM_LIMIT),
    )(mix, res, loss, text_grad, dq, do, df1, df2, dvec)
    scatter = functools.partial(postscatter, F=F, r=r)
    vectors = [scatter(v.reshape(-1)) for v in vectors]
    return (
        mix,
        res,
        loss.reshape(()),
        text_grad,
        vectors[0],
        vectors[1],
        scatter(dq).T,
        vectors[6],
        scatter(do).T,
        vectors[2],
        vectors[3],
        vectors[4],
        scatter(df1).T,
        vectors[7],
        scatter(df2),
        vectors[5],
    )


def solution(mesh):
    F = mesh.shape["fsdp"]
    n = mesh.shape["dp"] * F
    r = n // GROUPS
    both = ("dp", "fsdp")
    rows, columns = P(both), P(None, both)
    in_specs = (
        rows, rows, rows, rows, P(), rows, rows, columns, rows, columns, rows, rows, rows, columns, rows, rows, rows, rows
    )
    out_specs = (
        rows, rows, P(), rows, rows, rows, columns, rows, columns, rows, rows, rows, columns, rows, rows, rows
    )
    return jax.shard_map(
        functools.partial(per_device, F, r, n), mesh=mesh, in_specs=in_specs, out_specs=out_specs, check_vma=False
    )
```

```python
import functools
import math

import jax
import jax.numpy as jnp
from jax import lax
from jax.experimental import pallas as pl
from jax.experimental.pallas import tpu as pltpu
from jax.sharding import PartitionSpec as P

MESH = pl.DeviceIdType.MESH
MIB = 1024 * 1024
GROUPS = 32
D = 768
HEADS = 12
PAD = 208
IMG = 3
SLOTS = 196
PAIR_LANE = 72
TOK = IMG * PAD
QKV_ROWS, OUT_ROWS = 72, 24
ROWS = 96
VMEM_LIMIT = 63 * MIB
EPS = 1e-6
BF, F32 = jnp.bfloat16, jnp.float32


def dot(a, b):
    return lax.dot_general(a, b, (((1,), (0,)), ((), ())), preferred_element_type=F32)


def dot_nt(a, b):
    return lax.dot_general(a, b, (((1,), (1,)), ((), ())), preferred_element_type=F32)


def dot_exact(a, b, dims):
    return lax.dot_general(a, b, (dims, ((), ())), preferred_element_type=F32, precision=lax.Precision.HIGHEST)


def iota(shape, dim):
    return lax.broadcasted_iota(jnp.int32, shape, dim)


def split(numbers, by):
    quotient = jnp.floor((numbers.astype(F32) + 0.5) * (1.0 / by)).astype(jnp.int32)
    return quotient, numbers - quotient * by


class Pos:
    def __init__(p, F, r, n):
        p.F, p.r, p.n = F, r, n
        p.index = lax.axis_index("dp") * F + lax.axis_index("fsdp")
        p.g, p.rho = lax.div(p.index, r), lax.rem(p.index, r)
        p.c, p.z = lax.rem(p.g, 2), lax.rem(lax.div(p.g, 2), 4)
        p.x, p.y = lax.rem(lax.div(p.g, 8), 2), lax.div(p.g, 16)
        p.l = p.y + p.c * (p.x - p.y)
        p.f = p.x + p.c * (p.y - p.x)
        c, x, y, z = p.c, p.x, p.y, p.z
        p.sib = p.chip(y, x, z, 1 - c)
        p.fn = p.chip(y + c * (1 - 2 * y), x + (1 - c) * (1 - 2 * x), z, c)
        p.ln = p.chip(y + (1 - c) * (1 - 2 * y), x + c * (1 - 2 * x), z, c)
        p.up = p.chip(y, x, jnp.minimum(z + 1, 3), c)
        p.dn = p.chip(y, x, jnp.maximum(z - 1, 0), c)
        p.plane = lax.div(p.g, 2) * r + p.rho

    def device(p, linear):
        return (lax.div(linear, p.F), lax.rem(linear, p.F))

    def chip(p, y, x, z, c):
        return p.device((((y * 2 + x) * 4 + z) * 2 + c) * p.r + p.rho)

    def column(p, zz):
        return p.chip(p.y, p.x, zz, p.c)

    def at_distance(p, h, fn):
        if h == 0:
            fn(p.z)
            return

        @pl.when(p.z + h <= 3)
        def _():
            fn(p.z + h)

        @pl.when(p.z - h >= 0)
        def _():
            fn(p.z - h)

    def for_others(p, fn):
        for h in (1, 2, 3):
            p.at_distance(h, fn)

    def in_plane(p, q):
        return p.device((lax.div(q, p.r) * 2 + p.c) * p.r + lax.rem(q, p.r))

    def block(p, l, z, f):
        y, x = l + p.c * (f - l), f + p.c * (l - f)
        return p.chip(y, x, z, p.c)


def group_of(block):
    c = block // 16 if isinstance(block, int) else jnp.where(block >= 16, 1, 0)
    rest = block - c * 16
    if isinstance(block, int):
        l, z, f = rest // 8, rest // 2 % 4, rest % 2
    else:
        l = jnp.where(rest >= 8, 1, 0)
        zf = rest - 8 * l
        z = jnp.where(zf >= 2, 1, 0) + jnp.where(zf >= 4, 1, 0) + jnp.where(zf >= 6, 1, 0)
        f = zf - 2 * z
    y, x = l + c * (f - l), f + c * (l - f)
    return ((y * 2 + x) * 4 + z) * 2 + c


def enter(p):
    bar = pltpu.get_barrier_semaphore()
    for device in (p.sib, p.fn, p.ln):
        pl.semaphore_signal(bar, inc=1, device_id=device, device_id_type=MESH)
    p.for_others(lambda zz: pl.semaphore_signal(bar, inc=1, device_id=p.column(zz), device_id_type=MESH))


class Gather:
    def __init__(s, p, held, send, recv, line_first=False):
        s.p, s.held, s.send, s.recv, s.line_first = p, held, send, recv, line_first

    def cp(s, at, ks, kr, dev):
        ref = s.held.at[at]
        return pltpu.make_async_remote_copy(
            src_ref=ref, dst_ref=ref, send_sem=s.send.at[ks], recv_sem=s.recv.at[kr], device_id=dev, device_id_type=MESH
        )

    def first(s):
        p = s.p
        return s.cp((p.c, p.l, p.z, p.f), 0, 0, p.fn)

    def first_in(s):
        p = s.p
        return s.cp((p.c, p.l, p.z, 1 - p.f), 0, 0, p.fn)

    def f_of(s, b):
        return s.p.f + b * (1 - 2 * s.p.f)

    def up(s, zz, b):
        return s.cp((s.p.c, s.p.l, zz, s.f_of(b)), 1 + 2 * zz + b, 1 + 2 * zz + b, s.p.up)

    def dn(s, zz, b):
        return s.cp((s.p.c, s.p.l, zz, s.f_of(b)), 9 + 2 * zz + b, 1 + 2 * zz + b, s.p.dn)

    def cross(s, zz):
        return s.cp((s.p.c, s.p.l, zz, s.p.f), 2 + 2 * zz, 2 + 2 * zz, s.p.fn)

    def cross_in(s, zz):
        return s.cp((s.p.c, s.p.l, zz, 1 - s.p.f), 2 + 2 * zz, 2 + 2 * zz, s.p.fn)

    def last(s, zz):
        return s.cp((s.p.c, s.p.l, zz), 17 + zz, 9 + zz, s.p.ln)

    def last_in(s, zz):
        return s.cp((s.p.c, 1 - s.p.l, zz), 17 + zz, 9 + zz, s.p.ln)

    def core(s, l, zz):
        return s.cp((s.p.c, l, zz), 21 + 4 * l + zz, 13 + 4 * l + zz, s.p.sib)

    def core_in(s, l, zz):
        return s.cp((1 - s.p.c, l, zz), 21 + 4 * l + zz, 13 + 4 * l + zz, s.p.sib)

    def own(s, b):
        p = s.p
        if b:
            s.first_in().wait_recv()
        else:
            s.first().start()
        if not (b and s.line_first):

            @pl.when(p.z < 3)
            def _():
                s.up(p.z, b).start()

            @pl.when(p.z > 0)
            def _():
                s.dn(p.z, b).start()

        if b:
            s.last(p.z).start()
            s.core(p.l, p.z).start()

    def line(s, h, b):
        p = s.p

        def one(zz, copy, onward):
            if b and s.line_first:
                s.cross_in(zz).wait_recv()
            else:
                copy(zz, b).wait_recv()

                @pl.when(onward)
                def _():
                    copy(zz, b).start()

                if s.line_first:
                    s.cross(zz).start()
            if b:
                s.last(zz).start()
                s.core(p.l, zz).start()

        @pl.when(p.z - h >= 0)
        def _():
            one(p.z - h, s.up, p.z < 3)

        @pl.when(p.z + h <= 3)
        def _():
            one(p.z + h, s.dn, p.z > 0)

    def arrive(s, h):
        p = s.p

        def one(zz):
            s.last_in(zz).wait_recv()
            s.core(1 - p.l, zz).start()

        if h == 0:
            one(p.z)
        else:

            @pl.when(p.z - h >= 0)
            def _():
                one(p.z - h)

            @pl.when(p.z + h <= 3)
            def _():
                one(p.z + h)

    def finish(s):
        for zz in range(4):
            for l in range(2):
                s.core_in(l, zz).wait_recv()

    def drain(s):
        p = s.p
        s.first().wait_send()
        for zz in range(4):

            @pl.when((p.z < 3) & (zz <= p.z))
            def _():
                s.up(zz, 0).wait_send()
                if not s.line_first:
                    s.up(zz, 1).wait_send()

            @pl.when((p.z > 0) & (zz >= p.z))
            def _():
                s.dn(zz, 0).wait_send()
                if not s.line_first:
                    s.dn(zz, 1).wait_send()

            if s.line_first:

                @pl.when(zz != p.z)
                def _():
                    s.cross(zz).wait_send()

            s.last(zz).wait_send()
            for l in range(2):
                s.core(l, zz).wait_send()


class Scatter:
    def __init__(s, p, sums, room, landing, send, recv, line_last=False):
        s.p, s.sums, s.room, s.landing, s.send, s.recv, s.line_last = p, sums, room, landing, send, recv, line_last

    def cp(s, src, dst, ks, kr, dev):
        return pltpu.make_async_remote_copy(
            src_ref=src, dst_ref=dst, send_sem=s.send.at[ks], recv_sem=s.recv.at[kr], device_id=dev, device_id_type=MESH
        )

    def core_cp(s, l):
        return s.cp(s.sums.at[1 - s.p.c, l], s.room(l), 1 + l, 1 + l, s.p.sib)

    def side_cp(s, zz):
        return s.cp(s.sums.at[s.p.c, 1 - s.p.l, zz], s.room(2).at[zz], 3 + zz, 3 + zz, s.p.ln)

    def f_of(s, b):
        return 1 - s.p.f if b == 0 else s.p.f

    def here(s, zz, b):
        return s.sums.at[s.p.c, s.p.l, zz, s.f_of(b)]

    def up_far(s, zz, b):
        return s.cp(s.here(zz, b), s.room(3).at[zz, b], 7 + 2 * zz + b, 7 + 2 * zz + b, s.p.up)

    def up_end(s, zz, b):
        return s.cp(s.here(zz, b), s.landing.at[b], 7 + 2 * zz + b, 15 + b, s.p.up)

    def down(s, zz, b):
        return s.cp(s.here(zz, b), s.room(3).at[zz, b], 15 + 2 * zz + b, 7 + 2 * zz + b, s.p.dn)

    def last_cp(s):
        return s.cp(s.here(s.p.z, 0), s.landing.at[2], 0, 0, s.p.fn)

    def cross_cp(s, zz):
        return s.cp(s.here(zz, 0), s.room(3).at[zz, 0], 23 + zz, 17 + zz, s.p.fn)

    def cross_send(s, h):
        s.by_distance(h, lambda zz: s.cross_cp(zz).start())

    def cross_add(s, h):
        def one(zz):
            s.cross_cp(zz).wait_recv()
            s.add(zz, 1, s.room(3).at[zz, 0])
            if h > 0:
                s.straight(zz).start()

        s.by_distance(h, one)

    def core_send(s, l):
        s.core_cp(l).start()

    def core_add(s, l):
        s.core_cp(l).wait_recv()
        room = s.room(l)

        def body(zz, carry):
            for f in range(2):
                ref = s.sums.at[s.p.c, l, zz, f]
                ref[...] = (ref[...].astype(F32) + room[zz, f].astype(F32)).astype(BF)
            return carry

        lax.fori_loop(0, 4, body, 0)

    def add(s, zz, b, ref):
        total = s.here(zz, b)
        total[...] = (total[...].astype(F32) + ref[...].astype(F32)).astype(BF)

    def by_distance(s, h, fn):
        s.p.at_distance(h, fn)

    def side_send(s):
        for h in (3, 2, 1, 0):
            s.by_distance(h, lambda zz: s.side_cp(zz).start())

    def side_add(s, h):
        def one(zz):
            s.side_cp(zz).wait_recv()
            for f in (0, 1):
                total = s.sums.at[s.p.c, s.p.l, zz, f]
                total[...] = (total[...].astype(F32) + s.room(2)[zz, f].astype(F32)).astype(BF)

        s.by_distance(h, one)

    def ends(s, h):
        p = s.p

        @pl.when(p.z == 0)
        def _():
            for b in (0, 1):
                (s.up_end if h == 1 else s.up_far)(p.z + h, b).start()

        @pl.when(p.z == 3)
        def _():
            for b in (0, 1):
                s.down(p.z - h, b).start()

    def inner(s, h, upward):
        p = s.p
        if upward:

            @pl.when((p.z == 1) | (p.z == 2) if h == 1 else p.z == 1)
            def _():
                zz = p.z + h
                for b in (0, 1):
                    s.up_far(zz, b).wait_recv()
                    s.add(zz, b, s.room(3).at[zz, b])
                    (s.up_end if h == 1 else s.up_far)(zz, b).start()

        else:

            @pl.when((p.z == 1) | (p.z == 2) if h == 1 else p.z == 2)
            def _():
                zz = p.z - h
                for b in (0, 1):
                    s.down(zz, b).wait_recv()
                    s.add(zz, b, s.room(3).at[zz, b])
                    s.down(zz, b).start()

    def come(s):
        p = s.p
        for b in (0, 1):

            @pl.when(p.z > 0)
            def _():
                s.up_end(p.z, b).wait_recv()
                s.add(p.z, b, s.landing.at[b])

            @pl.when(p.z < 3)
            def _():
                s.down(p.z, b).wait_recv()
                s.add(p.z, b, s.room(3).at[p.z, b])

            if b == 0:
                s.last_cp().start()

    def straight(s, zz):
        return s.cp(s.here(zz, 1), s.room(3).at[s.p.z, 1], 7 + zz, 7 + s.p.z, s.p.column(zz))

    def straight_in(s, zz):
        return s.cp(s.here(zz, 1), s.room(3).at[zz, 1], 7 + zz, 7 + zz, s.p.column(zz))

    def final(s):
        p = s.p
        if s.line_last:

            def one(zz):
                s.straight_in(zz).wait_recv()
                s.add(p.z, 1, s.room(3).at[zz, 1])

            p.for_others(one)
            return s.here(p.z, 1)[...].astype(F32)
        s.last_cp().wait_recv()
        return s.here(p.z, 1)[...].astype(F32) + s.landing[2].astype(F32)

    def drain(s):
        p = s.p
        for l in range(2):
            s.core_cp(l).wait_send()
        for zz in range(4):
            s.side_cp(zz).wait_send()
            if s.line_last:
                s.cross_cp(zz).wait_send()

                @pl.when(zz != p.z)
                def _():
                    s.straight(zz).wait_send()

            else:

                @pl.when(zz > p.z)
                def _():
                    s.up_far(zz, 0).wait_send()
                    s.up_far(zz, 1).wait_send()

                @pl.when(zz < p.z)
                def _():
                    s.down(zz, 0).wait_send()
                    s.down(zz, 1).wait_send()

        if not s.line_last:
            s.last_cp().wait_send()


def qkv_runs(start, stop):
    runs, row = [], start
    while row < stop:
        chip, inside = divmod(row, 2 * QKV_ROWS)
        z, x, y = chip % 4, chip // 4 % 2, chip // 8
        first = inside < ROWS
        until = min(stop, chip * 2 * QKV_ROWS + (ROWS if first else 2 * QKV_ROWS))
        low = inside if first else inside - ROWS
        at = (0, y, z, x) if first else (1, x, z, y)
        runs.append((at, low, low + until - row))
        row = until
    return runs


def out_runs(start, stop):
    runs, row = [], start
    while row < stop:
        chip, inside = divmod(row, 2 * OUT_ROWS)
        z, x, y = chip % 4, chip // 4 % 2, chip // 8
        until = min(stop, (chip + 1) * 2 * OUT_ROWS)
        low = inside + 2 * (QKV_ROWS - OUT_ROWS) // 2
        runs.append(((1, x, z, y), low, low + until - row))
        row = until
    return runs


def load_runs(ref, runs, lanes=slice(None)):
    return jnp.concatenate([ref[at + (slice(a, b), lanes)] for at, a, b in runs], 0)


def store_runs(ref, runs, value):
    row = 0
    for at, a, b in runs:
        ref[at + (slice(a, b), slice(None))] = value[row : row + b - a]
        row += b - a


def slabs(ref, first, count):
    return jnp.concatenate([ref[first + k] for k in range(count)], 1)


def norm_parts(values):
    centered = values - jnp.mean(values, -1, keepdims=True)
    inverse = lax.rsqrt(jnp.mean(centered * centered, -1, keepdims=True) + EPS)
    return centered * inverse, inverse


def norm_grad(grad, gain, normalized, inverse):
    h = grad * gain
    return (h - jnp.mean(h, -1, keepdims=True) - normalized * jnp.mean(h * normalized, -1, keepdims=True)) * inverse


def gelu_parts(x):
    z = jnp.abs(x) * math.sqrt(0.5)
    under = 1.0 + 0.3275911 * z
    t = pl.reciprocal(under, approx=True)
    t = t * (2.0 - under * t)
    bell = jnp.exp(-0.5 * x * x)
    poly = ((((1.061405429 * t - 1.453152027) * t + 1.421413741) * t - 0.284496736) * t + 0.254829592) * t
    tail = 0.5 * poly * bell
    cdf = jnp.where(x >= 0, 1.0 - tail, tail)
    return x * cdf, cdf + x * bell * (1.0 / math.sqrt(2.0 * math.pi))


CUTS = ((0, 48), (48, 48), (96, 48), (144, SLOTS - 144))


def by_rows(fn):
    def body(i, carry):
        for start, size in CUTS:
            fn((i, slice(start, start + size)), pl.ds(pl.multiple_of(i * PAD + start, 16), size))
        return carry

    lax.fori_loop(0, IMG, body, 0)


def layer_kernel(
    F,
    r,
    n,
    wq_ref,
    wo_ref,
    f1_ref,
    f2_ref,
    thin_ref,
    group_ref,
    img_ref,
    cot_ref,
    tissue_ref,
    text_ref,
    scale_ref,
    mix_ref,
    res_ref,
    loss_ref,
    tg_ref,
    dq_ref,
    do_ref,
    df1_ref,
    df2_ref,
    dvec_ref,
    W,
    G,
    room,
    ends,
    small,
    mask_ref,
    mask_line,
    text_rows,
    swap_grad,
    norm1,
    qkv,
    att,
    lse,
    sec,
    act,
    slope,
    grad2,
    temp,
    vec,
    vec_grad,
    pooled,
    row_grad,
    pair_rows,
    units,
    vec_out,
    vec_core,
    vec_in,
    g_send,
    g_recv,
    s_send,
    s_recv,
    misc,
    credit,
):
    p = Pos(F, r, n)
    half = n // 2
    total = IMG * n
    per_group = IMG * r
    small_rows = small.shape[4]
    qo_g, f1_g, f2_g = (Gather(p, W.at[m], g_send.at[m], g_recv.at[m], m == 0) for m in range(3))
    sm_g = Gather(p, small, g_send.at[3], g_recv.at[3], True)

    def remote(src, dst, k, dev):
        return pltpu.make_async_remote_copy(
            src_ref=src, dst_ref=dst, send_sem=misc.at[2 * k], recv_sem=misc.at[2 * k + 1], device_id=dev, device_id_type=MESH
        )

    enter(p)
    first_core = p.c == 0
    q_t, o_t = wq_ref[...].astype(F32), wo_ref[...].astype(F32)

    def empty(rows):
        return jnp.zeros((rows, D), F32)

    gap = QKV_ROWS - OUT_ROWS
    to_zero = (
        jnp.concatenate([q_t, empty(ROWS - QKV_ROWS)], 0),
        jnp.concatenate([empty(QKV_ROWS), q_t[: ROWS - QKV_ROWS]], 0),
    )
    to_one = (
        jnp.concatenate([empty(gap), o_t, empty(OUT_ROWS)], 0),
        jnp.concatenate([q_t[ROWS - QKV_ROWS :], empty(OUT_ROWS), o_t], 0),
    )
    W[0, p.c, p.l, p.z, p.f] = jnp.where(first_core, to_zero[0], to_one[1]).astype(BF)
    G[0, 0, 0, 0, 1] = jnp.where(first_core, to_one[0], to_zero[1]).astype(BF)
    pl.semaphore_wait(pltpu.get_barrier_semaphore(), 6)
    swap_copy = remote(G.at[0, 0, 0, 0, 1], G.at[0, 0, 0, 0, 0], 0, p.sib)
    swap_copy.start()

    def unit(values):
        inverse = lax.rsqrt(jnp.sum(values * values, -1, keepdims=True) + EPS)
        return values * inverse, inverse

    text_rows[...] = jnp.zeros(text_rows.shape, F32)
    text_rows[0:per_group] = group_ref[...].astype(F32)
    group_units = unit(text_rows[...])[0].astype(BF)
    own_small = jnp.zeros((small_rows, 128), F32)
    for k in range(6):
        shape = (small_rows, group_units.shape[0])
        at = (iota(shape, 0) == iota(shape, 1) + 3 + per_group * k) & (iota(shape, 1) < per_group)
        own_small = own_small + dot(jnp.where(at, 1.0, 0.0).astype(BF), group_units[:, 128 * k : 128 * k + 128])
    at = jnp.where(iota((small_rows, 8), 0) == iota((small_rows, 8), 1), 1.0, 0.0)
    thin = jnp.where(iota((8, 128), 0) < 3, jnp.concatenate([thin_ref[...].astype(F32)] + [jnp.zeros((5, 128), F32)], 0), 0.0)
    small[p.c, p.l, p.z, p.f] = (own_small + dot(at.astype(BF), thin.astype(BF))).astype(BF)
    sm_g.own(0)
    W[1, p.c, p.l, p.z, p.f] = f1_ref[...]
    swap_copy.wait_recv()
    own_block = W.at[0, p.c, p.l, p.z, p.f]
    own_block[...] = (own_block[...].astype(F32) + G[0, 0, 0, 0, 0].astype(F32)).astype(BF)
    qo_g.own(0)
    f1_g.own(0)
    W[2, p.c, p.l, p.z, p.f] = f2_ref[...]
    vec_grad[...] = jnp.zeros(vec_grad.shape, F32)
    mask_line[...] = jnp.zeros(mask_line.shape, F32)
    mask_line[0:IMG, 0:SLOTS] = tissue_ref[...].astype(F32)
    for i in range(IMG):
        tail = slice(i * PAD + SLOTS // 16 * 16, (i + 1) * PAD)
        nothing = jnp.zeros((PAD - SLOTS // 16 * 16, D), BF)
        norm1[tail] = nothing
        grad2[tail] = nothing
        for k in range(6):
            sec[k, tail] = nothing[:, :128]
        line = jnp.broadcast_to(mask_line[i : i + 1], (128, 256))
        mask_ref[i * PAD : i * PAD + PAD] = line.T[:PAD]
    sm_g.own(1)
    qo_g.own(1)
    for h in (1, 2, 3):
        sm_g.line(h, 0)
        qo_g.line(h, 0)
        sm_g.line(h, 1)
        qo_g.line(h, 1)
        sm_g.arrive(h - 1)
        if h == 1:
            f1_g.own(1)
        if h == 2:
            f1_g.line(1, 0)
        if h == 3:
            f1_g.line(1, 1)
            sm_g.arrive(3)
        qo_g.arrive(h - 1)
    qo_g.arrive(3)
    sm_g.finish()


    def picked(k):
        source, target = iota((GROUPS, GROUPS * small_rows), 1), iota((GROUPS, GROUPS * small_rows), 0)
        return dot(jnp.where(source == target * small_rows + k, 1.0, 0.0).astype(BF), small[...].reshape(GROUPS * small_rows, 128)).astype(BF)

    table = [(0, 0, 24, 0), (0, 24, 24, 0), (0, 48, 24, 0), (0, 72, 24, 0), (0, 96, 24, 0), (1, 0, 24, 0), (1, 24, 48, 0), (1, 24, 48, D)]
    table += [(2, 0, 96, D * q) for q in range(4)]

    def spread(k, offset, width, base):
        owner, inside = split(iota((1, D), 1) + base, width)
        names = iota((GROUPS, 1), 0)
        names = names if k == 2 else group_of(names)
        mask = jnp.where(names == owner, 1.0, 0.0)
        places = jnp.where(iota((128, D), 0) == inside + offset, 1.0, 0.0)
        return mask, places

    @pl.when(p.index >= 0)
    def _():
      message_rows = [picked(k) for k in range(3)]
      for row, (k, offset, width, base) in enumerate(table):
        mask, places = spread(k, offset, width, base)
        vec[row : row + 1, :] = jnp.sum(mask * dot(message_rows[k], places.astype(BF)), 0, keepdims=True)

    def first_norm(slots, rows):
        normalized, _ = norm_parts(img_ref[slots].astype(F32))
        norm1[rows] = (normalized * vec[0:1] + vec[1:2]).astype(BF)

    f1_g.arrive(0)
    f1_g.line(2, 0)
    f2_g.own(0)
    by_rows(first_norm)
    qo_g.finish()
    swap_copy.wait_send()

    for j in range(9):
        part = dot_nt(norm1[...], load_runs(W.at[0], qkv_runs(256 * j, 256 * j + 256)))
        if j < 3:
            part = part + vec[6:7, 256 * j : 256 * j + 256]
        elif j >= 6:
            part = part + vec[7:8, 256 * (j - 6) : 256 * (j - 6) + 256]
        part = part.astype(BF)
        qkv[2 * j] = part[:, :128]
        qkv[2 * j + 1] = part[:, 128:]
        if j == 4:
            f1_g.line(2, 1)
            f1_g.arrive(1)
            f2_g.own(1)

    def image_rows(i):
        return pl.ds(pl.multiple_of(i * PAD, 16), PAD)

    low = iota((1, 128), 1) < 64

    def halves(value):
        zero = jnp.zeros_like(value)
        return jnp.where(low, value, zero), jnp.where(low, zero, value)

    def head_pair(i, pair):
        rows = pl.ds(pl.multiple_of(i * PAD, 16), PAD)
        return rows, qkv[pair, rows], qkv[6 + pair, rows], qkv[12 + pair, rows]

    PAIRS = 2

    def attend(it, carry):
        i, first = lax.div(it, 6 // PAIRS), lax.rem(it, 6 // PAIRS) * PAIRS
        bars = jnp.concatenate([jnp.where(mask_ref[image_rows(i)] > 0, 0.0, -1e30)] * 2, 1)[:, :PAD]
        results = []
        for step in range(PAIRS):
            rows, q, k, v = head_pair(i, first + step)
            v_t = v.T
            parts = []
            for h, k_h in enumerate(halves(k * jnp.asarray(0.125, BF))):
                scores = dot_nt(k_h, q) + bars
                top = jnp.max(scores, 0, keepdims=True)
                terms = jnp.exp(scores - top)
                amount = jnp.sum(terms, 0, keepdims=True)
                lse[(i * 6 + first + step) * 2 + h] = top + jnp.log(amount)
                parts.append(dot(v_t[64 * h : 64 * h + 64], terms.astype(BF)) * (1.0 / amount))
            results.append(jnp.concatenate(parts, 0).T.astype(BF))
        for step in range(PAIRS):
            att[first + step, rows] = results[step]
        return carry

    lax.fori_loop(0, 3, attend, 0)
    f1_g.line(3, 0)
    f2_g.line(1, 0)
    f1_g.line(3, 1)
    f1_g.arrive(2)
    lax.fori_loop(3, 5, attend, 0)
    f2_g.line(1, 1)
    f1_g.arrive(3)
    f2_g.arrive(0)
    lax.fori_loop(5, 7, attend, 0)
    f2_g.line(2, 0)
    f2_g.line(2, 1)
    f2_g.arrive(1)
    lax.fori_loop(7, 9, attend, 0)

    attended = slabs(att, 0, 6)
    for j in range(3):
        lanes = slice(256 * j, 256 * j + 256)
        part = dot_nt(attended, load_runs(W.at[0], out_runs(256 * j, 256 * j + 256)))
        for i in range(IMG):
            res_ref[i, :, lanes] = img_ref[i, :, lanes].astype(F32) + part[i * PAD : i * PAD + SLOTS] + vec[2:3, lanes]

    def second_norm(slots, rows):
        normalized, _ = norm_parts(res_ref[slots])
        value = (normalized * vec[3:4] + vec[4:5]).astype(BF)
        for k in range(6):
            sec[k, rows] = value[:, 128 * k : 128 * k + 128]

    by_rows(second_norm)
    f1_g.finish()

    def expand(it, carry):
        q, rows = lax.div(it, IMG), image_rows(lax.rem(it, IMG))
        left = jnp.concatenate([sec[k, rows] for k in range(6)], 1)
        pre = dot_nt(left, W[1, lax.div(q, 2), lax.rem(q, 2)].reshape(D, D)) + vec[pl.ds(8 + q, 1), :]
        value, derivative = gelu_parts(pre)
        act[q, rows] = value.astype(BF)
        slope[q, rows] = derivative.astype(BF)
        return carry

    lax.fori_loop(0, 3, expand, 0)
    f2_g.line(3, 0)
    f2_g.line(3, 1)
    f2_g.arrive(2)
    lax.fori_loop(3, 9, expand, 0)
    f2_g.arrive(3)
    lax.fori_loop(9, 12, expand, 0)
    f2_g.finish()

    def contract(hidden_units, m):
        def body(i, carry):
            rows = image_rows(i)
            for j in range(3):
                lanes = slice(256 * j, 256 * j + 256)
                left = jnp.concatenate([hidden_units[q, rows] for q in range(4)], 1)
                temp[rows, lanes] = dot(left, W[m, :, :, :, :, :, lanes].reshape(4 * D, 256))
            return carry

        lax.fori_loop(0, IMG, body, 0)

    contract(act, 2)

    def wide(column):
        return jnp.concatenate([column] * 6, 1)

    pooled[...] = jnp.zeros(pooled.shape, F32)
    for i in range(IMG):
        sums, count = jnp.zeros((1, D), F32), jnp.zeros((1, 128), F32)
        for start, size in CUTS:
            rows = pl.ds(i * PAD + start, size)
            mask = mask_ref[rows]
            slots = (i, slice(start, start + size))
            outputs = (res_ref[slots] + temp[rows] + vec[5:6]) * wide(mask)
            mix_ref[slots] = outputs.astype(BF)
            sums = sums + jnp.sum(outputs, 0, keepdims=True)
            count = count + jnp.sum(mask, 0, keepdims=True)
        pooled[i : i + 1, :] = sums / wide(count)
        pooled[8 + i : 9 + i, :] = wide(count)

    def unit_grad(grad, values, inverse):
        return inverse * grad - inverse * inverse * inverse * values * jnp.sum(values * grad, -1, keepdims=True)

    own_pooled = pooled[0:8]
    image_unit, image_inverse = unit(own_pooled)
    image_unit = image_unit.astype(BF)
    message = jnp.zeros((32, 128), F32)
    for k in range(6):
        at = jnp.where((iota((32, 8), 0) == iota((32, 8), 1) + IMG * k) & (iota((32, 8), 1) < IMG), 1.0, 0.0).astype(BF)
        message = message + dot(at, image_unit[:, 128 * k : 128 * k + 128])
    units[p.c, p.plane] = message.astype(BF)

    def push(i, carry):
        q = lax.rem(p.plane + i, half)
        remote(units.at[p.c, p.plane], units.at[p.c, p.plane], 1, p.in_plane(q)).start()
        return carry

    lax.fori_loop(1, half, push, 0)
    all_but_own = remote(units.at[p.c, pl.ds(0, half - 1)], units.at[p.c, pl.ds(0, half - 1)], 1, p.sib)

    def gathered(source_chunks, chunk_rows, row_of, tiles, base):
        results = []
        for k in range(tiles):
            value = jnp.zeros((total, 128), F32)
            for number, chunk in source_chunks:
                owner, inside = split(iota((1, chunk_rows), 1), base)
                target = row_of(owner, inside, number, k)
                value = value + dot(jnp.where(iota((total, chunk_rows), 0) == target, 1.0, 0.0).astype(BF), chunk)
            results.append(value)
        return results

    def text_row(owner, inside, number, k):
        at = inside - 3 - per_group * k
        group = group_of(owner + 8 * number)
        return jnp.where((at >= 0) & (at < per_group), group * per_group + at, -1)

    chunks = [(2 * c + l, small[c, l].reshape(8 * small_rows, 128)) for c in range(2) for l in range(2)]
    tiles = gathered(chunks, 8 * small_rows, text_row, 6, small_rows)
    for b in range(r):
        for k in range(6):
            G[1, b // 16, b // 8 % 2, b // 2 % 4, b % 2, :, 128 * k : 128 * k + 128] = tiles[k][ROWS * b : ROWS * b + ROWS].astype(BF)

    def texts():
        return jnp.concatenate([G[1, b // 16, b // 8 % 2, b // 2 % 4, b % 2] for b in range(r)], 0)

    owner, inside = split(iota((total, 1), 0), per_group)
    lines = dot(jnp.where(owner == group_of(iota((1, GROUPS), 1)), 1.0, 0.0).astype(BF), picked(1))
    places = iota((1, 128), 1)
    high = jnp.sum(jnp.where(places == inside + PAIR_LANE, lines, 0.0), 1, keepdims=True)
    rest = jnp.sum(jnp.where(places == inside + PAIR_LANE + per_group, lines, 0.0), 1, keepdims=True)
    pair_rows[...] = jnp.broadcast_to(high * 256.0 + rest, (total, 128))

    all_but_own.wait_recv()
    share = remote(units.at[p.c], units.at[p.c], 2, p.sib)
    share.start()
    remote(units.at[1 - p.c], units.at[1 - p.c], 2, p.sib).wait_recv()

    for k in range(6):

        def add_chunk(number, value, k=k):
            c, at = lax.div(number * 16, half), lax.rem(number * 16, half)
            owner, inside = split(iota((1, 512), 1), 32)
            q = owner + at
            t = inside - IMG * k
            if r == 1:
                linear = 2 * q + c
            else:
                chip, rho = split(q, r)
                linear = (2 * chip + c) * r + rho
            target = jnp.where((t >= 0) & (t < IMG), linear * IMG + t, -1)
            pick = jnp.where(iota((total, 512), 0) == target, 1.0, 0.0).astype(BF)
            return value + dot(pick, units[c, pl.ds(at, 16)].reshape(512, 128))

        value = lax.fori_loop(0, n // 16, add_chunk, jnp.zeros((total, 128), F32)).astype(BF)
        for b in range(r):
            G[2, b // 16, b // 8 % 2, b // 2 % 4, b % 2, :, 128 * k : 128 * k + 128] = value[ROWS * b : ROWS * b + ROWS]

    def block(m, b):
        return G[m, lax.div(b, 16), lax.rem(lax.div(b, 8), 2), lax.rem(lax.div(b, 2), 4), lax.rem(b, 2)]

    scale = scale_ref[0, 0]
    row = jnp.zeros((1, total), F32)

    def similar(b, col_top):
        rows = pl.ds(pl.multiple_of(b * ROWS, ROWS), ROWS)
        part = dot_nt(block(2, b), texts()) * scale
        temp[rows, :total] = part
        return jnp.maximum(col_top, jnp.max(part, 0, keepdims=True))

    col_top = lax.fori_loop(0, r, similar, row - jnp.inf)

    def by_blocks(fn):
        def body(b, carry):
            rows = pl.ds(pl.multiple_of(b * ROWS, ROWS), ROWS)
            part = temp[rows, :total]
            top = jnp.max(part, 1, keepdims=True)
            row_lse = top + jnp.log(jnp.sum(jnp.exp(part - top), 1, keepdims=True))
            match = jnp.where(iota((ROWS, total), 1) == pair_of(rows), 1.0, 0.0)
            return fn(b, part, row_lse, match, carry)

        return body

    def pair_of(rows):
        return pair_rows[rows][:, 0:1].astype(jnp.int32)

    def sums(b, part, row_lse, match, carry):
        col_sum, loss = carry
        paired = jnp.sum(jnp.sum(part * match, 1, keepdims=True), 0, keepdims=True)
        return col_sum + jnp.sum(jnp.exp(part - col_top), 0, keepdims=True), loss + jnp.sum(row_lse, 0, keepdims=True) - 2.0 * paired

    col_sum, loss = lax.fori_loop(0, r, by_blocks(sums), (row, jnp.zeros((1, 1), F32)))
    col_lse = col_top + jnp.log(col_sum)
    loss = (loss + jnp.sum(col_lse, 1, keepdims=True)) / (2.0 * total)
    loss_ref[...] = jnp.broadcast_to(loss, (8, 128))

    def own_of(places):
        return jnp.where((places == iota(places.shape, 0) + IMG * p.index) & (iota(places.shape, 0) < IMG), 1.0, 0.0).astype(BF)

    own = own_of(iota((8, total), 1))

    def similar_grad(b, part, row_lse, match, carry):
        grad_rows, grad_text = carry
        grad = 0.5 * (jnp.exp(part - row_lse) + jnp.exp(part - col_lse)) - match
        grad = (scale * grad).astype(BF)
        own_rows = own_of(iota((8, ROWS), 1) + b * ROWS)
        return grad_rows + dot(own_rows, grad), grad_text + dot(dot_nt(own, grad).astype(BF), block(2, b))

    grad_rows, grad_text = lax.fori_loop(0, r, by_blocks(similar_grad), (jnp.zeros((8, total), F32), jnp.zeros((8, D), F32)))
    grad_unit = dot(grad_rows.astype(BF), texts())
    row_grad[...] = unit_grad(grad_unit, own_pooled, image_inverse) / jnp.maximum(pooled[8:16], 1.0)
    own_text = text_ref[...].astype(F32)
    _, text_inverse = unit(own_text)
    tg_ref[...] = unit_grad(grad_text[:IMG], own_text, text_inverse)

    sc0, sc1, sc2 = (
        Scatter(p, G.at[m], area, ends.at[1 if m == 1 else 0], s_send.at[m], s_recv.at[m], m == 0)
        for m, area in (
            (0, lambda k: room.at[k]),
            (1, lambda k: W.at[2, k // 2, k % 2] if isinstance(k, int) else W.at[2, 0, k]),
            (2, lambda k: room.at[k]),
        )
    )

    def out_grad(slots, rows):
        return wide(mask_ref[rows]) * (cot_ref[slots].astype(F32) + row_grad[pl.ds(slots[0], 1), :])

    def first_round(slots, rows):
        value = out_grad(slots, rows).astype(BF)
        grad2[rows] = value
        vec_grad[5:6] += jnp.sum(value.astype(F32), 0, keepdims=True)

    by_rows(first_round)
    order = ((1 - p.c, 1 - p.f), (p.c, 1 - p.l), (1 - p.c, p.f), (p.c, p.l))

    def weight_grad(m, at, left, right):
        left = left.T
        for j in range(3):
            lanes = slice(256 * j, 256 * j + 256)
            G[(m,) + at + (slice(None), slice(None), slice(None), lanes)] = (
                dot(left, right[:, lanes]).astype(BF).reshape(4, 2, ROWS, 256)
            )

    for step, at in enumerate(order):
        weight_grad(2, at, act[2 * at[0] + at[1]], grad2[...])
        if step == 0:
            sc2.core_send(1 - p.f)
        if step == 2:
            sc2.core_send(p.f)
    for q in range(4):
        for part in range(2):
            lanes = slice(384 * part, 384 * part + 384)
            value = dot_nt(grad2[...], W[2, q // 2, q % 2, 2 * part : 2 * part + 2].reshape(384, D)) * slope[q, :, lanes].astype(F32)
            value = value.astype(BF)
            slope[q, :, lanes] = value
            vec_grad[8 + q : 9 + q, lanes] = jnp.sum(value.astype(F32), 0, keepdims=True)
        if q == 0:
            sc2.core_add(1 - p.l)
            sc2.side_send()
        if q == 1:
            sc2.core_add(p.l)
    sc2.side_add(3)
    sc2.ends(3)
    f2_g.drain()

    def give(k):
        for at, device in ((0, p.sib), (1, p.ln), (2, p.fn)):
            pl.semaphore_signal(credit.at[k, at], inc=1, device_id=device, device_id_type=MESH)
        p.for_others(lambda zz: pl.semaphore_signal(credit.at[k, 3 + p.z], inc=1, device_id=p.column(zz), device_id_type=MESH))

    def take(k, *which):
        for at in which:
            pl.semaphore_wait(credit.at[k, at], 1)

    def take_column(k):
        p.for_others(lambda zz: pl.semaphore_wait(credit.at[k, 3 + zz], 1))

    give(0)
    for step, at in enumerate(order):
        weight_grad(1, at, slope[2 * at[0] + at[1]], slabs(sec, 0, 6))
        if step == 0:
            take(0, 0)
            sc1.core_send(1 - p.f)
        if step == 2:
            sc1.core_send(p.f)
            sc2.side_add(2)
            sc2.ends(2)
    contract(slope, 1)
    sc1.core_add(1 - p.l)
    take(0, 1)
    sc1.side_send()
    sc1.core_add(p.l)
    sc2.side_add(1)
    sc2.ends(1)
    sc2.side_add(0)

    def second_back(slots, rows):
        grad = temp[rows]
        normalized, inverse = norm_parts(res_ref[slots])
        total_grad = out_grad(slots, rows) + norm_grad(grad, vec[3:4], normalized, inverse)
        res_ref[slots] = total_grad
        rounded = total_grad.astype(BF)
        grad2[rows] = rounded
        vec_grad[3:4] += jnp.sum(grad * normalized, 0, keepdims=True)
        vec_grad[4:5] += jnp.sum(grad, 0, keepdims=True)
        vec_grad[2:3] += jnp.sum(rounded.astype(F32), 0, keepdims=True)

    by_rows(second_back)
    sc2.inner(2, True)
    sc2.inner(2, False)
    attended = slabs(att, 0, 6)
    for j in range(3):
        lanes = slice(256 * j, 256 * j + 256)
        store_runs(G.at[0], out_runs(256 * j, 256 * j + 256), dot(grad2[:, lanes].T, attended).astype(BF))
    for j in range(3):
        lanes = slice(256 * j, 256 * j + 256)
        part = dot(grad2[...], load_runs(W.at[0], out_runs(0, D), lanes)).astype(BF)
        sec[2 * j] = part[:, :128]
        sec[2 * j + 1] = part[:, 128:]

    def attend_back(it, carry):
        i, first = lax.div(it, 6 // PAIRS), lax.rem(it, 6 // PAIRS) * PAIRS
        bars = jnp.concatenate([jnp.where(mask_ref[image_rows(i)] > 0, 0.0, -1e30)] * 2, 1)[:, :PAD]
        results = []
        for step in range(PAIRS):
            rows, plain_q, k, v = head_pair(i, first + step)
            grad_out = sec[first + step, rows]
            q, k = plain_q * jnp.asarray(0.125, BF), k * jnp.asarray(0.125, BF)
            k_t = k.T
            q_halves, out_halves, v_halves = halves(q), halves(grad_out), halves(v)
            grad_v, grad_k, grad_q = 0.0, 0.0, []
            for h, k_h in enumerate(halves(k)):
                scores = dot_nt(k_h, plain_q) + bars
                probs = jnp.exp(scores - lse[(i * 6 + first + step) * 2 + h])
                grad_v = grad_v + dot(probs.astype(BF), out_halves[h])
                grad_probs = dot_nt(v_halves[h], grad_out)
                grad_scores = (probs * (grad_probs - jnp.sum(grad_probs * probs, 0, keepdims=True))).astype(BF)
                grad_k = grad_k + dot(grad_scores, q_halves[h])
                grad_q.append(dot(k_t[64 * h : 64 * h + 64], grad_scores))
            results.append((jnp.concatenate(grad_q, 0).T.astype(BF), grad_k.astype(BF), grad_v.astype(BF)))
        for step in range(PAIRS):
            for which in range(3):
                qkv[6 * which + first + step, rows] = results[step][which]
        return carry

    take(0, 2)
    take_column(0)
    lax.fori_loop(0, 2, attend_back, 0)
    sc1.side_add(3)
    sc1.ends(3)
    lax.fori_loop(2, 4, attend_back, 0)
    sc2.inner(1, True)
    sc2.inner(1, False)
    sc1.side_add(2)
    sc1.ends(2)
    lax.fori_loop(4, 6, attend_back, 0)
    sc1.side_add(1)
    sc1.ends(1)
    sc1.side_add(0)
    lax.fori_loop(6, 9, attend_back, 0)
    sc2.come()
    for j in range(9):
        left = slabs(qkv, 2 * j, 2)
        store_runs(G.at[0], qkv_runs(256 * j, 256 * j + 256), dot(left.T, norm1[...]).astype(BF))
        if j < 3 or j >= 6:
            row, lanes = (6, slice(256 * j, 256 * j + 256)) if j < 3 else (7, slice(256 * (j - 6), 256 * (j - 6) + 256))
            vec_grad[row : row + 1, lanes] = jnp.sum(left.astype(F32), 0, keepdims=True)
    sc1.inner(2, True)
    sc1.inner(2, False)
    df2_ref[...] = sc2.final()
    give(1)
    take(1, 0)
    sc0.core_send(1 - p.f)
    sc0.core_send(p.f)
    sc0.core_add(1 - p.l)
    take(1, 1)
    sc0.side_send()

    def contract_joined(i, carry):
        rows = image_rows(i)
        for j in range(3):
            lanes = slice(256 * j, 256 * j + 256)
            left = jnp.concatenate([qkv[k, rows] for k in range(18)], 1)
            temp[rows, lanes] = dot(left, load_runs(W.at[0], qkv_runs(0, 3 * D), lanes))
        return carry

    lax.fori_loop(0, IMG, contract_joined, 0)
    sc0.core_add(p.l)
    sc1.inner(1, True)
    sc1.inner(1, False)
    take(1, 2)
    take_column(1)

    def first_back(slots, rows):
        grad = temp[rows]
        normalized, inverse = norm_parts(img_ref[slots].astype(F32))
        res_ref[slots] += norm_grad(grad, vec[0:1], normalized, inverse)
        vec_grad[0:1] += jnp.sum(grad * normalized, 0, keepdims=True)
        vec_grad[1:2] += jnp.sum(grad, 0, keepdims=True)

    by_rows(first_back)
    for h in (3, 2):
        sc0.side_add(h)
        sc0.cross_send(h)

    def two_parts(value):
        high = value.astype(BF)
        return jnp.concatenate([high, (value - high.astype(F32)).astype(BF)], 0)

    @pl.when(p.index >= 0)
    def _():
        lines = [jnp.zeros((2 * GROUPS, 128), F32)] * 8
        for row, (k, offset, width, base) in enumerate(table):
            mask, places = spread(k, 0, width, base)
            line = dot_nt(two_parts(mask * vec_grad[row : row + 1]), places.astype(BF))
            line_at = row if row < 6 else 6 if row < 8 else 7
            lines[line_at] = lines[line_at] + line
        lines = [line[:GROUPS] + line[GROUPS:] for line in lines]
        shape = (GROUPS * 8, 8 * GROUPS)
        k, block_at = split(iota(shape, 1), GROUPS)
        at = jnp.where(iota(shape, 0) == 8 * block_at + k, 1.0, 0.0).astype(BF)
        both = two_parts(jnp.concatenate(lines, 0))
        vec_out[...] = (dot(at, both[: 8 * GROUPS]) + dot(at, both[8 * GROUPS :])).reshape(2, 16, 8, 128)

    vec_swap = remote(vec_out.at[1 - p.c], vec_core, 3, p.sib)
    vec_swap.start()
    for h in (1, 0):
        sc0.side_add(h)
        sc0.cross_send(h)
    vec_swap.wait_recv()
    vec_out[p.c] += vec_core[...]
    mine = (p.l * 4 + p.z) * 2 + p.f

    def push_vec(i, carry):
        q = lax.rem(mine + i, 16)
        dev = p.block(lax.div(q, 8), lax.rem(lax.div(q, 2), 4), lax.rem(q, 2))
        remote(vec_out.at[p.c, q], vec_in.at[mine], 4, dev).start()
        return carry

    lax.fori_loop(1, 16, push_vec, 0)
    vec_in[mine] = vec_out[p.c, mine]
    sc0.cross_add(3)
    sc1.come()
    for h in (2, 1, 0):
        sc0.cross_add(h)
    df1_ref[...] = sc1.final()
    own_qo = sc0.final()
    swap_grad[0] = own_qo
    qo_back = remote(swap_grad.at[0], swap_grad.at[1], 5, p.sib)
    qo_back.start()
    most = remote(vec_out.at[p.c, pl.ds(0, 15)], vec_in.at[pl.ds(0, 15)], 4, p.sib)
    most.wait_recv()
    dvec_ref[...] = jnp.sum(vec_in[...], 0)
    qo_back.wait_recv()
    other_qo = swap_grad[1]
    dq_ref[...] = jnp.where(
        first_core, own_qo[:QKV_ROWS], jnp.concatenate([other_qo[QKV_ROWS:], own_qo[:gap]], 0)
    )
    do_ref[...] = jnp.where(first_core, other_qo[gap : gap + OUT_ROWS], own_qo[QKV_ROWS:])

    all_but_own.wait_send()
    share.wait_send()
    vec_swap.wait_send()
    most.wait_send()
    qo_back.wait_send()
    for g in (sm_g, qo_g, f1_g):
        g.drain()
    for s in (sc0, sc1, sc2):
        s.drain()


def results_kernel(*refs):
    sources, results = refs[:9], refs[9:]
    for k in (0, 1, 3, 4, 5, 6, 7):
        results[k][...] = sources[k][...]
    results[2][...] = sources[2][0:1, 0:1]
    for k in range(8):
        results[8 + k][...] = sources[8][k : k + 1, 0 : results[8 + k].shape[1]]


def swap(block, step, size):
    return lax.ppermute(block, "fsdp", [(i, i ^ step) for i in range(size)])


def pregather(block, F, r):
    step = 1
    while step < r:
        high = (lax.axis_index("fsdp") // step) % 2 == 1
        other = swap(block, step, F)
        block = jnp.concatenate([jnp.where(high, other, block), jnp.where(high, block, other)], 0)
        step *= 2
    return block


def postscatter(block, F, r):
    step = r // 2
    while step:
        high = (lax.axis_index("fsdp") // step) % 2 == 1
        lower, upper = jnp.split(block, 2)
        block = jnp.where(high, upper, lower) + swap(jnp.where(high, lower, upper), step, F)
        step //= 2
    return block


def per_device(
    F,
    r,
    n,
    images,
    tissue,
    pair_index,
    text_embed,
    logit_scale,
    ln1_gain,
    ln1_bias,
    w_qkv,
    bias_qv,
    w_out,
    bias_out,
    ln2_gain,
    ln2_bias,
    w_fc1,
    bias_fc1,
    w_fc2,
    bias_fc2,
    cotangent,
):
    gather = functools.partial(pregather, F=F, r=r)

    pair = gather(pair_index)
    vectors = [gather(v) for v in (ln1_gain, ln1_bias, bias_out, ln2_gain, ln2_bias, bias_fc2, bias_qv, bias_fc1)]
    vectors += [(pair // 256).astype(BF), (pair % 256).astype(BF)]
    pair_at = 128 + PAIR_LANE
    places = (0, 24, 48, 72, 96, 128, 152, 256, pair_at, pair_at + IMG * r)
    thin = sum(jnp.pad(v, (at, 384 - at - v.shape[0])) for v, at in zip(vectors, places)).reshape(3, 128)
    small_rows = -(-(3 + 18 * r) // 16) * 16
    vmem = pl.BlockSpec(memory_space=pltpu.VMEM)
    shape = jax.ShapeDtypeStruct
    mix, res, loss, text_grad, dq, do, df1, df2, dvec = pl.pallas_call(
        functools.partial(layer_kernel, F, r, n),
        out_shape=(
            shape((IMG, SLOTS, D), BF),
            shape((IMG, SLOTS, D), F32),
            shape((8, 128), F32),
            shape((IMG, D), F32),
            shape((QKV_ROWS, D), F32),
            shape((OUT_ROWS, D), F32),
            shape((ROWS, D), F32),
            shape((ROWS, D), F32),
            shape((8, 128), F32),
        ),
        in_specs=[vmem] * 10 + [pl.BlockSpec(memory_space=pltpu.SMEM)],
        out_specs=(vmem,) * 9,
        scratch_shapes=[
            pltpu.VMEM((3, 2, 2, 4, 2, ROWS, D), BF),
            pltpu.VMEM((3, 2, 2, 4, 2, ROWS, D), BF),
            pltpu.VMEM((4, 4, 2, ROWS, D), BF),
            pltpu.VMEM((2, 3, ROWS, D), BF),
            pltpu.VMEM((2, 2, 4, 2, small_rows, 128), BF),
            pltpu.VMEM((TOK, 128), F32),
            pltpu.VMEM((8, 256), F32),
            pltpu.VMEM((-(-IMG * r // 8) * 8, D), F32),
            pltpu.VMEM((2, ROWS, D), F32),
            pltpu.VMEM((TOK, D), BF),
            pltpu.VMEM((18, TOK, 128), BF),
            pltpu.VMEM((6, TOK, 128), BF),
            pltpu.VMEM((2 * IMG * 6, 1, PAD), F32),
            pltpu.VMEM((6, TOK, 128), BF),
            pltpu.VMEM((4, TOK, D), BF),
            pltpu.VMEM((4, TOK, D), BF),
            pltpu.VMEM((TOK, D), BF),
            pltpu.VMEM((max(TOK, IMG * n), D), F32),
            pltpu.VMEM((16, D), F32),
            pltpu.VMEM((16, D), F32),
            pltpu.VMEM((16, D), F32),
            pltpu.VMEM((8, D), F32),
            pltpu.VMEM((IMG * n, 128), F32),
            pltpu.VMEM((2, n // 2, 32, 128), BF),
            pltpu.VMEM((2, 16, 8, 128), F32),
            pltpu.VMEM((16, 8, 128), F32),
            pltpu.VMEM((16, 8, 128), F32),
            pltpu.SemaphoreType.DMA((4, 32)),
            pltpu.SemaphoreType.DMA((4, 32)),
            pltpu.SemaphoreType.DMA((3, 32)),
            pltpu.SemaphoreType.DMA((3, 32)),
            pltpu.SemaphoreType.DMA((16,)),
            pltpu.SemaphoreType.REGULAR((2, 8)),
        ],
        compiler_params=pltpu.CompilerParams(collective_id=0, has_side_effects=True, vmem_limit_bytes=VMEM_LIMIT),
    )(
        gather(w_qkv.T),
        gather(w_out.T),
        gather(w_fc1.T),
        gather(w_fc2),
        thin,
        gather(text_embed),
        images,
        cotangent,
        tissue,
        text_embed,
        logit_scale.reshape(1, 1),
    )
    widths = (24,) * 6 + (48, 96)
    mix, res, loss, text_grad, dq, do, df1, df2, *vectors = pl.pallas_call(
        results_kernel,
        out_shape=(
            shape((IMG, SLOTS, D), BF),
            shape((IMG, SLOTS, D), F32),
            shape((1, 1), F32),
            shape((IMG, D), F32),
            shape((QKV_ROWS, D), F32),
            shape((OUT_ROWS, D), F32),
            shape((ROWS, D), F32),
            shape((ROWS, D), F32),
        )
        + tuple(shape((1, width), F32) for width in widths),
        in_specs=[vmem] * 9,
        out_specs=(vmem,) * 16,
        compiler_params=pltpu.CompilerParams(vmem_limit_bytes=VMEM_LIMIT),
    )(mix, res, loss, text_grad, dq, do, df1, df2, dvec)
    scatter = functools.partial(postscatter, F=F, r=r)
    vectors = [scatter(v.reshape(-1)) for v in vectors]
    return (
        mix,
        res,
        loss.reshape(()),
        text_grad,
        vectors[0],
        vectors[1],
        scatter(dq).T,
        vectors[6],
        scatter(do).T,
        vectors[2],
        vectors[3],
        vectors[4],
        scatter(df1).T,
        vectors[7],
        scatter(df2),
        vectors[5],
    )


def solution(mesh):
    F = mesh.shape["fsdp"]
    n = mesh.shape["dp"] * F
    r = n // GROUPS
    both = ("dp", "fsdp")
    rows, columns = P(both), P(None, both)
    in_specs = (
        rows, rows, rows, rows, P(), rows, rows, columns, rows, columns, rows, rows, rows, columns, rows, rows, rows, rows
    )
    out_specs = (
        rows, rows, P(), rows, rows, rows, columns, rows, columns, rows, rows, rows, columns, rows, rows, rows
    )
    return jax.shard_map(
        functools.partial(per_device, F, r, n), mesh=mesh, in_specs=in_specs, out_specs=out_specs, check_vma=False
    )
```
